128 devices in a mesh: source: 8 (over y_hi, z), gx: 4 (over x), gy: 4 (over y_lo, core).
Axes of the slice: x: 4, y: 4 (y_hi: 2, y_lo: 2; y = y_hi * 2 + y_lo), z: 4, core: 2. Of those that a mesh axis runs over, the one named last changes fastest.
Arguments:
- fwd_field: bfloat16 [16, 6, 8, 16, 128, 128], P('source', None, None, 'gx', 'gy'), may hold values from -6 to 6
- adj_field: bfloat16 [16, 6, 8, 16, 128, 128], P('source', None, None, 'gx', 'gy'), may hold values from -6 to 6
- conductivity: float32 [2, 8, 16, 128, 128], P(None, None, 'gx', 'gy'), may hold values from 0.3 to 3
- tensor: bfloat16 [6, 8, 16, 128, 128], P(None, None, 'gx', 'gy'), may hold values from -0.08 to 1, as said below
Outputs:
- update: float32 [2, 8, 16, 128, 128], P(None, None, 'gx', 'gy')
The draws below stay inside these ranges and needn't reach their ends.
Inputs may be any that keep to these rules, and one draw needn't show every extreme that they name: Each cell's tensor has diagonal entries of 0.25 or more and off-diagonal entries of magnitude 0.08 or less.
All inputs are finite; a program needn't handle non-finite values.
Results may differ from the reference program's by a relative error of at most 0.0003.
Values sent between devices are 32-bit elements; how exact they have to be, the bound alone decides.
No kernel may reach another device: no remote copies, remote signals or barrier semaphores. Data moves between devices by JAX's collectives and lax.ppermute only.
A program may use at most 256 MiB of HBM per device.

```python
import math
import jax
import jax.numpy as jnp
from jax import lax

NZ = 128
PASSES = 4
NXB = 16
NX = 128
NY = 128
TRANSMITTERS = 16
N_SOURCE = 8


def draw_tensor(key, part):
    key = jax.random.fold_in(key, 7)
    key_diag, key_off = jax.random.split(key)
    shape = (3, N_SOURCE, NXB, NY, NZ)
    spread = jax.random.uniform(key_diag, shape, jnp.float32)
    diag = 0.25 + 0.75 * spread
    off = jax.random.uniform(key_off, shape, jnp.float32, -0.078, 0.078)
    return jnp.concatenate([diag, off], axis=0).astype(jnp.bfloat16)


def raised(drawn, rng, source, target, shards_of, factor):
    owner, partner = [(jnp.arange(drawn.shape[dim]) // (drawn.shape[dim] // shards_of)).reshape([-1 if axis == dim else 1 for axis in range(drawn.ndim)]) for dim in (source, target)]
    chosen = jax.random.permutation(rng, shards_of)[partner]
    strong = (owner == chosen) | (owner == (partner + shards_of // 2) % shards_of)
    return jnp.where(strong, factor * drawn, drawn)


def block_levels(key, dims, cuts, smallest, high):
    loudness = 1.0
    for position, parts in cuts:
        steps = jax.random.uniform(jax.random.fold_in(jax.random.fold_in(key, 6), position), (parts,), jnp.float32, smallest / len(cuts), high / len(cuts))
        loudness = loudness * jnp.repeat(jnp.exp(steps), dims[position] // parts).reshape((-1,) + (1,) * (len(dims) - 1 - position))
    return loudness


def noise(key, extent, scale, reach, cuts=(), held_as=jnp.bfloat16):
    entries = jax.random.normal(key, extent, jnp.float32) * scale
    if len(cuts) > 0:
        entries = block_levels(key, extent, cuts, -0.22, 0.18) * entries
    return jnp.clip(entries, min=-reach, max=reach).astype(held_as)


def heavy_noise(key, shape, scale, reach, cuts, heavy, dtype=jnp.bfloat16):
    result = scale * jax.random.normal(key, shape, jnp.float32)
    if cuts:
        result = result * block_levels(key, shape, cuts, -0.22, 0.18)
    return jnp.clip(raised(result, jax.random.fold_in(key, 3), *heavy), -reach, reach).astype(dtype)


def setup_inputs(seed: int = 0) -> dict:
    streams_of = jax.random.split(jax.random.key(seed), 5)
    fwd_field = heavy_noise(streams_of[0], (TRANSMITTERS, 6, N_SOURCE, NXB, NY, NZ), 1.0, 6.0, ((0, 8), (3, 4), (4, 4)), (0, 2, 8, 2.0))
    adj_field = noise(streams_of[1], (TRANSMITTERS, 6, N_SOURCE, NXB, NY, NZ), 1.0, 6.0, ((0, 8), (3, 4), (4, 4)))
    conductivity = jnp.clip(jnp.exp(math.log(3.0) - 2.3025851 * jax.random.uniform(streams_of[2], (2, N_SOURCE, NXB, NY, NZ), jnp.float32) ** block_levels(streams_of[2], (2, N_SOURCE, NXB, NY, NZ), ((2, 4), (3, 4)), -0.2, 0.2)), 0.3, 3.0)
    tensor = draw_tensor(jax.random.fold_in(streams_of[4], 71), 0)
    return {"fwd_field": fwd_field, "adj_field": adj_field, "conductivity": conductivity, "tensor": tensor}


step_size = 0.13


def diffuse(field, tens):
    core = field[..., :-1, :-1, :-1]
    grad_x = field[..., 1:, :-1, :-1] - core
    grad_y = field[..., :-1, 1:, :-1] - core
    grad_z = field[..., :-1, :-1, 1:] - core
    dcore = tens[:, ..., :-1, :-1, :-1]
    flux_x = dcore[0] * grad_x + dcore[3] * grad_y + dcore[4] * grad_z
    flux_y = dcore[3] * grad_x + dcore[1] * grad_y + dcore[5] * grad_z
    flux_z = dcore[4] * grad_x + dcore[5] * grad_y + dcore[2] * grad_z
    spread = flux_x[..., 1:, 1:, 1:] - flux_x[..., :-1, 1:, 1:]
    spread = spread + flux_y[..., 1:, 1:, 1:] - flux_y[..., 1:, :-1, 1:]
    spread = spread + flux_z[..., 1:, 1:, 1:] - flux_z[..., 1:, 1:, :-1]
    inner = tens[:, ..., 1:-1, 1:-1, 1:-1]
    inside = (inner[0] > 0).astype(jnp.float32)
    return field[..., 1:-1, 1:-1, 1:-1] + step_size * inside * spread, inner


def pad_cells(array, width):
    lead = [(0, 0)] * (array.ndim - 3)
    return jnp.pad(array, lead + [(width, width)] * 3)


def reference(fwd_field, adj_field, conductivity, tensor):
    def accumulate(carry, pair):
        fwd_one = pair[0].astype(jnp.float32).reshape(6, NX, NY, NZ)
        adj_one = pair[1].astype(jnp.float32).reshape(6, NX, NY, NZ)
        prods = fwd_one * adj_one
        horizontal = prods[0] + prods[1] - prods[3] - prods[4]
        vertical = prods[2] - prods[5]
        return carry + jnp.stack([horizontal, vertical]), None

    start = jnp.zeros((2, NX, NY, NZ), jnp.float32)
    total, _ = lax.scan(accumulate, start, (fwd_field, adj_field))
    field = conductivity.reshape(2, NX, NY, NZ) * total * (1.0 / TRANSMITTERS)
    tens = tensor.astype(jnp.float32).reshape(6, NX, NY, NZ)
    padded_tens = pad_cells(tens, 1)
    for step in range(PASSES):
        field, _ = diffuse(pad_cells(field, 1), padded_tens)
    return field.reshape(2, N_SOURCE, NXB, NY, NZ)
```

```python
import jax
import jax.numpy as jnp
from jax import lax
from jax.experimental import pallas as pl
from jax.experimental.pallas import tpu as pltpu
from jax.sharding import PartitionSpec as P

PASSES = 4
STEP = 0.13
NZC = 4
F32 = jnp.float32


def block_of(h, z):
    return jnp.where(h == 0, z, 2 * NZC - 1 - z)


def source_of(b):
    return b if b < NZC else 3 * NZC - 1 - b


def z_perm(k):
    return [(h * NZC + z, h * NZC + (z + k) % NZC) for h in range(2) for z in range(NZC)]


Y_PERM = [(s, (s + NZC) % (2 * NZC)) for s in range(2 * NZC)]
CORE_PERM = [(i, i ^ 1) for i in range(4)]
CROSS_PERM = [(1, 2), (2, 1)]
X_EVEN = [(i, i ^ 1) for i in range(4)]
X_ODD_RING = [(1, 2), (2, 1), (3, 0), (0, 3)]


def x_odd_owner():
    pairs = []
    for s in range(2 * NZC):
        pairs += [(s * 4 + 1, s * 4 + 2), (s * 4 + 2, s * 4 + 1)]
    for b in range(2 * NZC - 1):
        low, high = source_of(b) * 4 + 3, source_of(b + 1) * 4
        pairs += [(low, high), (high, low)]
    return pairs


def products_kernel(idx_ref, f_ref, a_ref, *outs):
    step = pl.program_id(0)
    for j, out in enumerate(outs):

        @pl.when(step == j)
        def _(out=out):
            for r in range(4):
                hor = ver = None
                for t in range(2):
                    prod = [f_ref[t, c, 0, r].astype(F32) * a_ref[t, c, 0, r].astype(F32) for c in range(6)]
                    h1 = (prod[0] + prod[1]) - (prod[3] + prod[4])
                    v1 = prod[2] - prod[5]
                    hor = h1 if hor is None else hor + h1
                    ver = v1 if ver is None else ver + v1
                out[0, r] = hor
                out[1, r] = ver


def products(blocks, fwd, adj):
    n = 4
    spec = pl.BlockSpec((2, 6, 1, 4, 32, 128), lambda k, idx: (0, 0, idx[k], 0, 0, 0))
    return pl.pallas_call(
        products_kernel,
        grid_spec=pltpu.PrefetchScalarGridSpec(
            num_scalar_prefetch=1,
            grid=(n,),
            in_specs=[spec, spec],
            out_specs=[pl.BlockSpec((2, 4, 32, 128), lambda k, idx: (0, 0, 0, 0))] * n,
        ),
        out_shape=[jax.ShapeDtypeStruct((2, 4, 32, 128), F32)] * n,
        compiler_params=pltpu.CompilerParams(vmem_limit_bytes=32 << 20),
    )(blocks, fwd, adj)


def diffuse_kernel(f_lo, f_own, f_hi, d_lo, d_own, d_hi, out, buf):
    fs, ds = (f_lo, f_own, f_hi), (d_lo, d_own, d_hi)
    lane = lax.broadcasted_iota(jnp.int32, (40, 128), 1)
    first, last = lane == 0, lane == 127

    for p in range(PASSES):
        m = PASSES - 1 - p

        def field(c, r):
            if p == 0:
                return fs[(r + 4) // 4][c, (r + 4) % 4]
            return buf[(p - 1) % 2, c, r + 4]

        flux_x_before = [None, None]
        here = [field(c, -m - 1) for c in range(2)]
        for r in range(-m - 1, 4 + m):
            d = [ds[(r + 4) // 4][e, (r + 4) % 4] for e in range(6)]
            gain = jnp.where(d[0] > 0, F32(STEP), F32(0))
            for c in range(2):
                f = here[c]
                nxt = field(c, r + 1)
                gx = nxt - f
                gy = pltpu.roll(f, 39, 0) - f
                gz = jnp.where(last, 0.0, pltpu.roll(f, 127, 1)) - f
                fx = d[0] * gx + d[3] * gy + d[4] * gz
                if r >= -m:
                    fy = d[3] * gx + d[1] * gy + d[5] * gz
                    fz = d[4] * gx + d[5] * gy + d[2] * gz
                    spread = (fx - flux_x_before[c]) + (fy - pltpu.roll(fy, 1, 0))
                    spread = spread + (fz - jnp.where(first, 0.0, pltpu.roll(fz, 1, 1)))
                    new = f + gain * spread
                    if p == PASSES - 1:
                        out[c, r] = new[:32]
                    else:
                        buf[p % 2, c, r + 4] = new
                flux_x_before[c] = fx
                here[c] = nxt


def diffuse(f_lo, f_own, f_hi, d_lo, d_own, d_hi):
    return pl.pallas_call(
        diffuse_kernel,
        out_shape=jax.ShapeDtypeStruct((2, 4, 32, 128), F32),
        scratch_shapes=[pltpu.VMEM((2, 2, 12, 40, 128), F32)],
        compiler_params=pltpu.CompilerParams(vmem_limit_bytes=32 << 20),
    )(f_lo, f_own, f_hi, d_lo, d_own, d_hi)


def with_y_halo(cells, gy):
    first, last = cells[..., :8, :], cells[..., 24:, :]
    even = gy % 2 == 0
    core = lax.ppermute(jnp.where(even, last, first), "gy", CORE_PERM)
    cross = lax.ppermute(jnp.where(even, first, last), "gy", CROSS_PERM)
    right, left = jnp.where(even, core, cross), jnp.where(even, cross, core)
    row = lax.broadcasted_iota(jnp.int32, right.shape, right.ndim - 2)
    return jnp.concatenate([cells, jnp.where(row < 4, right, left)], axis=-2)


def shards(fwd, adj, cond, tens):
    s, gx, gy = lax.axis_index("source"), lax.axis_index("gx"), lax.axis_index("gy")
    h, z = s // NZC, s % NZC
    own = block_of(h, z)
    around = (z + jnp.arange(NZC, dtype=jnp.int32)) % NZC
    far_blocks = block_of(1 - h, around)
    own_blocks = block_of(h, around)

    def tensor_block(b):
        got = lax.dynamic_index_in_dim(tens, jnp.clip(b, 0, 7), 1, keepdims=False).astype(F32)
        return jnp.where((b >= 0) & (b < 8), got, 0.0)

    d_own = tensor_block(own)
    d_odd = tensor_block(own + jnp.where(gx == 0, 1, 0) - jnp.where(gx == 3, 1, 0))
    d_even_in = lax.ppermute(d_own, "gx", X_EVEN)
    d_odd_in = lax.ppermute(d_odd, "gx", X_ODD_RING)
    x_even = gx % 2 == 0
    d_lo = jnp.where(x_even, d_odd_in, d_even_in)
    d_hi = jnp.where(x_even, d_even_in, d_odd_in)
    d_all = with_y_halo(jnp.concatenate([d_lo, d_own, d_hi], axis=1), gy)

    far = products(far_blocks, fwd, adj)
    far_in = [lax.ppermute(far[k], "source", z_perm(k)) for k in (1, 3, 2)]
    near = products(own_blocks, fwd, adj)
    near_in = [lax.ppermute(near[k], "source", z_perm(k)) for k in (1, 3, 2)]
    far_sum = far[0] + far_in[0] + far_in[1] + far_in[2]
    from_far = lax.ppermute(far_sum, "source", Y_PERM)
    near_sum = near[0] + near_in[0] + near_in[1] + near_in[2]
    cond_own = lax.dynamic_index_in_dim(cond, own, 1, keepdims=False)
    field = (near_sum + from_far) * cond_own * (1.0 / 16.0)

    f_own = with_y_halo(field, gy)
    f_even_in = lax.ppermute(f_own, "gx", X_EVEN)
    f_odd_in = lax.ppermute(f_own, ("source", "gx"), x_odd_owner())
    f_lo = jnp.where(x_even, f_odd_in, f_even_in)
    f_hi = jnp.where(x_even, f_even_in, f_odd_in)

    done = diffuse(f_lo, f_own, f_hi, d_all[:, :4], d_all[:, 4:8], d_all[:, 8:])

    from_y = lax.ppermute(done, "source", Y_PERM)
    ours = [done] + [lax.ppermute(done, "source", z_perm(k)) for k in (1, 3, 2)]
    theirs = [from_y] + [lax.ppermute(from_y, "source", z_perm(k)) for k in (1, 3, 2)]
    out = jnp.zeros((2, 8, 4, 32, 128), F32)
    for k, mine, other in zip((0, 1, 3, 2), ours, theirs):
        zz = (z + NZC - k) % NZC
        out = lax.dynamic_update_index_in_dim(out, mine, block_of(h, zz), 1)
        out = lax.dynamic_update_index_in_dim(out, other, block_of(1 - h, zz), 1)
    return out


def solution(mesh):
    fields = P("source", None, None, "gx", "gy", None)
    cells = P(None, None, "gx", "gy", None)
    return jax.shard_map(
        shards, mesh=mesh, in_specs=(fields, fields, cells, cells), out_specs=cells, check_vma=False
    )
```

```python
import jax
import jax.numpy as jnp
from jax import lax
from jax.experimental import pallas as pl
from jax.experimental.pallas import tpu as pltpu
from jax.sharding import PartitionSpec as P

PASSES = 4
STEP = 0.13
SCALE = 1.0 / 16.0
NZC = 4
BLOCKS = 2 * NZC
F32 = jnp.float32
SLAB = (2, 4, 32, 128)


def block_of(h, z):
    return jnp.where(h == 0, z, BLOCKS - 1 - z)


def source_of(b):
    return b if b < NZC else 3 * NZC - 1 - b


def z_perm(k):
    return [(s, s ^ k) for s in range(BLOCKS)]


Y_PERM = [(s, (s + NZC) % BLOCKS) for s in range(BLOCKS)]
CORE_PERM = [(i, i ^ 1) for i in range(4)]
CROSS_PERM = [(1, 2), (2, 1)]
X_EVEN = [(i, i ^ 1) for i in range(4)]
X_ODD_RING = [(1, 2), (2, 1), (3, 0), (0, 3)]


def x_odd_owner():
    pairs = []
    for s in range(BLOCKS):
        pairs += [(s * 4 + 1, s * 4 + 2), (s * 4 + 2, s * 4 + 1)]
    for b in range(BLOCKS - 1):
        low, high = source_of(b) * 4 + 3, source_of(b + 1) * 4
        pairs += [(low, high), (high, low)]
    return pairs


SENT = [(0, 2), (0, 1), (1, 1), (0, 3), (1, 3)]
KEPT = [(1, 2), (0, 0), (1, 0)]


def start_products(idx_ref, f_hbm, a_hbm, c_hbm, f_buf, a_buf, c_buf, sems, count):
    copies = []
    for k in range(count):
        b = idx_ref[k]
        group = [
            pltpu.make_async_copy(f_hbm.at[:, :, b], f_buf.at[k], sems.at[0, k]),
            pltpu.make_async_copy(a_hbm.at[:, :, b], a_buf.at[k], sems.at[1, k]),
            pltpu.make_async_copy(c_hbm.at[:, b], c_buf.at[k], sems.at[2, k]),
        ]
        for copy in group:
            copy.start()
        copies.append(group)
    return copies


def block_products(k, copies, f_buf, a_buf, c_buf, out):
    for copy in copies[k]:
        copy.wait()
    for r in range(4):
        hor = ver = None
        for t in range(2):
            prod = [f_buf[k, t, c, r].astype(F32) * a_buf[k, t, c, r].astype(F32) for c in range(6)]
            h1 = (prod[0] + prod[1]) - (prod[3] + prod[4])
            v1 = prod[2] - prod[5]
            hor = h1 if hor is None else hor + h1
            ver = v1 if ver is None else ver + v1
        out[0, r] = hor * (c_buf[k, 0, r] * SCALE)
        out[1, r] = ver * (c_buf[k, 1, r] * SCALE)


def sent_kernel(
    idx_ref, f_hbm, a_hbm, c_hbm, t_hbm, far2, one, three, d_own, d_odd, d_core, d_cross, f_buf, a_buf, c_buf, t_buf,
    sems, t_sems
):
    n = len(SENT)
    copies = start_products(idx_ref, f_hbm, a_hbm, c_hbm, f_buf, a_buf, c_buf, sems, n)
    t_copies = [pltpu.make_async_copy(t_hbm.at[:, idx_ref[n + k]], t_buf.at[k], t_sems.at[k]) for k in range(2)]
    for copy in t_copies:
        copy.start()
    for k, out in enumerate((far2, one.at[0], one.at[1], three.at[0], three.at[1])):
        block_products(k, copies, f_buf, a_buf, c_buf, out)
    inside, even = idx_ref[n + 2] > 0, idx_ref[n + 3] > 0
    for copy in t_copies:
        copy.wait()
    for k, out in enumerate((d_own, d_odd)):
        for e in range(6):
            for r in range(4):
                cells = t_buf[k, e, r].astype(F32)
                if k == 1:
                    cells = jnp.where(inside, cells, 0.0)
                out[e, r] = cells
                d_core[k, e, r] = jnp.where(even, cells[24:], cells[:8])
                d_cross[k, e, r] = jnp.where(even, cells[:8], cells[24:])


def kept_kernel(idx_ref, f_hbm, a_hbm, c_hbm, near2, far0, near0, f_buf, a_buf, c_buf, sems):
    copies = start_products(idx_ref, f_hbm, a_hbm, c_hbm, f_buf, a_buf, c_buf, sems, len(KEPT))
    for k, out in enumerate((near2, far0, near0)):
        block_products(k, copies, f_buf, a_buf, c_buf, out)


def products_scratch(n):
    return [
        pltpu.VMEM((n, 2, 6, 4, 32, 128), jnp.bfloat16),
        pltpu.VMEM((n, 2, 6, 4, 32, 128), jnp.bfloat16),
        pltpu.VMEM((n, *SLAB), F32),
    ]


def in_hbm(*arrays):
    return [pltpu.with_memory_space_constraint(x, pltpu.HBM) for x in arrays]


def sent_products(idx, fwd, adj, cond, tens):
    hbm = pl.BlockSpec(memory_space=pltpu.HBM)
    pair = jax.ShapeDtypeStruct((2, *SLAB), F32)
    rim = jax.ShapeDtypeStruct((6, 4, 32, 128), F32)
    tiles = jax.ShapeDtypeStruct((2, 6, 4, 8, 128), F32)
    return pl.pallas_call(
        sent_kernel,
        in_specs=[pl.BlockSpec(memory_space=pltpu.SMEM), hbm, hbm, hbm, hbm],
        out_shape=[jax.ShapeDtypeStruct(SLAB, F32), pair, pair, rim, rim, tiles, tiles],
        scratch_shapes=products_scratch(len(SENT))
        + [
            pltpu.VMEM((2, 6, 4, 32, 128), jnp.bfloat16),
            pltpu.SemaphoreType.DMA((3, len(SENT))),
            pltpu.SemaphoreType.DMA((2,)),
        ],
        compiler_params=pltpu.CompilerParams(vmem_limit_bytes=32 << 20),
    )(idx, *in_hbm(fwd, adj, cond, tens))


def kept_products(idx, fwd, adj, cond):
    hbm = pl.BlockSpec(memory_space=pltpu.HBM)
    return pl.pallas_call(
        kept_kernel,
        in_specs=[pl.BlockSpec(memory_space=pltpu.SMEM), hbm, hbm, hbm],
        out_shape=[jax.ShapeDtypeStruct(SLAB, F32)] * 3,
        scratch_shapes=products_scratch(len(KEPT)) + [pltpu.SemaphoreType.DMA((3, len(KEPT)))],
        compiler_params=pltpu.CompilerParams(vmem_limit_bytes=32 << 20),
    )(idx, *in_hbm(fwd, adj, cond))


def diffuse_kernel(f_lo, f_own, f_hi, d_lo, d_own, d_hi, out, buf, after, part, flux_z):
    fs, ds = (f_lo, f_own, f_hi), (d_lo, d_own, d_hi)
    lane = lax.broadcasted_iota(jnp.int32, (40, 128), 1)
    first, last = lane == 0, lane == 127

    def tensor(e, r):
        return ds[(r + 4) // 4][e, (r + 4) % 4]

    for p in range(PASSES):
        m = PASSES - 1 - p

        def field(c, r):
            if p == 0:
                return fs[(r + 4) // 4][c, (r + 4) % 4]
            return buf[(p - 1) % 2, c, r + 4]

        for r in range(-m - 1, 4 + m):
            for c in range(2):
                after[c, r + 4] = jnp.where(last, 0.0, pltpu.roll(field(c, r), 127, 1))
        flux_x_before = [None, None]
        here = [field(c, -m - 1) for c in range(2)]
        for r in range(-m - 1, 4 + m):
            d = [tensor(e, r) for e in range(6)]
            for c in range(2):
                f = here[c]
                nxt = field(c, r + 1)
                gx = nxt - f
                gy = pltpu.roll(f, 39, 0) - f
                gz = after[c, r + 4] - f
                fx = d[0] * gx + d[3] * gy + d[4] * gz
                if r >= -m:
                    fy = d[3] * gx + d[1] * gy + d[5] * gz
                    fz = d[4] * gx + d[5] * gy + d[2] * gz
                    part[c, r + 4] = (fx - flux_x_before[c]) + (fy - pltpu.roll(fy, 1, 0)) + fz
                    flux_z[c, r + 4] = fz
                flux_x_before[c] = fx
                here[c] = nxt
        for r in range(-m, 4 + m):
            gain = jnp.where(tensor(0, r) > 0, F32(STEP), F32(0))
            for c in range(2):
                spread = part[c, r + 4] - jnp.where(first, 0.0, pltpu.roll(flux_z[c, r + 4], 1, 1))
                new = field(c, r) + gain * spread
                if p == PASSES - 1:
                    out[c, r] = new[:32]
                else:
                    buf[p % 2, c, r + 4] = new


def diffuse(*args):
    rows = pltpu.VMEM((2, 12, 40, 128), F32)
    return pl.pallas_call(
        diffuse_kernel,
        out_shape=jax.ShapeDtypeStruct(SLAB, F32),
        scratch_shapes=[pltpu.VMEM((2, 2, 12, 40, 128), F32), rows, rows, rows],
        compiler_params=pltpu.CompilerParams(vmem_limit_bytes=32 << 20),
    )(*args)


def core_tile(cells, even):
    return jnp.where(even, cells[..., 24:, :], cells[..., :8, :])


def cross_tile(cells, even):
    return jnp.where(even, cells[..., :8, :], cells[..., 24:, :])


def halo_tile(core, cross, even):
    right, left = jnp.where(even, core, cross), jnp.where(even, cross, core)
    row = lax.broadcasted_iota(jnp.int32, right.shape, right.ndim - 2)
    return jnp.where(row < 4, right, left)


def shards(fwd, adj, cond, tens):
    s, gx, gy = lax.axis_index("source"), lax.axis_index("gx"), lax.axis_index("gy")
    h, z = s // NZC, s % NZC
    own = block_of(h, z)
    x_even, y_even = gx % 2 == 0, gy % 2 == 0

    def blocks(keys):
        return [block_of(jnp.where(half == 0, 1 - h, h), z ^ k) for half, k in keys]

    wrap = own + jnp.where(gx == 0, 1, 0) - jnp.where(gx == 3, 1, 0)
    inside = jnp.where((wrap >= 0) & (wrap < BLOCKS), 1, 0)
    sent_idx = jnp.stack(blocks(SENT) + [own, jnp.clip(wrap, 0, BLOCKS - 1), inside, jnp.where(y_even, 1, 0)])
    kept_idx = jnp.stack(blocks(KEPT)).astype(jnp.int32)
    far2, one, three, d_own, d_odd, d_core, d_cross = sent_products(sent_idx.astype(jnp.int32), fwd, adj, cond, tens)
    kept_idx, far2, one, three = lax.optimization_barrier((kept_idx, far2, one, three))
    near2, far0, near0 = kept_products(kept_idx, fwd, adj, cond)

    two_add = near2 + lax.ppermute(far2, "source", Y_PERM)
    two_in = lax.ppermute(two_add, "source", z_perm(2))
    one_in = lax.ppermute(one, "source", z_perm(1))
    three_in = lax.ppermute(three, "source", z_perm(3))
    far_sum = far0 + one_in[0] + three_in[0]
    from_far = lax.ppermute(far_sum, "source", Y_PERM)
    field = two_in + (near0 + one_in[1] + three_in[1]) + from_far

    _, d_core, d_cross = lax.optimization_barrier((two_add, d_core, d_cross))
    d_core = lax.ppermute(d_core, "gy", CORE_PERM)
    d_cross = lax.ppermute(d_cross, "gy", CROSS_PERM)
    tiles = halo_tile(d_core, d_cross, y_even)
    d_own = jnp.concatenate([d_own, tiles[0]], axis=-2)
    d_odd = jnp.concatenate([d_odd, tiles[1]], axis=-2)
    d_even_in = lax.ppermute(d_own, "gx", X_EVEN)
    d_odd_in = lax.ppermute(d_odd, "gx", X_ODD_RING)

    core = lax.ppermute(core_tile(field, y_even), "gy", CORE_PERM)
    cross = lax.ppermute(cross_tile(field, y_even), "gy", CROSS_PERM)
    f_own = jnp.concatenate([field, halo_tile(core, cross, y_even)], axis=-2)
    f_own, d_even_in, d_odd_in = lax.optimization_barrier((f_own, d_even_in, d_odd_in))
    d_lo = jnp.where(x_even, d_odd_in, d_even_in)
    d_hi = jnp.where(x_even, d_even_in, d_odd_in)
    f_even_in = lax.ppermute(f_own, "gx", X_EVEN)
    f_odd_in = lax.ppermute(f_own, ("source", "gx"), x_odd_owner())
    f_lo = jnp.where(x_even, f_odd_in, f_even_in)
    f_hi = jnp.where(x_even, f_even_in, f_odd_in)

    done = diffuse(f_lo, f_own, f_hi, d_lo, d_own, d_hi)

    two = lax.ppermute(done, "source", z_perm(2))
    other = lax.ppermute(done, "source", Y_PERM)
    one, three = (lax.ppermute(done, "source", z_perm(k)) for k in (1, 3))
    other_two = lax.ppermute(two, "source", Y_PERM)
    other_one, other_three = (lax.ppermute(other, "source", z_perm(k)) for k in (1, 3))
    out = jnp.zeros((2, BLOCKS, 4, 32, 128), F32)
    for half, k, piece in (
        (h, 2, two),
        (h, 0, done),
        (1 - h, 0, other),
        (h, 1, one),
        (h, 3, three),
        (1 - h, 2, other_two),
        (1 - h, 1, other_one),
        (1 - h, 3, other_three),
    ):
        out = lax.dynamic_update_index_in_dim(out, piece, block_of(half, z ^ k), 1)
    return out


def solution(mesh):
    fields = P("source", None, None, "gx", "gy", None)
    cells = P(None, None, "gx", "gy", None)
    return jax.shard_map(
        shards, mesh=mesh, in_specs=(fields, fields, cells, cells), out_specs=cells, check_vma=False
    )
```

```python
import jax
import jax.numpy as jnp
from jax import lax
from jax.experimental import pallas as pl
from jax.experimental.pallas import tpu as pltpu
from jax.sharding import PartitionSpec as P

PASSES = 4
STEP = 0.13
SCALE = 1.0 / 16.0
NZC = 4
BLOCKS = 2 * NZC
F32 = jnp.float32
SLAB = (2, 4, 32, 128)


def block_of(h, z):
    return jnp.where(h == 0, z, BLOCKS - 1 - z)


def source_of(b):
    return b if b < NZC else 3 * NZC - 1 - b


def z_perm(k):
    return [(s, s ^ k) for s in range(BLOCKS)]


Y_PERM = [(s, (s + NZC) % BLOCKS) for s in range(BLOCKS)]
CORE_PERM = [(i, i ^ 1) for i in range(4)]
CROSS_PERM = [(1, 2), (2, 1)]
X_EVEN = [(i, i ^ 1) for i in range(4)]
X_ODD_RING = [(1, 2), (2, 1), (3, 0), (0, 3)]


def x_odd_owner():
    pairs = []
    for s in range(BLOCKS):
        pairs += [(s * 4 + 1, s * 4 + 2), (s * 4 + 2, s * 4 + 1)]
    for b in range(BLOCKS - 1):
        low, high = source_of(b) * 4 + 3, source_of(b + 1) * 4
        pairs += [(low, high), (high, low)]
    return pairs


ORDER = [(0, 2), (0, 1), (1, 1), (0, 3), (1, 3), (1, 2), (0, 0), (1, 0)]


def products_kernel(
    idx_ref, f_hbm, a_hbm, c_hbm, t_hbm, far2, one, three, near2, far0, near0, d_own, d_odd, f_buf, a_buf, c_buf, t_buf,
    sems, t_sems
):
    copies = []
    for k in range(BLOCKS):
        b = idx_ref[k]
        group = [
            pltpu.make_async_copy(f_hbm.at[:, :, b], f_buf.at[k], sems.at[0, k]),
            pltpu.make_async_copy(a_hbm.at[:, :, b], a_buf.at[k], sems.at[1, k]),
            pltpu.make_async_copy(c_hbm.at[:, b], c_buf.at[k], sems.at[2, k]),
        ]
        for copy in group:
            copy.start()
        copies.append(group)
        if k == 1:
            t_copies = [
                pltpu.make_async_copy(t_hbm.at[:, idx_ref[BLOCKS + i]], t_buf.at[i], t_sems.at[i]) for i in range(2)
            ]
            for copy in t_copies:
                copy.start()
    for k, out in enumerate((far2, one.at[0], one.at[1], three.at[0], three.at[1], near2, far0, near0)):
        for copy in copies[k]:
            copy.wait()
        for r in range(4):
            hor = ver = None
            for t in range(2):
                prod = [f_buf[k, t, c, r].astype(F32) * a_buf[k, t, c, r].astype(F32) for c in range(6)]
                h1 = (prod[0] + prod[1]) - (prod[3] + prod[4])
                v1 = prod[2] - prod[5]
                hor = h1 if hor is None else hor + h1
                ver = v1 if ver is None else ver + v1
            out[0, r] = hor * (c_buf[k, 0, r] * SCALE)
            out[1, r] = ver * (c_buf[k, 1, r] * SCALE)
        if k == 2:
            inside = idx_ref[BLOCKS + 2] > 0
            for copy in t_copies:
                copy.wait()
            for e in range(6):
                for r in range(4):
                    d_own[e, r] = t_buf[0, e, r].astype(F32)
                    d_odd[e, r] = jnp.where(inside, t_buf[1, e, r].astype(F32), 0.0)


def in_hbm(*arrays):
    return [pltpu.with_memory_space_constraint(x, pltpu.HBM) for x in arrays]


def products(idx, fwd, adj, cond, tens):
    hbm = pl.BlockSpec(memory_space=pltpu.HBM)
    slab = jax.ShapeDtypeStruct(SLAB, F32)
    pair = jax.ShapeDtypeStruct((2, *SLAB), F32)
    rim = jax.ShapeDtypeStruct((6, 4, 32, 128), F32)
    return pl.pallas_call(
        products_kernel,
        in_specs=[pl.BlockSpec(memory_space=pltpu.SMEM), hbm, hbm, hbm, hbm],
        out_shape=[slab, pair, pair, slab, slab, slab, rim, rim],
        scratch_shapes=[
            pltpu.VMEM((BLOCKS, 2, 6, 4, 32, 128), jnp.bfloat16),
            pltpu.VMEM((BLOCKS, 2, 6, 4, 32, 128), jnp.bfloat16),
            pltpu.VMEM((BLOCKS, *SLAB), F32),
            pltpu.VMEM((2, 6, 4, 32, 128), jnp.bfloat16),
            pltpu.SemaphoreType.DMA((3, BLOCKS)),
            pltpu.SemaphoreType.DMA((2,)),
        ],
        compiler_params=pltpu.CompilerParams(vmem_limit_bytes=32 << 20),
    )(idx, *in_hbm(fwd, adj, cond, tens))


def diffuse_kernel(f_lo, f_own, f_hi, d_lo, d_own, d_hi, d_tile, out, buf, after, part, flux_z):
    fs, ds = (f_lo, f_own, f_hi), (d_lo, d_own, d_hi)
    lane = lax.broadcasted_iota(jnp.int32, (40, 128), 1)
    first, last = lane == 0, lane == 127

    def tensor(e, r):
        return jnp.concatenate([ds[(r + 4) // 4][e, (r + 4) % 4], d_tile[e, r + 4]], axis=0)

    for p in range(PASSES):
        m = PASSES - 1 - p

        def field(c, r):
            if p == 0:
                return fs[(r + 4) // 4][c, (r + 4) % 4]
            return buf[(p - 1) % 2, c, r + 4]

        for r in range(-m - 1, 4 + m):
            for c in range(2):
                after[c, r + 4] = jnp.where(last, 0.0, pltpu.roll(field(c, r), 127, 1))
        flux_x_before = [None, None]
        here = [field(c, -m - 1) for c in range(2)]
        for r in range(-m - 1, 4 + m):
            d = [tensor(e, r) for e in range(6)]
            for c in range(2):
                f = here[c]
                nxt = field(c, r + 1)
                gx = nxt - f
                gy = pltpu.roll(f, 39, 0) - f
                gz = after[c, r + 4] - f
                fx = d[0] * gx + d[3] * gy + d[4] * gz
                if r >= -m:
                    fy = d[3] * gx + d[1] * gy + d[5] * gz
                    fz = d[4] * gx + d[5] * gy + d[2] * gz
                    part[c, r + 4] = (fx - flux_x_before[c]) + (fy - pltpu.roll(fy, 1, 0)) + fz
                    flux_z[c, r + 4] = fz
                flux_x_before[c] = fx
                here[c] = nxt
        for r in range(-m, 4 + m):
            gain = jnp.where(tensor(0, r) > 0, F32(STEP), F32(0))
            for c in range(2):
                spread = part[c, r + 4] - jnp.where(first, 0.0, pltpu.roll(flux_z[c, r + 4], 1, 1))
                new = field(c, r) + gain * spread
                if p == PASSES - 1:
                    out[c, r] = new[:32]
                else:
                    buf[p % 2, c, r + 4] = new


def diffuse(*args):
    rows = pltpu.VMEM((2, 12, 40, 128), F32)
    return pl.pallas_call(
        diffuse_kernel,
        out_shape=jax.ShapeDtypeStruct(SLAB, F32),
        scratch_shapes=[pltpu.VMEM((2, 2, 12, 40, 128), F32), rows, rows, rows],
        compiler_params=pltpu.CompilerParams(vmem_limit_bytes=32 << 20),
    )(*args)


def core_tile(cells, even):
    return jnp.where(even, cells[..., 28:, :], cells[..., :4, :])


def cross_tile(cells, even):
    return jnp.where(even, cells[..., :4, :], cells[..., 28:, :])


def halo_tile(core, cross, even):
    return jnp.concatenate([jnp.where(even, core, cross), jnp.where(even, cross, core)], axis=-2)


def shards(fwd, adj, cond, tens):
    s, gx, gy = lax.axis_index("source"), lax.axis_index("gx"), lax.axis_index("gy")
    h, z = s // NZC, s % NZC
    own = block_of(h, z)
    x_even, y_even = gx % 2 == 0, gy % 2 == 0

    blocks = [block_of(jnp.where(half == 0, 1 - h, h), z ^ k) for half, k in ORDER]
    wrap = own + jnp.where(gx == 0, 1, 0) - jnp.where(gx == 3, 1, 0)
    inside = jnp.where((wrap >= 0) & (wrap < BLOCKS), 1, 0)
    idx = jnp.stack(blocks + [own, jnp.clip(wrap, 0, BLOCKS - 1), inside]).astype(jnp.int32)
    far2, one, three, near2, far0, near0, d_own, d_odd = products(idx, fwd, adj, cond, tens)

    two_sum = near2 + lax.ppermute(far2, "source", Y_PERM)
    two_in = lax.ppermute(two_sum, "source", z_perm(2))
    one_in = lax.ppermute(one, "source", z_perm(1))
    three_in = lax.ppermute(three, "source", z_perm(3))
    far_sum = far0 + one_in[0] + three_in[0]
    near_sum = near0 + one_in[1] + three_in[1]
    from_far = lax.ppermute(far_sum, "source", Y_PERM)

    _, d_own, d_odd = lax.optimization_barrier((two_sum, d_own, d_odd))
    d_even_in = lax.ppermute(d_own, "gx", X_EVEN)
    d_odd_in = lax.ppermute(d_odd, "gx", X_ODD_RING)
    near_sum, two_in, d_even_in, d_odd_in = lax.optimization_barrier((near_sum, two_in, d_even_in, d_odd_in))
    d_lo = jnp.where(x_even, d_odd_in, d_even_in)
    d_hi = jnp.where(x_even, d_even_in, d_odd_in)
    from_far, d_lo, d_hi = lax.optimization_barrier((from_far, d_lo, d_hi))
    field = two_in + near_sum + from_far

    core = lax.ppermute(core_tile(field, y_even), "gy", CORE_PERM)
    cross = lax.ppermute(cross_tile(field, y_even), "gy", CROSS_PERM)
    f_own = jnp.concatenate([field, halo_tile(core, cross, y_even)], axis=-2)
    d_all = jnp.concatenate([d_lo, d_own, d_hi], axis=1)
    f_own, d_all = lax.optimization_barrier((f_own, d_all))
    d_cross = lax.ppermute(cross_tile(d_all, y_even), "gy", CROSS_PERM)
    d_core = lax.ppermute(core_tile(d_all, y_even), "gy", CORE_PERM)
    f_odd_in = lax.ppermute(f_own, ("source", "gx"), x_odd_owner())
    f_even_in = lax.ppermute(f_own, "gx", X_EVEN)
    f_hi = jnp.where(x_even, f_even_in, f_odd_in)
    f_lo = jnp.where(x_even, f_odd_in, f_even_in)

    f_hi, f_lo, d_cross = lax.optimization_barrier((f_hi, f_lo, d_cross))
    d_cross, d_core = lax.optimization_barrier((d_cross, d_core))
    d_tile = halo_tile(d_core, d_cross, y_even)
    done = diffuse(f_lo, f_own, f_hi, d_lo, d_own, d_hi, d_tile)

    two = lax.ppermute(done, "source", z_perm(2))
    other = lax.ppermute(done, "source", Y_PERM)
    one, three = (lax.ppermute(done, "source", z_perm(k)) for k in (1, 3))
    other_two = lax.ppermute(two, "source", Y_PERM)
    other_one, other_three = (lax.ppermute(other, "source", z_perm(k)) for k in (1, 3))
    out = jnp.zeros((2, BLOCKS, 4, 32, 128), F32)
    for half, k, piece in (
        (h, 2, two),
        (h, 0, done),
        (1 - h, 0, other),
        (h, 1, one),
        (h, 3, three),
        (1 - h, 2, other_two),
        (1 - h, 1, other_one),
        (1 - h, 3, other_three),
    ):
        out = lax.dynamic_update_index_in_dim(out, piece, block_of(half, z ^ k), 1)
    return out


def solution(mesh):
    fields = P("source", None, None, "gx", "gy", None)
    cells = P(None, None, "gx", "gy", None)
    return jax.shard_map(
        shards, mesh=mesh, in_specs=(fields, fields, cells, cells), out_specs=cells, check_vma=False
    )
```

```python
import jax
import jax.numpy as jnp
from jax import lax
from jax.experimental import pallas as pl
from jax.experimental.pallas import tpu as pltpu
from jax.sharding import PartitionSpec as P

PASSES = 4
STEP = 0.13
SCALE = 1.0 / 16.0
NZC = 4
BLOCKS = 2 * NZC
F32 = jnp.float32
SLAB = (2, 4, 32, 128)


def block_of(h, z):
    return jnp.where(h == 0, z, BLOCKS - 1 - z)


def source_of(b):
    return b if b < NZC else 3 * NZC - 1 - b


def z_perm(k):
    return [(s, s ^ k) for s in range(BLOCKS)]


Y_PERM = [(s, (s + NZC) % BLOCKS) for s in range(BLOCKS)]
CORE_PERM = [(i, i ^ 1) for i in range(4)]
CROSS_PERM = [(1, 2), (2, 1)]
X_EVEN = [(i, i ^ 1) for i in range(4)]
X_ODD_RING = [(1, 2), (2, 1), (3, 0), (0, 3)]


def x_odd_owner():
    pairs = []
    for s in range(BLOCKS):
        pairs += [(s * 4 + 1, s * 4 + 2), (s * 4 + 2, s * 4 + 1)]
    for b in range(BLOCKS - 1):
        low, high = source_of(b) * 4 + 3, source_of(b + 1) * 4
        pairs += [(low, high), (high, low)]
    return pairs


SENT = [(0, 2), (0, 1), (1, 1), (0, 3), (1, 3)]
KEPT = [(1, 2), (0, 0), (1, 0)]


def start_products(idx_ref, f_hbm, a_hbm, c_hbm, f_buf, a_buf, c_buf, sems, count):
    copies = []
    for k in range(count):
        b = idx_ref[k]
        group = [
            pltpu.make_async_copy(f_hbm.at[:, :, b], f_buf.at[k], sems.at[0, k]),
            pltpu.make_async_copy(a_hbm.at[:, :, b], a_buf.at[k], sems.at[1, k]),
            pltpu.make_async_copy(c_hbm.at[:, b], c_buf.at[k], sems.at[2, k]),
        ]
        for copy in group:
            copy.start()
        copies.append(group)
    return copies


def block_products(k, copies, f_buf, a_buf, c_buf, out):
    for copy in copies[k]:
        copy.wait()
    for r in range(4):
        hor = ver = None
        for t in range(2):
            prod = [f_buf[k, t, c, r].astype(F32) * a_buf[k, t, c, r].astype(F32) for c in range(6)]
            h1 = (prod[0] + prod[1]) - (prod[3] + prod[4])
            v1 = prod[2] - prod[5]
            hor = h1 if hor is None else hor + h1
            ver = v1 if ver is None else ver + v1
        out[0, r] = hor * (c_buf[k, 0, r] * SCALE)
        out[1, r] = ver * (c_buf[k, 1, r] * SCALE)


def sent_kernel(
    idx_ref, f_hbm, a_hbm, c_hbm, t_hbm, far2, one, three, d_own, d_odd, f_buf, a_buf, c_buf, t_buf, sems, t_sems
):
    n = len(SENT)
    t_copies = [pltpu.make_async_copy(t_hbm.at[:, idx_ref[n + k]], t_buf.at[k], t_sems.at[k]) for k in range(2)]
    for copy in t_copies:
        copy.start()
    copies = start_products(idx_ref, f_hbm, a_hbm, c_hbm, f_buf, a_buf, c_buf, sems, n)
    inside = idx_ref[n + 2] > 0
    for copy in t_copies:
        copy.wait()
    for e in range(6):
        for r in range(4):
            d_own[e, r] = t_buf[0, e, r].astype(F32)
            d_odd[e, r] = jnp.where(inside, t_buf[1, e, r].astype(F32), 0.0)
    for k, out in enumerate((far2, one.at[0], one.at[1], three.at[0], three.at[1])):
        block_products(k, copies, f_buf, a_buf, c_buf, out)


def kept_kernel(idx_ref, f_hbm, a_hbm, c_hbm, near2, far0, near0, f_buf, a_buf, c_buf, sems):
    copies = start_products(idx_ref, f_hbm, a_hbm, c_hbm, f_buf, a_buf, c_buf, sems, len(KEPT))
    for k, out in enumerate((near2, far0, near0)):
        block_products(k, copies, f_buf, a_buf, c_buf, out)


def products_scratch(n):
    return [
        pltpu.VMEM((n, 2, 6, 4, 32, 128), jnp.bfloat16),
        pltpu.VMEM((n, 2, 6, 4, 32, 128), jnp.bfloat16),
        pltpu.VMEM((n, *SLAB), F32),
    ]


def in_hbm(*arrays):
    return [pltpu.with_memory_space_constraint(x, pltpu.HBM) for x in arrays]


def sent_products(idx, fwd, adj, cond, tens):
    hbm = pl.BlockSpec(memory_space=pltpu.HBM)
    pair = jax.ShapeDtypeStruct((2, *SLAB), F32)
    rim = jax.ShapeDtypeStruct((6, 4, 32, 128), F32)
    return pl.pallas_call(
        sent_kernel,
        in_specs=[pl.BlockSpec(memory_space=pltpu.SMEM), hbm, hbm, hbm, hbm],
        out_shape=[jax.ShapeDtypeStruct(SLAB, F32), pair, pair, rim, rim],
        scratch_shapes=products_scratch(len(SENT))
        + [
            pltpu.VMEM((2, 6, 4, 32, 128), jnp.bfloat16),
            pltpu.SemaphoreType.DMA((3, len(SENT))),
            pltpu.SemaphoreType.DMA((2,)),
        ],
        compiler_params=pltpu.CompilerParams(vmem_limit_bytes=32 << 20),
    )(idx, *in_hbm(fwd, adj, cond, tens))


def kept_products(idx, fwd, adj, cond):
    hbm = pl.BlockSpec(memory_space=pltpu.HBM)
    return pl.pallas_call(
        kept_kernel,
        in_specs=[pl.BlockSpec(memory_space=pltpu.SMEM), hbm, hbm, hbm],
        out_shape=[jax.ShapeDtypeStruct(SLAB, F32)] * 3,
        scratch_shapes=products_scratch(len(KEPT)) + [pltpu.SemaphoreType.DMA((3, len(KEPT)))],
        compiler_params=pltpu.CompilerParams(vmem_limit_bytes=32 << 20),
    )(idx, *in_hbm(fwd, adj, cond))


def diffuse_kernel(f_lo, f_own, f_hi, d_lo, d_own, d_hi, d_tile, out, buf, after, part, flux_z):
    fs, ds = (f_lo, f_own, f_hi), (d_lo, d_own, d_hi)
    lane = lax.broadcasted_iota(jnp.int32, (40, 128), 1)
    first, last = lane == 0, lane == 127

    def tensor(e, r):
        return jnp.concatenate([ds[(r + 4) // 4][e, (r + 4) % 4], d_tile[e, r + 4]], axis=0)

    for p in range(PASSES):
        m = PASSES - 1 - p

        def field(c, r):
            if p == 0:
                return fs[(r + 4) // 4][c, (r + 4) % 4]
            return buf[(p - 1) % 2, c, r + 4]

        for r in range(-m - 1, 4 + m):
            for c in range(2):
                after[c, r + 4] = jnp.where(last, 0.0, pltpu.roll(field(c, r), 127, 1))
        flux_x_before = [None, None]
        here = [field(c, -m - 1) for c in range(2)]
        for r in range(-m - 1, 4 + m):
            d = [tensor(e, r) for e in range(6)]
            for c in range(2):
                f = here[c]
                nxt = field(c, r + 1)
                gx = nxt - f
                gy = pltpu.roll(f, 39, 0) - f
                gz = after[c, r + 4] - f
                fx = d[0] * gx + d[3] * gy + d[4] * gz
                if r >= -m:
                    fy = d[3] * gx + d[1] * gy + d[5] * gz
                    fz = d[4] * gx + d[5] * gy + d[2] * gz
                    part[c, r + 4] = (fx - flux_x_before[c]) + (fy - pltpu.roll(fy, 1, 0)) + fz
                    flux_z[c, r + 4] = fz
                flux_x_before[c] = fx
                here[c] = nxt
        for r in range(-m, 4 + m):
            gain = jnp.where(tensor(0, r) > 0, F32(STEP), F32(0))
            for c in range(2):
                spread = part[c, r + 4] - jnp.where(first, 0.0, pltpu.roll(flux_z[c, r + 4], 1, 1))
                new = field(c, r) + gain * spread
                if p == PASSES - 1:
                    out[c, r] = new[:32]
                else:
                    buf[p % 2, c, r + 4] = new


def diffuse(*args):
    rows = pltpu.VMEM((2, 12, 40, 128), F32)
    return pl.pallas_call(
        diffuse_kernel,
        out_shape=jax.ShapeDtypeStruct(SLAB, F32),
        scratch_shapes=[pltpu.VMEM((2, 2, 12, 40, 128), F32), rows, rows, rows],
        compiler_params=pltpu.CompilerParams(vmem_limit_bytes=32 << 20),
    )(*args)


def core_tile(cells, even):
    return jnp.where(even, cells[..., 28:, :], cells[..., :4, :])


def cross_tile(cells, even):
    return jnp.where(even, cells[..., :4, :], cells[..., 28:, :])


def halo_tile(core, cross, even):
    return jnp.concatenate([jnp.where(even, core, cross), jnp.where(even, cross, core)], axis=-2)


def shards(fwd, adj, cond, tens):
    s, gx, gy = lax.axis_index("source"), lax.axis_index("gx"), lax.axis_index("gy")
    h, z = s // NZC, s % NZC
    own = block_of(h, z)
    x_even, y_even = gx % 2 == 0, gy % 2 == 0

    def blocks(keys):
        return [block_of(jnp.where(half == 0, 1 - h, h), z ^ k) for half, k in keys]

    wrap = own + jnp.where(gx == 0, 1, 0) - jnp.where(gx == 3, 1, 0)
    inside = jnp.where((wrap >= 0) & (wrap < BLOCKS), 1, 0)
    sent_idx = jnp.stack(blocks(SENT) + [own, jnp.clip(wrap, 0, BLOCKS - 1), inside]).astype(jnp.int32)
    kept_idx = jnp.stack(blocks(KEPT)).astype(jnp.int32)
    far2, one, three, d_own, d_odd = sent_products(sent_idx, fwd, adj, cond, tens)
    kept_idx, far2, one, three = lax.optimization_barrier((kept_idx, far2, one, three))
    near2, far0, near0 = kept_products(kept_idx, fwd, adj, cond)

    two_sum = near2 + lax.ppermute(far2, "source", Y_PERM)
    two_in = lax.ppermute(two_sum, "source", z_perm(2))
    one_in = lax.ppermute(one, "source", z_perm(1))
    three_in = lax.ppermute(three, "source", z_perm(3))
    far_sum = far0 + one_in[0] + three_in[0]
    near_sum = near0 + one_in[1] + three_in[1]
    from_far = lax.ppermute(far_sum, "source", Y_PERM)

    _, d_own, d_odd = lax.optimization_barrier((two_sum, d_own, d_odd))
    d_even_in = lax.ppermute(d_own, "gx", X_EVEN)
    d_odd_in = lax.ppermute(d_odd, "gx", X_ODD_RING)
    near_sum, two_in, d_even_in, d_odd_in = lax.optimization_barrier((near_sum, two_in, d_even_in, d_odd_in))
    d_lo = jnp.where(x_even, d_odd_in, d_even_in)
    d_hi = jnp.where(x_even, d_even_in, d_odd_in)
    from_far, d_lo, d_hi = lax.optimization_barrier((from_far, d_lo, d_hi))
    field = two_in + near_sum + from_far

    d_all = jnp.concatenate([d_lo, d_own, d_hi], axis=1)
    both = jnp.concatenate([field.reshape(8, 32, 128), d_all.reshape(72, 32, 128)], axis=0)
    core = lax.ppermute(core_tile(both, y_even), "gy", CORE_PERM)
    cross = lax.ppermute(cross_tile(both, y_even), "gy", CROSS_PERM)
    tiles = halo_tile(core, cross, y_even)
    d_tile = tiles[8:].reshape(6, 12, 8, 128)
    f_own = jnp.concatenate([field, tiles[:8].reshape(2, 4, 8, 128)], axis=-2)
    f_odd_in = lax.ppermute(f_own, ("source", "gx"), x_odd_owner())
    f_even_in = lax.ppermute(f_own, "gx", X_EVEN)
    f_hi = jnp.where(x_even, f_even_in, f_odd_in)
    f_lo = jnp.where(x_even, f_odd_in, f_even_in)

    done = diffuse(f_lo, f_own, f_hi, d_lo, d_own, d_hi, d_tile)

    two = lax.ppermute(done, "source", z_perm(2))
    other = lax.ppermute(done, "source", Y_PERM)
    one, three = (lax.ppermute(done, "source", z_perm(k)) for k in (1, 3))
    other_two = lax.ppermute(two, "source", Y_PERM)
    other_one, other_three = (lax.ppermute(other, "source", z_perm(k)) for k in (1, 3))
    out = jnp.zeros((2, BLOCKS, 4, 32, 128), F32)
    for half, k, piece in (
        (h, 2, two),
        (h, 0, done),
        (1 - h, 0, other),
        (h, 1, one),
        (h, 3, three),
        (1 - h, 2, other_two),
        (1 - h, 1, other_one),
        (1 - h, 3, other_three),
    ):
        out = lax.dynamic_update_index_in_dim(out, piece, block_of(half, z ^ k), 1)
    return out


def solution(mesh):
    fields = P("source", None, None, "gx", "gy", None)
    cells = P(None, None, "gx", "gy", None)
    return jax.shard_map(
        shards, mesh=mesh, in_specs=(fields, fields, cells, cells), out_specs=cells, check_vma=False
    )
```

```python
import jax
import jax.numpy as jnp
from jax import lax
from jax.experimental import pallas as pl
from jax.experimental.pallas import tpu as pltpu
from jax.sharding import PartitionSpec as P

PASSES = 4
STEP = 0.13
SCALE = 1.0 / 16.0
NZC = 4
BLOCKS = 2 * NZC
F32 = jnp.float32
SLAB = (2, 4, 32, 128)


def block_of(h, z):
    return jnp.where(h == 0, z, BLOCKS - 1 - z)


def source_of(b):
    return b if b < NZC else 3 * NZC - 1 - b


def z_perm(k):
    return [(s, s ^ k) for s in range(BLOCKS)]


Y_PERM = [(s, (s + NZC) % BLOCKS) for s in range(BLOCKS)]
CORE_PERM = [(i, i ^ 1) for i in range(4)]
CROSS_PERM = [(1, 2), (2, 1)]
X_EVEN = [(i, i ^ 1) for i in range(4)]
X_ODD_RING = [(1, 2), (2, 1), (3, 0), (0, 3)]


def x_odd_owner():
    pairs = []
    for s in range(BLOCKS):
        pairs += [(s * 4 + 1, s * 4 + 2), (s * 4 + 2, s * 4 + 1)]
    for b in range(BLOCKS - 1):
        low, high = source_of(b) * 4 + 3, source_of(b + 1) * 4
        pairs += [(low, high), (high, low)]
    return pairs


SENT = [(0, 2), (0, 1), (1, 1), (0, 3), (1, 3)]
KEPT = [(1, 2), (0, 0), (1, 0)]


def start_products(idx_ref, f_hbm, a_hbm, c_hbm, f_buf, a_buf, c_buf, sems, count):
    copies = []
    for k in range(count):
        b = idx_ref[k]
        group = [
            pltpu.make_async_copy(f_hbm.at[:, :, b], f_buf.at[k], sems.at[0, k]),
            pltpu.make_async_copy(a_hbm.at[:, :, b], a_buf.at[k], sems.at[1, k]),
            pltpu.make_async_copy(c_hbm.at[:, b], c_buf.at[k], sems.at[2, k]),
        ]
        for copy in group:
            copy.start()
        copies.append(group)
    return copies


def block_products(k, copies, f_buf, a_buf, c_buf, out):
    for copy in copies[k]:
        copy.wait()
    for r in range(4):
        hor = ver = None
        for t in range(2):
            prod = [f_buf[k, t, c, r].astype(F32) * a_buf[k, t, c, r].astype(F32) for c in range(6)]
            h1 = (prod[0] + prod[1]) - (prod[3] + prod[4])
            v1 = prod[2] - prod[5]
            hor = h1 if hor is None else hor + h1
            ver = v1 if ver is None else ver + v1
        out[0, r] = hor * (c_buf[k, 0, r] * SCALE)
        out[1, r] = ver * (c_buf[k, 1, r] * SCALE)


def sent_kernel(
    idx_ref, f_hbm, a_hbm, c_hbm, t_hbm, far2, one, three, d_own, d_odd, f_buf, a_buf, c_buf, t_buf, sems, t_sems
):
    n = len(SENT)
    t_copies = [pltpu.make_async_copy(t_hbm.at[:, idx_ref[n + k]], t_buf.at[k], t_sems.at[k]) for k in range(2)]
    for copy in t_copies:
        copy.start()
    copies = start_products(idx_ref, f_hbm, a_hbm, c_hbm, f_buf, a_buf, c_buf, sems, n)
    inside = idx_ref[n + 2] > 0
    for copy in t_copies:
        copy.wait()
    for e in range(6):
        for r in range(4):
            d_own[e, r] = t_buf[0, e, r].astype(F32)
            d_odd[e, r] = jnp.where(inside, t_buf[1, e, r].astype(F32), 0.0)
    for k, out in enumerate((far2, one.at[0], one.at[1], three.at[0], three.at[1])):
        block_products(k, copies, f_buf, a_buf, c_buf, out)


def kept_kernel(idx_ref, f_hbm, a_hbm, c_hbm, near2, far0, near0, f_buf, a_buf, c_buf, sems):
    copies = start_products(idx_ref, f_hbm, a_hbm, c_hbm, f_buf, a_buf, c_buf, sems, len(KEPT))
    for k, out in enumerate((near2, far0, near0)):
        block_products(k, copies, f_buf, a_buf, c_buf, out)


def products_scratch(n):
    return [
        pltpu.VMEM((n, 2, 6, 4, 32, 128), jnp.bfloat16),
        pltpu.VMEM((n, 2, 6, 4, 32, 128), jnp.bfloat16),
        pltpu.VMEM((n, *SLAB), F32),
    ]


def in_hbm(*arrays):
    return [pltpu.with_memory_space_constraint(x, pltpu.HBM) for x in arrays]


def sent_products(idx, fwd, adj, cond, tens):
    hbm = pl.BlockSpec(memory_space=pltpu.HBM)
    pair = jax.ShapeDtypeStruct((2, *SLAB), F32)
    rim = jax.ShapeDtypeStruct((6, 4, 32, 128), F32)
    return pl.pallas_call(
        sent_kernel,
        in_specs=[pl.BlockSpec(memory_space=pltpu.SMEM), hbm, hbm, hbm, hbm],
        out_shape=[jax.ShapeDtypeStruct(SLAB, F32), pair, pair, rim, rim],
        scratch_shapes=products_scratch(len(SENT))
        + [
            pltpu.VMEM((2, 6, 4, 32, 128), jnp.bfloat16),
            pltpu.SemaphoreType.DMA((3, len(SENT))),
            pltpu.SemaphoreType.DMA((2,)),
        ],
        compiler_params=pltpu.CompilerParams(vmem_limit_bytes=32 << 20),
    )(idx, *in_hbm(fwd, adj, cond, tens))


def kept_products(idx, fwd, adj, cond):
    hbm = pl.BlockSpec(memory_space=pltpu.HBM)
    return pl.pallas_call(
        kept_kernel,
        in_specs=[pl.BlockSpec(memory_space=pltpu.SMEM), hbm, hbm, hbm],
        out_shape=[jax.ShapeDtypeStruct(SLAB, F32)] * 3,
        scratch_shapes=products_scratch(len(KEPT)) + [pltpu.SemaphoreType.DMA((3, len(KEPT)))],
        compiler_params=pltpu.CompilerParams(vmem_limit_bytes=32 << 20),
    )(idx, *in_hbm(fwd, adj, cond))


def diffuse_kernel(f_lo, f_own, f_hi, d_lo, d_own, d_hi, out, buf, after, part, flux_z):
    fs, ds = (f_lo, f_own, f_hi), (d_lo, d_own, d_hi)
    lane = lax.broadcasted_iota(jnp.int32, (40, 128), 1)
    first, last = lane == 0, lane == 127

    def tensor(e, r):
        return ds[(r + 4) // 4][e, (r + 4) % 4]

    for p in range(PASSES):
        m = PASSES - 1 - p

        def field(c, r):
            if p == 0:
                return fs[(r + 4) // 4][c, (r + 4) % 4]
            return buf[(p - 1) % 2, c, r + 4]

        for r in range(-m - 1, 4 + m):
            for c in range(2):
                after[c, r + 4] = jnp.where(last, 0.0, pltpu.roll(field(c, r), 127, 1))
        flux_x_before = [None, None]
        here = [field(c, -m - 1) for c in range(2)]
        for r in range(-m - 1, 4 + m):
            d = [tensor(e, r) for e in range(6)]
            for c in range(2):
                f = here[c]
                nxt = field(c, r + 1)
                gx = nxt - f
                gy = pltpu.roll(f, 39, 0) - f
                gz = after[c, r + 4] - f
                fx = d[0] * gx + d[3] * gy + d[4] * gz
                if r >= -m:
                    fy = d[3] * gx + d[1] * gy + d[5] * gz
                    fz = d[4] * gx + d[5] * gy + d[2] * gz
                    part[c, r + 4] = (fx - flux_x_before[c]) + (fy - pltpu.roll(fy, 1, 0)) + fz
                    flux_z[c, r + 4] = fz
                flux_x_before[c] = fx
                here[c] = nxt
        for r in range(-m, 4 + m):
            gain = jnp.where(tensor(0, r) > 0, F32(STEP), F32(0))
            for c in range(2):
                spread = part[c, r + 4] - jnp.where(first, 0.0, pltpu.roll(flux_z[c, r + 4], 1, 1))
                new = field(c, r) + gain * spread
                if p == PASSES - 1:
                    out[c, r] = new[:32]
                else:
                    buf[p % 2, c, r + 4] = new


def diffuse(*args):
    rows = pltpu.VMEM((2, 12, 40, 128), F32)
    return pl.pallas_call(
        diffuse_kernel,
        out_shape=jax.ShapeDtypeStruct(SLAB, F32),
        scratch_shapes=[pltpu.VMEM((2, 2, 12, 40, 128), F32), rows, rows, rows],
        compiler_params=pltpu.CompilerParams(vmem_limit_bytes=32 << 20),
    )(*args)


def core_tile(cells, even):
    return jnp.where(even, cells[..., 28:, :], cells[..., :4, :])


def cross_tile(cells, even):
    return jnp.where(even, cells[..., :4, :], cells[..., 28:, :])


def halo_tile(core, cross, even):
    return jnp.concatenate([jnp.where(even, core, cross), jnp.where(even, cross, core)], axis=-2)


def shards(fwd, adj, cond, tens):
    s, gx, gy = lax.axis_index("source"), lax.axis_index("gx"), lax.axis_index("gy")
    h, z = s // NZC, s % NZC
    own = block_of(h, z)
    x_even, y_even = gx % 2 == 0, gy % 2 == 0

    def blocks(keys):
        return [block_of(jnp.where(half == 0, 1 - h, h), z ^ k) for half, k in keys]

    wrap = own + jnp.where(gx == 0, 1, 0) - jnp.where(gx == 3, 1, 0)
    inside = jnp.where((wrap >= 0) & (wrap < BLOCKS), 1, 0)
    sent_idx = jnp.stack(blocks(SENT) + [own, jnp.clip(wrap, 0, BLOCKS - 1), inside]).astype(jnp.int32)
    kept_idx = jnp.stack(blocks(KEPT)).astype(jnp.int32)
    far2, one, three, d_own, d_odd = sent_products(sent_idx, fwd, adj, cond, tens)
    kept_idx, far2, one, three = lax.optimization_barrier((kept_idx, far2, one, three))
    near2, far0, near0 = kept_products(kept_idx, fwd, adj, cond)

    two_sum = near2 + lax.ppermute(far2, "source", Y_PERM)
    two_in = lax.ppermute(two_sum, "source", z_perm(2))
    one_in = lax.ppermute(one, "source", z_perm(1))
    three_in = lax.ppermute(three, "source", z_perm(3))
    far_sum = far0 + one_in[0] + three_in[0]
    near_sum = near0 + one_in[1] + three_in[1]
    from_far = lax.ppermute(far_sum, "source", Y_PERM)

    rims = jnp.stack([d_own, d_odd])
    d_core = lax.ppermute(core_tile(rims, y_even), "gy", CORE_PERM)
    d_cross = lax.ppermute(cross_tile(rims, y_even), "gy", CROSS_PERM)
    _, d_core, d_cross = lax.optimization_barrier((far_sum, d_core, d_cross))
    tiles = halo_tile(d_core, d_cross, y_even)
    d_own = jnp.concatenate([d_own, tiles[0]], axis=-2)
    d_odd = jnp.concatenate([d_odd, tiles[1]], axis=-2)
    d_odd_in = lax.ppermute(d_odd, "gx", X_ODD_RING)
    d_even_in = lax.ppermute(d_own, "gx", X_EVEN)
    field = two_in + near_sum + from_far

    core = lax.ppermute(core_tile(field, y_even), "gy", CORE_PERM)
    cross = lax.ppermute(cross_tile(field, y_even), "gy", CROSS_PERM)
    f_own = jnp.concatenate([field, halo_tile(core, cross, y_even)], axis=-2)
    f_odd_in = lax.ppermute(f_own, ("source", "gx"), x_odd_owner())
    f_even_in = lax.ppermute(f_own, "gx", X_EVEN)
    d_lo = jnp.where(x_even, d_odd_in, d_even_in)
    d_hi = jnp.where(x_even, d_even_in, d_odd_in)
    d_lo, d_hi, f_odd_in = lax.optimization_barrier((d_lo, d_hi, f_odd_in))
    f_hi = jnp.where(x_even, f_even_in, f_odd_in)
    f_lo = jnp.where(x_even, f_odd_in, f_even_in)
    f_hi, f_lo = lax.optimization_barrier((f_hi, f_lo))

    done = diffuse(f_lo, f_own, f_hi, d_lo, d_own, d_hi)

    two = lax.ppermute(done, "source", z_perm(2))
    other = lax.ppermute(done, "source", Y_PERM)
    one, three = (lax.ppermute(done, "source", z_perm(k)) for k in (1, 3))
    other_two = lax.ppermute(two, "source", Y_PERM)
    other_one, other_three = (lax.ppermute(other, "source", z_perm(k)) for k in (1, 3))
    out = jnp.zeros((2, BLOCKS, 4, 32, 128), F32)
    for half, k, piece in (
        (h, 2, two),
        (h, 0, done),
        (1 - h, 0, other),
        (h, 1, one),
        (h, 3, three),
        (1 - h, 2, other_two),
        (1 - h, 1, other_one),
        (1 - h, 3, other_three),
    ):
        out = lax.dynamic_update_index_in_dim(out, piece, block_of(half, z ^ k), 1)
    return out


def solution(mesh):
    fields = P("source", None, None, "gx", "gy", None)
    cells = P(None, None, "gx", "gy", None)
    return jax.shard_map(
        shards, mesh=mesh, in_specs=(fields, fields, cells, cells), out_specs=cells, check_vma=False
    )
```

```python
import jax
import jax.numpy as jnp
from jax import lax
from jax.experimental import pallas as pl
from jax.experimental.pallas import tpu as pltpu
from jax.sharding import PartitionSpec as P

PASSES = 4
STEP = 0.13
SCALE = 1.0 / 16.0
NZC = 4
BLOCKS = 2 * NZC
F32 = jnp.float32
SLAB = (2, 4, 32, 128)


def block_of(h, z):
    return jnp.where(h == 0, z, BLOCKS - 1 - z)


def source_of(b):
    return b if b < NZC else 3 * NZC - 1 - b


def z_perm(k):
    return [(s, s ^ k) for s in range(BLOCKS)]


Y_PERM = [(s, (s + NZC) % BLOCKS) for s in range(BLOCKS)]
CORE_PERM = [(i, i ^ 1) for i in range(4)]
CROSS_PERM = [(1, 2), (2, 1)]
X_EVEN = [(i, i ^ 1) for i in range(4)]
X_ODD_RING = [(1, 2), (2, 1), (3, 0), (0, 3)]


def x_odd_owner():
    pairs = []
    for s in range(BLOCKS):
        pairs += [(s * 4 + 1, s * 4 + 2), (s * 4 + 2, s * 4 + 1)]
    for b in range(BLOCKS - 1):
        low, high = source_of(b) * 4 + 3, source_of(b + 1) * 4
        pairs += [(low, high), (high, low)]
    return pairs


SENT = [(0, 2), (0, 1), (1, 1), (0, 3), (1, 3)]
KEPT = [(1, 2), (0, 0), (1, 0)]


def start_products(idx_ref, f_hbm, a_hbm, c_hbm, f_buf, a_buf, c_buf, sems, count):
    copies = []
    for k in range(count):
        b = idx_ref[k]
        group = [
            pltpu.make_async_copy(f_hbm.at[:, :, b], f_buf.at[k], sems.at[0, k]),
            pltpu.make_async_copy(a_hbm.at[:, :, b], a_buf.at[k], sems.at[1, k]),
            pltpu.make_async_copy(c_hbm.at[:, b], c_buf.at[k], sems.at[2, k]),
        ]
        for copy in group:
            copy.start()
        copies.append(group)
    return copies


def block_products(k, copies, f_buf, a_buf, c_buf, out):
    for copy in copies[k]:
        copy.wait()
    for r in range(4):
        hor = ver = None
        for t in range(2):
            prod = [f_buf[k, t, c, r].astype(F32) * a_buf[k, t, c, r].astype(F32) for c in range(6)]
            h1 = (prod[0] + prod[1]) - (prod[3] + prod[4])
            v1 = prod[2] - prod[5]
            hor = h1 if hor is None else hor + h1
            ver = v1 if ver is None else ver + v1
        out[0, r] = hor * (c_buf[k, 0, r] * SCALE)
        out[1, r] = ver * (c_buf[k, 1, r] * SCALE)


def sent_kernel(
    idx_ref, f_hbm, a_hbm, c_hbm, t_hbm, far2, one, three, d_own, d_odd, f_buf, a_buf, c_buf, t_buf, sems, t_sems
):
    n = len(SENT)
    t_copies = [pltpu.make_async_copy(t_hbm.at[:, idx_ref[n + k]], t_buf.at[k], t_sems.at[k]) for k in range(2)]
    for copy in t_copies:
        copy.start()
    copies = start_products(idx_ref, f_hbm, a_hbm, c_hbm, f_buf, a_buf, c_buf, sems, n)
    inside = idx_ref[n + 2] > 0
    for copy in t_copies:
        copy.wait()
    for e in range(6):
        for r in range(4):
            d_own[e, r] = t_buf[0, e, r].astype(F32)
            d_odd[e, r] = jnp.where(inside, t_buf[1, e, r].astype(F32), 0.0)
    for k, out in enumerate((far2, one.at[0], one.at[1], three.at[0], three.at[1])):
        block_products(k, copies, f_buf, a_buf, c_buf, out)


def kept_kernel(idx_ref, f_hbm, a_hbm, c_hbm, near2, far0, near0, f_buf, a_buf, c_buf, sems):
    copies = start_products(idx_ref, f_hbm, a_hbm, c_hbm, f_buf, a_buf, c_buf, sems, len(KEPT))
    for k, out in enumerate((near2, far0, near0)):
        block_products(k, copies, f_buf, a_buf, c_buf, out)


def products_scratch(n):
    return [
        pltpu.VMEM((n, 2, 6, 4, 32, 128), jnp.bfloat16),
        pltpu.VMEM((n, 2, 6, 4, 32, 128), jnp.bfloat16),
        pltpu.VMEM((n, *SLAB), F32),
    ]


def in_hbm(*arrays):
    return [pltpu.with_memory_space_constraint(x, pltpu.HBM) for x in arrays]


def sent_products(idx, fwd, adj, cond, tens):
    hbm = pl.BlockSpec(memory_space=pltpu.HBM)
    pair = jax.ShapeDtypeStruct((2, *SLAB), F32)
    rim = jax.ShapeDtypeStruct((6, 4, 32, 128), F32)
    return pl.pallas_call(
        sent_kernel,
        in_specs=[pl.BlockSpec(memory_space=pltpu.SMEM), hbm, hbm, hbm, hbm],
        out_shape=[jax.ShapeDtypeStruct(SLAB, F32), pair, pair, rim, rim],
        scratch_shapes=products_scratch(len(SENT))
        + [
            pltpu.VMEM((2, 6, 4, 32, 128), jnp.bfloat16),
            pltpu.SemaphoreType.DMA((3, len(SENT))),
            pltpu.SemaphoreType.DMA((2,)),
        ],
        compiler_params=pltpu.CompilerParams(vmem_limit_bytes=32 << 20),
    )(idx, *in_hbm(fwd, adj, cond, tens))


def kept_products(idx, fwd, adj, cond):
    hbm = pl.BlockSpec(memory_space=pltpu.HBM)
    return pl.pallas_call(
        kept_kernel,
        in_specs=[pl.BlockSpec(memory_space=pltpu.SMEM), hbm, hbm, hbm],
        out_shape=[jax.ShapeDtypeStruct(SLAB, F32)] * 3,
        scratch_shapes=products_scratch(len(KEPT)) + [pltpu.SemaphoreType.DMA((3, len(KEPT)))],
        compiler_params=pltpu.CompilerParams(vmem_limit_bytes=32 << 20),
    )(idx, *in_hbm(fwd, adj, cond))


def diffuse_kernel(f_lo, f_own, f_hi, d_lo, d_own, d_hi, out, buf, after, part, flux_z):
    fs, ds = (f_lo, f_own, f_hi), (d_lo, d_own, d_hi)
    lane = lax.broadcasted_iota(jnp.int32, (40, 128), 1)
    first, last = lane == 0, lane == 127

    def tensor(e, r):
        return ds[(r + 4) // 4][e, (r + 4) % 4]

    for p in range(PASSES):
        m = PASSES - 1 - p

        def field(c, r):
            if p == 0:
                return fs[(r + 4) // 4][c, (r + 4) % 4]
            return buf[(p - 1) % 2, c, r + 4]

        for r in range(-m - 1, 4 + m):
            for c in range(2):
                after[c, r + 4] = jnp.where(last, 0.0, pltpu.roll(field(c, r), 127, 1))
        flux_x_before = [None, None]
        here = [field(c, -m - 1) for c in range(2)]
        for r in range(-m - 1, 4 + m):
            d = [tensor(e, r) for e in range(6)]
            for c in range(2):
                f = here[c]
                nxt = field(c, r + 1)
                gx = nxt - f
                gy = pltpu.roll(f, 39, 0) - f
                gz = after[c, r + 4] - f
                fx = d[0] * gx + d[3] * gy + d[4] * gz
                if r >= -m:
                    fy = d[3] * gx + d[1] * gy + d[5] * gz
                    fz = d[4] * gx + d[5] * gy + d[2] * gz
                    part[c, r + 4] = (fx - flux_x_before[c]) + (fy - pltpu.roll(fy, 1, 0)) + fz
                    flux_z[c, r + 4] = fz
                flux_x_before[c] = fx
                here[c] = nxt
        for r in range(-m, 4 + m):
            gain = jnp.where(tensor(0, r) > 0, F32(STEP), F32(0))
            for c in range(2):
                spread = part[c, r + 4] - jnp.where(first, 0.0, pltpu.roll(flux_z[c, r + 4], 1, 1))
                new = field(c, r) + gain * spread
                if p == PASSES - 1:
                    out[c, r] = new[:32]
                else:
                    buf[p % 2, c, r + 4] = new


def diffuse(*args):
    rows = pltpu.VMEM((2, 12, 40, 128), F32)
    return pl.pallas_call(
        diffuse_kernel,
        out_shape=jax.ShapeDtypeStruct(SLAB, F32),
        scratch_shapes=[pltpu.VMEM((2, 2, 12, 40, 128), F32), rows, rows, rows],
        compiler_params=pltpu.CompilerParams(vmem_limit_bytes=32 << 20),
    )(*args)


def core_tile(cells, even):
    return jnp.where(even, cells[..., 28:, :], cells[..., :4, :])


def cross_tile(cells, even):
    return jnp.where(even, cells[..., :4, :], cells[..., 28:, :])


def halo_tile(core, cross, even):
    return jnp.concatenate([jnp.where(even, core, cross), jnp.where(even, cross, core)], axis=-2)


def shards(fwd, adj, cond, tens):
    s, gx, gy = lax.axis_index("source"), lax.axis_index("gx"), lax.axis_index("gy")
    h, z = s // NZC, s % NZC
    own = block_of(h, z)
    x_even, y_even = gx % 2 == 0, gy % 2 == 0

    def blocks(keys):
        return [block_of(jnp.where(half == 0, 1 - h, h), z ^ k) for half, k in keys]

    wrap = own + jnp.where(gx == 0, 1, 0) - jnp.where(gx == 3, 1, 0)
    inside = jnp.where((wrap >= 0) & (wrap < BLOCKS), 1, 0)
    sent_idx = jnp.stack(blocks(SENT) + [own, jnp.clip(wrap, 0, BLOCKS - 1), inside]).astype(jnp.int32)
    kept_idx = jnp.stack(blocks(KEPT)).astype(jnp.int32)
    far2, one, three, d_own, d_odd = sent_products(sent_idx, fwd, adj, cond, tens)
    kept_idx, far2, one, three = lax.optimization_barrier((kept_idx, far2, one, three))
    near2, far0, near0 = kept_products(kept_idx, fwd, adj, cond)

    two_sum = near2 + lax.ppermute(far2, "source", Y_PERM)
    two_in = lax.ppermute(two_sum, "source", z_perm(2))
    one_in = lax.ppermute(one, "source", z_perm(1))
    three_in = lax.ppermute(three, "source", z_perm(3))
    far_sum = far0 + one_in[0] + three_in[0]
    near_sum = near0 + one_in[1] + three_in[1]
    from_far = lax.ppermute(far_sum, "source", Y_PERM)

    rims = jnp.stack([d_own, d_odd])
    d_core = lax.ppermute(core_tile(rims, y_even), "gy", CORE_PERM)
    d_cross = lax.ppermute(cross_tile(rims, y_even), "gy", CROSS_PERM)
    _, d_core, d_cross = lax.optimization_barrier((far_sum, d_core, d_cross))
    tiles = halo_tile(d_core, d_cross, y_even)
    d_own = jnp.concatenate([d_own, tiles[0]], axis=-2)
    d_odd = jnp.concatenate([d_odd, tiles[1]], axis=-2)
    d_odd_in = lax.ppermute(d_odd, "gx", X_ODD_RING)
    d_even_in = lax.ppermute(d_own, "gx", X_EVEN)
    field = two_in + near_sum + from_far

    core = lax.ppermute(core_tile(field, y_even), "gy", CORE_PERM)
    cross = lax.ppermute(cross_tile(field, y_even), "gy", CROSS_PERM)
    cross, core = lax.optimization_barrier((cross, core))
    f_own = jnp.concatenate([field, halo_tile(core, cross, y_even)], axis=-2)
    f_odd_in = lax.ppermute(f_own, ("source", "gx"), x_odd_owner())
    f_even_in = lax.ppermute(f_own, "gx", X_EVEN)
    d_lo = jnp.where(x_even, d_odd_in, d_even_in)
    d_hi = jnp.where(x_even, d_even_in, d_odd_in)
    d_lo, d_hi, f_odd_in = lax.optimization_barrier((d_lo, d_hi, f_odd_in))
    f_hi = jnp.where(x_even, f_even_in, f_odd_in)
    f_lo = jnp.where(x_even, f_odd_in, f_even_in)
    f_hi, f_lo = lax.optimization_barrier((f_hi, f_lo))

    done = diffuse(f_lo, f_own, f_hi, d_lo, d_own, d_hi)

    other = lax.ppermute(done, "source", Y_PERM)
    two = lax.ppermute(done, "source", z_perm(2))
    pair = jnp.stack([done, other])
    one, three = (lax.ppermute(pair, "source", z_perm(k)) for k in (1, 3))
    other_two = lax.ppermute(two, "source", Y_PERM)
    out = jnp.zeros((2, BLOCKS, 4, 32, 128), F32)
    for half, k, piece in (
        (h, 0, done),
        (1 - h, 0, other),
        (h, 2, two),
        (h, 1, one[0]),
        (1 - h, 1, one[1]),
        (h, 3, three[0]),
        (1 - h, 3, three[1]),
        (1 - h, 2, other_two),
    ):
        out = lax.dynamic_update_index_in_dim(out, piece, block_of(half, z ^ k), 1)
    return out


def solution(mesh):
    fields = P("source", None, None, "gx", "gy", None)
    cells = P(None, None, "gx", "gy", None)
    return jax.shard_map(
        shards, mesh=mesh, in_specs=(fields, fields, cells, cells), out_specs=cells, check_vma=False
    )
```

```python
import jax
import jax.numpy as jnp
from jax import lax
from jax.experimental import pallas as pl
from jax.experimental.pallas import tpu as pltpu
from jax.sharding import PartitionSpec as P

PASSES = 4
STEP = 0.13
SCALE = 1.0 / 16.0
NZC = 4
BLOCKS = 2 * NZC
F32 = jnp.float32
SLAB = (2, 4, 32, 128)


def block_of(h, z):
    return jnp.where(h == 0, z, BLOCKS - 1 - z)


def source_of(b):
    return b if b < NZC else 3 * NZC - 1 - b


def z_perm(k):
    return [(s, s ^ k) for s in range(BLOCKS)]


Y_PERM = [(s, (s + NZC) % BLOCKS) for s in range(BLOCKS)]
CORE_PERM = [(i, i ^ 1) for i in range(4)]
CROSS_PERM = [(1, 2), (2, 1)]
X_EVEN = [(i, i ^ 1) for i in range(4)]
X_ODD_RING = [(1, 2), (2, 1), (3, 0), (0, 3)]


def x_odd_owner():
    pairs = []
    for s in range(BLOCKS):
        pairs += [(s * 4 + 1, s * 4 + 2), (s * 4 + 2, s * 4 + 1)]
    for b in range(BLOCKS - 1):
        low, high = source_of(b) * 4 + 3, source_of(b + 1) * 4
        pairs += [(low, high), (high, low)]
    return pairs


SENT = [(0, 2), (0, 1), (1, 1), (0, 3), (1, 3)]
KEPT = [(1, 2), (0, 0), (1, 0)]


def start_products(idx_ref, f_hbm, a_hbm, c_hbm, f_buf, a_buf, c_buf, sems, count):
    copies = []
    for k in range(count):
        b = idx_ref[k]
        group = [
            pltpu.make_async_copy(f_hbm.at[:, :, b], f_buf.at[k], sems.at[0, k]),
            pltpu.make_async_copy(a_hbm.at[:, :, b], a_buf.at[k], sems.at[1, k]),
            pltpu.make_async_copy(c_hbm.at[:, b], c_buf.at[k], sems.at[2, k]),
        ]
        for copy in group:
            copy.start()
        copies.append(group)
    return copies


def block_products(k, copies, f_buf, a_buf, c_buf, out):
    for copy in copies[k]:
        copy.wait()
    for r in range(4):
        hor = ver = None
        for t in range(2):
            prod = [f_buf[k, t, c, r].astype(F32) * a_buf[k, t, c, r].astype(F32) for c in range(6)]
            h1 = (prod[0] + prod[1]) - (prod[3] + prod[4])
            v1 = prod[2] - prod[5]
            hor = h1 if hor is None else hor + h1
            ver = v1 if ver is None else ver + v1
        out[0, r] = hor * (c_buf[k, 0, r] * SCALE)
        out[1, r] = ver * (c_buf[k, 1, r] * SCALE)


def sent_kernel(
    idx_ref, f_hbm, a_hbm, c_hbm, t_hbm, far2, one, three, d_own, d_odd, f_buf, a_buf, c_buf, t_buf, sems, t_sems
):
    n = len(SENT)
    t_copies = [pltpu.make_async_copy(t_hbm.at[:, idx_ref[n + k]], t_buf.at[k], t_sems.at[k]) for k in range(2)]
    for copy in t_copies:
        copy.start()
    copies = start_products(idx_ref, f_hbm, a_hbm, c_hbm, f_buf, a_buf, c_buf, sems, n)
    inside = idx_ref[n + 2] > 0
    for copy in t_copies:
        copy.wait()
    for e in range(6):
        for r in range(4):
            d_own[e, r] = t_buf[0, e, r].astype(F32)
            d_odd[e, r] = jnp.where(inside, t_buf[1, e, r].astype(F32), 0.0)
    for k, out in enumerate((far2, one.at[0], one.at[1], three.at[0], three.at[1])):
        block_products(k, copies, f_buf, a_buf, c_buf, out)


def kept_kernel(idx_ref, f_hbm, a_hbm, c_hbm, near2, far0, near0, f_buf, a_buf, c_buf, sems):
    copies = start_products(idx_ref, f_hbm, a_hbm, c_hbm, f_buf, a_buf, c_buf, sems, len(KEPT))
    for k, out in enumerate((near2, far0, near0)):
        block_products(k, copies, f_buf, a_buf, c_buf, out)


def products_scratch(n):
    return [
        pltpu.VMEM((n, 2, 6, 4, 32, 128), jnp.bfloat16),
        pltpu.VMEM((n, 2, 6, 4, 32, 128), jnp.bfloat16),
        pltpu.VMEM((n, *SLAB), F32),
    ]


def in_hbm(*arrays):
    return [pltpu.with_memory_space_constraint(x, pltpu.HBM) for x in arrays]


def sent_products(idx, fwd, adj, cond, tens):
    hbm = pl.BlockSpec(memory_space=pltpu.HBM)
    pair = jax.ShapeDtypeStruct((2, *SLAB), F32)
    rim = jax.ShapeDtypeStruct((6, 4, 32, 128), F32)
    return pl.pallas_call(
        sent_kernel,
        in_specs=[pl.BlockSpec(memory_space=pltpu.SMEM), hbm, hbm, hbm, hbm],
        out_shape=[jax.ShapeDtypeStruct(SLAB, F32), pair, pair, rim, rim],
        scratch_shapes=products_scratch(len(SENT))
        + [
            pltpu.VMEM((2, 6, 4, 32, 128), jnp.bfloat16),
            pltpu.SemaphoreType.DMA((3, len(SENT))),
            pltpu.SemaphoreType.DMA((2,)),
        ],
        compiler_params=pltpu.CompilerParams(vmem_limit_bytes=32 << 20),
    )(idx, *in_hbm(fwd, adj, cond, tens))


def kept_products(idx, fwd, adj, cond):
    hbm = pl.BlockSpec(memory_space=pltpu.HBM)
    return pl.pallas_call(
        kept_kernel,
        in_specs=[pl.BlockSpec(memory_space=pltpu.SMEM), hbm, hbm, hbm],
        out_shape=[jax.ShapeDtypeStruct(SLAB, F32)] * 3,
        scratch_shapes=products_scratch(len(KEPT)) + [pltpu.SemaphoreType.DMA((3, len(KEPT)))],
        compiler_params=pltpu.CompilerParams(vmem_limit_bytes=32 << 20),
    )(idx, *in_hbm(fwd, adj, cond))


def diffuse_kernel(f_lo, f_own, f_hi, d_lo, d_own, d_hi, out, buf, after, part, flux_z):
    fs, ds = (f_lo, f_own, f_hi), (d_lo, d_own, d_hi)
    lane = lax.broadcasted_iota(jnp.int32, (40, 128), 1)
    first, last = lane == 0, lane == 127

    def tensor(e, r):
        return ds[(r + 4) // 4][e, (r + 4) % 4]

    for p in range(PASSES):
        m = PASSES - 1 - p

        def field(c, r):
            if p == 0:
                return fs[(r + 4) // 4][c, (r + 4) % 4]
            return buf[(p - 1) % 2, c, r + 4]

        for r in range(-m - 1, 4 + m):
            for c in range(2):
                after[c, r + 4] = jnp.where(last, 0.0, pltpu.roll(field(c, r), 127, 1))
        flux_x_before = [None, None]
        here = [field(c, -m - 1) for c in range(2)]
        for r in range(-m - 1, 4 + m):
            d = [tensor(e, r) for e in range(6)]
            for c in range(2):
                f = here[c]
                nxt = field(c, r + 1)
                gx = nxt - f
                gy = pltpu.roll(f, 39, 0) - f
                gz = after[c, r + 4] - f
                fx = d[0] * gx + d[3] * gy + d[4] * gz
                if r >= -m:
                    fy = d[3] * gx + d[1] * gy + d[5] * gz
                    fz = d[4] * gx + d[5] * gy + d[2] * gz
                    part[c, r + 4] = (fx - flux_x_before[c]) + (fy - pltpu.roll(fy, 1, 0)) + fz
                    flux_z[c, r + 4] = fz
                flux_x_before[c] = fx
                here[c] = nxt
        for r in range(-m, 4 + m):
            gain = jnp.where(tensor(0, r) > 0, F32(STEP), F32(0))
            for c in range(2):
                spread = part[c, r + 4] - jnp.where(first, 0.0, pltpu.roll(flux_z[c, r + 4], 1, 1))
                new = field(c, r) + gain * spread
                if p == PASSES - 1:
                    out[c, r] = new[:32]
                else:
                    buf[p % 2, c, r + 4] = new


def diffuse(*args):
    rows = pltpu.VMEM((2, 12, 40, 128), F32)
    return pl.pallas_call(
        diffuse_kernel,
        out_shape=jax.ShapeDtypeStruct(SLAB, F32),
        scratch_shapes=[pltpu.VMEM((2, 2, 12, 40, 128), F32), rows, rows, rows],
        compiler_params=pltpu.CompilerParams(vmem_limit_bytes=32 << 20),
    )(*args)


def core_tile(cells, even):
    return jnp.where(even, cells[..., 28:, :], cells[..., :4, :])


def cross_tile(cells, even):
    return jnp.where(even, cells[..., :4, :], cells[..., 28:, :])


def halo_tile(core, cross, even):
    return jnp.concatenate([jnp.where(even, core, cross), jnp.where(even, cross, core)], axis=-2)


def shards(fwd, adj, cond, tens):
    s, gx, gy = lax.axis_index("source"), lax.axis_index("gx"), lax.axis_index("gy")
    h, z = s // NZC, s % NZC
    own = block_of(h, z)
    x_even, y_even = gx % 2 == 0, gy % 2 == 0

    def blocks(keys):
        return [block_of(jnp.where(half == 0, 1 - h, h), z ^ k) for half, k in keys]

    wrap = own + jnp.where(gx == 0, 1, 0) - jnp.where(gx == 3, 1, 0)
    inside = jnp.where((wrap >= 0) & (wrap < BLOCKS), 1, 0)
    sent_idx = jnp.stack(blocks(SENT) + [own, jnp.clip(wrap, 0, BLOCKS - 1), inside]).astype(jnp.int32)
    kept_idx = jnp.stack(blocks(KEPT)).astype(jnp.int32)
    far2, one, three, d_own, d_odd = sent_products(sent_idx, fwd, adj, cond, tens)
    kept_idx, far2, one, three = lax.optimization_barrier((kept_idx, far2, one, three))
    near2, far0, near0 = kept_products(kept_idx, fwd, adj, cond)

    two_sum = near2 + lax.ppermute(far2, "source", Y_PERM)
    one_in = lax.ppermute(one, "source", z_perm(1))
    three_in = lax.ppermute(three, "source", z_perm(3))
    far_sum = far0 + one_in[0] + three_in[0]
    near_sum = near0 + one_in[1] + three_in[1]
    two_sum, far_sum = lax.optimization_barrier((two_sum, far_sum))
    two_in = lax.ppermute(two_sum, "source", z_perm(2))
    from_far = lax.ppermute(far_sum, "source", Y_PERM)

    rims = jnp.stack([d_own, d_odd])
    d_core = lax.ppermute(core_tile(rims, y_even), "gy", CORE_PERM)
    d_cross = lax.ppermute(cross_tile(rims, y_even), "gy", CROSS_PERM)
    _, d_core, d_cross = lax.optimization_barrier((far_sum, d_core, d_cross))
    tiles = halo_tile(d_core, d_cross, y_even)
    d_own = jnp.concatenate([d_own, tiles[0]], axis=-2)
    d_odd = jnp.concatenate([d_odd, tiles[1]], axis=-2)
    d_odd_in = lax.ppermute(d_odd, "gx", X_ODD_RING)
    d_even_in = lax.ppermute(d_own, "gx", X_EVEN)
    field = near_sum + from_far + two_in

    core = lax.ppermute(core_tile(field, y_even), "gy", CORE_PERM)
    cross = lax.ppermute(cross_tile(field, y_even), "gy", CROSS_PERM)
    f_own = jnp.concatenate([field, halo_tile(core, cross, y_even)], axis=-2)
    f_odd_in = lax.ppermute(f_own, ("source", "gx"), x_odd_owner())
    f_even_in = lax.ppermute(f_own, "gx", X_EVEN)
    d_lo = jnp.where(x_even, d_odd_in, d_even_in)
    d_hi = jnp.where(x_even, d_even_in, d_odd_in)
    d_lo, d_hi, f_odd_in = lax.optimization_barrier((d_lo, d_hi, f_odd_in))
    f_hi = jnp.where(x_even, f_even_in, f_odd_in)
    f_lo = jnp.where(x_even, f_odd_in, f_even_in)
    f_hi, f_lo = lax.optimization_barrier((f_hi, f_lo))

    done = diffuse(f_lo, f_own, f_hi, d_lo, d_own, d_hi)

    two = lax.ppermute(done, "source", z_perm(2))
    other = lax.ppermute(done, "source", Y_PERM)
    one, three = (lax.ppermute(done, "source", z_perm(k)) for k in (1, 3))
    other_two = lax.ppermute(two, "source", Y_PERM)
    other_one, other_three = (lax.ppermute(other, "source", z_perm(k)) for k in (1, 3))
    out = jnp.zeros((2, BLOCKS, 4, 32, 128), F32)
    for half, k, piece in (
        (h, 2, two),
        (h, 0, done),
        (1 - h, 0, other),
        (h, 1, one),
        (h, 3, three),
        (1 - h, 2, other_two),
        (1 - h, 1, other_one),
        (1 - h, 3, other_three),
    ):
        out = lax.dynamic_update_index_in_dim(out, piece, block_of(half, z ^ k), 1)
    return out


def solution(mesh):
    fields = P("source", None, None, "gx", "gy", None)
    cells = P(None, None, "gx", "gy", None)
    return jax.shard_map(
        shards, mesh=mesh, in_specs=(fields, fields, cells, cells), out_specs=cells, check_vma=False
    )
```

```python
import jax
import jax.numpy as jnp
from jax import lax
from jax.experimental import pallas as pl
from jax.experimental.pallas import tpu as pltpu
from jax.sharding import PartitionSpec as P

PASSES = 4
STEP = 0.13
SCALE = 1.0 / 16.0
NZC = 4
BLOCKS = 2 * NZC
F32 = jnp.float32
SLAB = (2, 4, 32, 128)


def block_of(h, z):
    return jnp.where(h == 0, z, BLOCKS - 1 - z)


def source_of(b):
    return b if b < NZC else 3 * NZC - 1 - b


def z_perm(k):
    return [(s, s ^ k) for s in range(BLOCKS)]


Y_PERM = [(s, (s + NZC) % BLOCKS) for s in range(BLOCKS)]
CORE_PERM = [(i, i ^ 1) for i in range(4)]
CROSS_PERM = [(1, 2), (2, 1)]
CROSS_FAR = [(s * 4 + a, ((s + NZC) % BLOCKS) * 4 + 3 - a) for s in range(BLOCKS) for a in (1, 2)]
X_EVEN = [(i, i ^ 1) for i in range(4)]
X_ODD_RING = [(1, 2), (2, 1), (3, 0), (0, 3)]


def x_odd_owner():
    pairs = []
    for s in range(BLOCKS):
        pairs += [(s * 4 + 1, s * 4 + 2), (s * 4 + 2, s * 4 + 1)]
    for b in range(BLOCKS - 1):
        low, high = source_of(b) * 4 + 3, source_of(b + 1) * 4
        pairs += [(low, high), (high, low)]
    return pairs


SENT = [(0, 2), (0, 1), (1, 1), (0, 3), (1, 3)]
KEPT = [(1, 2), (0, 0), (1, 0)]


def start_products(idx_ref, f_hbm, a_hbm, c_hbm, f_buf, a_buf, c_buf, sems, count):
    copies = []
    for k in range(count):
        b = idx_ref[k]
        group = [
            pltpu.make_async_copy(f_hbm.at[:, :, b], f_buf.at[k], sems.at[0, k]),
            pltpu.make_async_copy(a_hbm.at[:, :, b], a_buf.at[k], sems.at[1, k]),
            pltpu.make_async_copy(c_hbm.at[:, b], c_buf.at[k], sems.at[2, k]),
        ]
        for copy in group:
            copy.start()
        copies.append(group)
    return copies


def block_products(k, copies, f_buf, a_buf, c_buf, out):
    for copy in copies[k]:
        copy.wait()
    for r in range(4):
        hor = ver = None
        for t in range(2):
            prod = [f_buf[k, t, c, r].astype(F32) * a_buf[k, t, c, r].astype(F32) for c in range(6)]
            h1 = (prod[0] + prod[1]) - (prod[3] + prod[4])
            v1 = prod[2] - prod[5]
            hor = h1 if hor is None else hor + h1
            ver = v1 if ver is None else ver + v1
        out[0, r] = hor * (c_buf[k, 0, r] * SCALE)
        out[1, r] = ver * (c_buf[k, 1, r] * SCALE)


def sent_kernel(
    idx_ref, f_hbm, a_hbm, c_hbm, t_hbm, far2, one, three, d_own, d_odd, f_buf, a_buf, c_buf, t_buf, sems, t_sems
):
    n = len(SENT)
    t_copies = [pltpu.make_async_copy(t_hbm.at[:, idx_ref[n + k]], t_buf.at[k], t_sems.at[k]) for k in range(2)]
    for copy in t_copies:
        copy.start()
    copies = start_products(idx_ref, f_hbm, a_hbm, c_hbm, f_buf, a_buf, c_buf, sems, n)
    inside = idx_ref[n + 2] > 0
    for copy in t_copies:
        copy.wait()
    for e in range(6):
        for r in range(4):
            d_own[e, r] = t_buf[0, e, r].astype(F32)
            d_odd[e, r] = jnp.where(inside, t_buf[1, e, r].astype(F32), 0.0)
    for k, out in enumerate((far2, one.at[0], one.at[1], three.at[0], three.at[1])):
        block_products(k, copies, f_buf, a_buf, c_buf, out)


def kept_kernel(idx_ref, f_hbm, a_hbm, c_hbm, near2, far0, near0, f_buf, a_buf, c_buf, sems):
    copies = start_products(idx_ref, f_hbm, a_hbm, c_hbm, f_buf, a_buf, c_buf, sems, len(KEPT))
    for k, out in enumerate((near2, far0, near0)):
        block_products(k, copies, f_buf, a_buf, c_buf, out)


def products_scratch(n):
    return [
        pltpu.VMEM((n, 2, 6, 4, 32, 128), jnp.bfloat16),
        pltpu.VMEM((n, 2, 6, 4, 32, 128), jnp.bfloat16),
        pltpu.VMEM((n, *SLAB), F32),
    ]


def in_hbm(*arrays):
    return [pltpu.with_memory_space_constraint(x, pltpu.HBM) for x in arrays]


def sent_products(idx, fwd, adj, cond, tens):
    hbm = pl.BlockSpec(memory_space=pltpu.HBM)
    pair = jax.ShapeDtypeStruct((2, *SLAB), F32)
    rim = jax.ShapeDtypeStruct((6, 4, 32, 128), F32)
    return pl.pallas_call(
        sent_kernel,
        in_specs=[pl.BlockSpec(memory_space=pltpu.SMEM), hbm, hbm, hbm, hbm],
        out_shape=[jax.ShapeDtypeStruct(SLAB, F32), pair, pair, rim, rim],
        scratch_shapes=products_scratch(len(SENT))
        + [
            pltpu.VMEM((2, 6, 4, 32, 128), jnp.bfloat16),
            pltpu.SemaphoreType.DMA((3, len(SENT))),
            pltpu.SemaphoreType.DMA((2,)),
        ],
        compiler_params=pltpu.CompilerParams(vmem_limit_bytes=32 << 20),
    )(idx, *in_hbm(fwd, adj, cond, tens))


def kept_products(idx, fwd, adj, cond):
    hbm = pl.BlockSpec(memory_space=pltpu.HBM)
    return pl.pallas_call(
        kept_kernel,
        in_specs=[pl.BlockSpec(memory_space=pltpu.SMEM), hbm, hbm, hbm],
        out_shape=[jax.ShapeDtypeStruct(SLAB, F32)] * 3,
        scratch_shapes=products_scratch(len(KEPT)) + [pltpu.SemaphoreType.DMA((3, len(KEPT)))],
        compiler_params=pltpu.CompilerParams(vmem_limit_bytes=32 << 20),
    )(idx, *in_hbm(fwd, adj, cond))


def diffuse_kernel(f_lo, f_own, f_hi, d_lo, d_own, d_hi, out, buf, after, part, flux_z):
    fs, ds = (f_lo, f_own, f_hi), (d_lo, d_own, d_hi)
    lane = lax.broadcasted_iota(jnp.int32, (40, 128), 1)
    first, last = lane == 0, lane == 127

    def tensor(e, r):
        return ds[(r + 4) // 4][e, (r + 4) % 4]

    for p in range(PASSES):
        m = PASSES - 1 - p

        def field(c, r):
            if p == 0:
                return fs[(r + 4) // 4][c, (r + 4) % 4]
            return buf[(p - 1) % 2, c, r + 4]

        for r in range(-m - 1, 4 + m):
            for c in range(2):
                after[c, r + 4] = jnp.where(last, 0.0, pltpu.roll(field(c, r), 127, 1))
        flux_x_before = [None, None]
        here = [field(c, -m - 1) for c in range(2)]
        for r in range(-m - 1, 4 + m):
            d = [tensor(e, r) for e in range(6)]
            for c in range(2):
                f = here[c]
                nxt = field(c, r + 1)
                gx = nxt - f
                gy = pltpu.roll(f, 39, 0) - f
                gz = after[c, r + 4] - f
                fx = d[0] * gx + d[3] * gy + d[4] * gz
                if r >= -m:
                    fy = d[3] * gx + d[1] * gy + d[5] * gz
                    fz = d[4] * gx + d[5] * gy + d[2] * gz
                    part[c, r + 4] = (fx - flux_x_before[c]) + (fy - pltpu.roll(fy, 1, 0)) + fz
                    flux_z[c, r + 4] = fz
                flux_x_before[c] = fx
                here[c] = nxt
        for r in range(-m, 4 + m):
            gain = jnp.where(tensor(0, r) > 0, F32(STEP), F32(0))
            for c in range(2):
                spread = part[c, r + 4] - jnp.where(first, 0.0, pltpu.roll(flux_z[c, r + 4], 1, 1))
                new = field(c, r) + gain * spread
                if p == PASSES - 1:
                    out[c, r] = new[:32]
                else:
                    buf[p % 2, c, r + 4] = new


def diffuse(*args):
    rows = pltpu.VMEM((2, 12, 40, 128), F32)
    return pl.pallas_call(
        diffuse_kernel,
        out_shape=jax.ShapeDtypeStruct(SLAB, F32),
        scratch_shapes=[pltpu.VMEM((2, 2, 12, 40, 128), F32), rows, rows, rows],
        compiler_params=pltpu.CompilerParams(vmem_limit_bytes=32 << 20),
    )(*args)


def core_tile(cells, even):
    return jnp.where(even, cells[..., 28:, :], cells[..., :4, :])


def cross_tile(cells, even):
    return jnp.where(even, cells[..., :4, :], cells[..., 28:, :])


def halo_tile(core, cross, even):
    return jnp.concatenate([jnp.where(even, core, cross), jnp.where(even, cross, core)], axis=-2)


def shards(fwd, adj, cond, tens):
    s, gx, gy = lax.axis_index("source"), lax.axis_index("gx"), lax.axis_index("gy")
    h, z = s // NZC, s % NZC
    own = block_of(h, z)
    x_even, y_even = gx % 2 == 0, gy % 2 == 0

    def blocks(keys):
        return [block_of(jnp.where(half == 0, 1 - h, h), z ^ k) for half, k in keys]

    wrap = own + jnp.where(gx == 0, 1, 0) - jnp.where(gx == 3, 1, 0)
    inside = jnp.where((wrap >= 0) & (wrap < BLOCKS), 1, 0)
    sent_idx = jnp.stack(blocks(SENT) + [own, jnp.clip(wrap, 0, BLOCKS - 1), inside]).astype(jnp.int32)
    kept_idx = jnp.stack(blocks(KEPT)).astype(jnp.int32)
    far2, one, three, d_own, d_odd = sent_products(sent_idx, fwd, adj, cond, tens)
    kept_idx, far2, one, three = lax.optimization_barrier((kept_idx, far2, one, three))
    near2, far0, near0 = kept_products(kept_idx, fwd, adj, cond)

    two_sum = near2 + lax.ppermute(far2, "source", Y_PERM)
    two_in = lax.ppermute(two_sum, "source", z_perm(2))
    one_in = lax.ppermute(one, "source", z_perm(1))
    three_in = lax.ppermute(three, "source", z_perm(3))
    far_sum = far0 + one_in[0] + three_in[0]
    near_sum = near0 + one_in[1] + three_in[1]
    from_far = lax.ppermute(far_sum, "source", Y_PERM)
    cross_far = lax.ppermute(cross_tile(far_sum, y_even), ("source", "gy"), CROSS_FAR)

    rims = jnp.stack([d_own, d_odd])
    d_core = lax.ppermute(core_tile(rims, y_even), "gy", CORE_PERM)
    d_cross = lax.ppermute(cross_tile(rims, y_even), "gy", CROSS_PERM)
    _, d_core, d_cross = lax.optimization_barrier((far_sum, d_core, d_cross))
    tiles = halo_tile(d_core, d_cross, y_even)
    d_own = jnp.concatenate([d_own, tiles[0]], axis=-2)
    d_odd = jnp.concatenate([d_odd, tiles[1]], axis=-2)
    d_odd_in = lax.ppermute(d_odd, "gx", X_ODD_RING)
    d_even_in = lax.ppermute(d_own, "gx", X_EVEN)
    near_sum = two_in + near_sum
    cross_near = lax.ppermute(cross_tile(near_sum, y_even), "gy", CROSS_PERM)
    field = near_sum + from_far

    core = lax.ppermute(core_tile(field, y_even), "gy", CORE_PERM)
    f_own = jnp.concatenate([field, halo_tile(core, cross_far + cross_near, y_even)], axis=-2)
    f_odd_in = lax.ppermute(f_own, ("source", "gx"), x_odd_owner())
    f_even_in = lax.ppermute(f_own, "gx", X_EVEN)
    d_lo = jnp.where(x_even, d_odd_in, d_even_in)
    d_hi = jnp.where(x_even, d_even_in, d_odd_in)
    d_lo, d_hi, f_odd_in = lax.optimization_barrier((d_lo, d_hi, f_odd_in))
    f_hi = jnp.where(x_even, f_even_in, f_odd_in)
    f_lo = jnp.where(x_even, f_odd_in, f_even_in)
    f_hi, f_lo = lax.optimization_barrier((f_hi, f_lo))

    done = diffuse(f_lo, f_own, f_hi, d_lo, d_own, d_hi)

    two = lax.ppermute(done, "source", z_perm(2))
    other = lax.ppermute(done, "source", Y_PERM)
    one, three = (lax.ppermute(done, "source", z_perm(k)) for k in (1, 3))
    other_two = lax.ppermute(two, "source", Y_PERM)
    other_one, other_three = (lax.ppermute(other, "source", z_perm(k)) for k in (1, 3))
    out = jnp.zeros((2, BLOCKS, 4, 32, 128), F32)
    for half, k, piece in (
        (h, 2, two),
        (h, 0, done),
        (1 - h, 0, other),
        (h, 1, one),
        (h, 3, three),
        (1 - h, 2, other_two),
        (1 - h, 1, other_one),
        (1 - h, 3, other_three),
    ):
        out = lax.dynamic_update_index_in_dim(out, piece, block_of(half, z ^ k), 1)
    return out


def solution(mesh):
    fields = P("source", None, None, "gx", "gy", None)
    cells = P(None, None, "gx", "gy", None)
    return jax.shard_map(
        shards, mesh=mesh, in_specs=(fields, fields, cells, cells), out_specs=cells, check_vma=False
    )
```

```python
import jax
import jax.numpy as jnp
from jax import lax
from jax.experimental import pallas as pl
from jax.experimental.pallas import tpu as pltpu
from jax.sharding import PartitionSpec as P

PASSES = 4
STEP = 0.13
SCALE = 1.0 / 16.0
NZC = 4
BLOCKS = 2 * NZC
F32 = jnp.float32
SLAB = (2, 4, 32, 128)


def block_of(h, z):
    return jnp.where(h == 0, z, BLOCKS - 1 - z)


def source_of(b):
    return b if b < NZC else 3 * NZC - 1 - b


def z_perm(k):
    return [(s, s ^ k) for s in range(BLOCKS)]


Y_PERM = [(s, (s + NZC) % BLOCKS) for s in range(BLOCKS)]
CORE_PERM = [(i, i ^ 1) for i in range(4)]
CROSS_PERM = [(1, 2), (2, 1)]
X_EVEN = [(i, i ^ 1) for i in range(4)]
X_ODD_RING = [(1, 2), (2, 1), (3, 0), (0, 3)]


def x_odd_owner():
    pairs = []
    for s in range(BLOCKS):
        pairs += [(s * 4 + 1, s * 4 + 2), (s * 4 + 2, s * 4 + 1)]
    for b in range(BLOCKS - 1):
        low, high = source_of(b) * 4 + 3, source_of(b + 1) * 4
        pairs += [(low, high), (high, low)]
    return pairs


SENT = [(0, 2), (0, 1), (1, 1), (0, 3), (1, 3)]
KEPT = [(1, 2), (0, 0), (1, 0)]


def start_products(idx_ref, f_hbm, a_hbm, c_hbm, f_buf, a_buf, c_buf, sems, count):
    copies = []
    for k in range(count):
        b = idx_ref[k]
        group = [
            pltpu.make_async_copy(f_hbm.at[:, :, b], f_buf.at[k], sems.at[0, k]),
            pltpu.make_async_copy(a_hbm.at[:, :, b], a_buf.at[k], sems.at[1, k]),
            pltpu.make_async_copy(c_hbm.at[:, b], c_buf.at[k], sems.at[2, k]),
        ]
        for copy in group:
            copy.start()
        copies.append(group)
    return copies


def block_products(k, copies, f_buf, a_buf, c_buf, out):
    for copy in copies[k]:
        copy.wait()
    for r in range(4):
        hor = ver = None
        for t in range(2):
            prod = [f_buf[k, t, c, r].astype(F32) * a_buf[k, t, c, r].astype(F32) for c in range(6)]
            h1 = (prod[0] + prod[1]) - (prod[3] + prod[4])
            v1 = prod[2] - prod[5]
            hor = h1 if hor is None else hor + h1
            ver = v1 if ver is None else ver + v1
        out[0, r] = hor * (c_buf[k, 0, r] * SCALE)
        out[1, r] = ver * (c_buf[k, 1, r] * SCALE)


def sent_kernel(idx_ref, f_hbm, a_hbm, c_hbm, far2, one, three, f_buf, a_buf, c_buf, sems):
    copies = start_products(idx_ref, f_hbm, a_hbm, c_hbm, f_buf, a_buf, c_buf, sems, len(SENT))
    for k, out in enumerate((far2, one.at[0], one.at[1], three.at[0], three.at[1])):
        block_products(k, copies, f_buf, a_buf, c_buf, out)


def kept_kernel(
    idx_ref, f_hbm, a_hbm, c_hbm, t_hbm, near2, far0, near0, d_own, d_odd, f_buf, a_buf, c_buf, t_buf, sems, t_sems
):
    n = len(KEPT)
    t_copies = [pltpu.make_async_copy(t_hbm.at[:, idx_ref[n + k]], t_buf.at[k], t_sems.at[k]) for k in range(2)]
    for copy in t_copies:
        copy.start()
    copies = start_products(idx_ref, f_hbm, a_hbm, c_hbm, f_buf, a_buf, c_buf, sems, n)
    inside = idx_ref[n + 2] > 0
    for copy in t_copies:
        copy.wait()
    for e in range(6):
        for r in range(4):
            d_own[e, r] = t_buf[0, e, r].astype(F32)
            d_odd[e, r] = jnp.where(inside, t_buf[1, e, r].astype(F32), 0.0)
    for k, out in enumerate((near2, far0, near0)):
        block_products(k, copies, f_buf, a_buf, c_buf, out)


def products_scratch(n):
    return [
        pltpu.VMEM((n, 2, 6, 4, 32, 128), jnp.bfloat16),
        pltpu.VMEM((n, 2, 6, 4, 32, 128), jnp.bfloat16),
        pltpu.VMEM((n, *SLAB), F32),
    ]


def in_hbm(*arrays):
    return [pltpu.with_memory_space_constraint(x, pltpu.HBM) for x in arrays]


def sent_products(idx, fwd, adj, cond):
    hbm = pl.BlockSpec(memory_space=pltpu.HBM)
    pair = jax.ShapeDtypeStruct((2, *SLAB), F32)
    return pl.pallas_call(
        sent_kernel,
        in_specs=[pl.BlockSpec(memory_space=pltpu.SMEM), hbm, hbm, hbm],
        out_shape=[jax.ShapeDtypeStruct(SLAB, F32), pair, pair],
        scratch_shapes=products_scratch(len(SENT)) + [pltpu.SemaphoreType.DMA((3, len(SENT)))],
        compiler_params=pltpu.CompilerParams(vmem_limit_bytes=32 << 20),
    )(idx, *in_hbm(fwd, adj, cond))


def kept_products(idx, fwd, adj, cond, tens):
    hbm = pl.BlockSpec(memory_space=pltpu.HBM)
    slab = jax.ShapeDtypeStruct(SLAB, F32)
    rim = jax.ShapeDtypeStruct((6, 4, 32, 128), F32)
    return pl.pallas_call(
        kept_kernel,
        in_specs=[pl.BlockSpec(memory_space=pltpu.SMEM), hbm, hbm, hbm, hbm],
        out_shape=[slab, slab, slab, rim, rim],
        scratch_shapes=products_scratch(len(KEPT))
        + [
            pltpu.VMEM((2, 6, 4, 32, 128), jnp.bfloat16),
            pltpu.SemaphoreType.DMA((3, len(KEPT))),
            pltpu.SemaphoreType.DMA((2,)),
        ],
        compiler_params=pltpu.CompilerParams(vmem_limit_bytes=32 << 20),
    )(idx, *in_hbm(fwd, adj, cond, tens))


def diffuse_kernel(f_lo, f_own, f_hi, d_lo, d_own, d_hi, out, buf, after, part, flux_z):
    fs, ds = (f_lo, f_own, f_hi), (d_lo, d_own, d_hi)
    lane = lax.broadcasted_iota(jnp.int32, (40, 128), 1)
    first, last = lane == 0, lane == 127

    def tensor(e, r):
        return ds[(r + 4) // 4][e, (r + 4) % 4]

    for p in range(PASSES):
        m = PASSES - 1 - p

        def field(c, r):
            if p == 0:
                return fs[(r + 4) // 4][c, (r + 4) % 4]
            return buf[(p - 1) % 2, c, r + 4]

        for r in range(-m - 1, 4 + m):
            for c in range(2):
                after[c, r + 4] = jnp.where(last, 0.0, pltpu.roll(field(c, r), 127, 1))
        flux_x_before = [None, None]
        here = [field(c, -m - 1) for c in range(2)]
        for r in range(-m - 1, 4 + m):
            d = [tensor(e, r) for e in range(6)]
            for c in range(2):
                f = here[c]
                nxt = field(c, r + 1)
                gx = nxt - f
                gy = pltpu.roll(f, 39, 0) - f
                gz = after[c, r + 4] - f
                fx = d[0] * gx + d[3] * gy + d[4] * gz
                if r >= -m:
                    fy = d[3] * gx + d[1] * gy + d[5] * gz
                    fz = d[4] * gx + d[5] * gy + d[2] * gz
                    part[c, r + 4] = (fx - flux_x_before[c]) + (fy - pltpu.roll(fy, 1, 0)) + fz
                    flux_z[c, r + 4] = fz
                flux_x_before[c] = fx
                here[c] = nxt
        for r in range(-m, 4 + m):
            gain = jnp.where(tensor(0, r) > 0, F32(STEP), F32(0))
            for c in range(2):
                spread = part[c, r + 4] - jnp.where(first, 0.0, pltpu.roll(flux_z[c, r + 4], 1, 1))
                new = field(c, r) + gain * spread
                if p == PASSES - 1:
                    out[c, r] = new[:32]
                else:
                    buf[p % 2, c, r + 4] = new


def diffuse(*args):
    rows = pltpu.VMEM((2, 12, 40, 128), F32)
    return pl.pallas_call(
        diffuse_kernel,
        out_shape=jax.ShapeDtypeStruct(SLAB, F32),
        scratch_shapes=[pltpu.VMEM((2, 2, 12, 40, 128), F32), rows, rows, rows],
        compiler_params=pltpu.CompilerParams(vmem_limit_bytes=32 << 20),
    )(*args)


def core_tile(cells, even):
    return jnp.where(even, cells[..., 28:, :], cells[..., :4, :])


def cross_tile(cells, even):
    return jnp.where(even, cells[..., :4, :], cells[..., 28:, :])


def halo_tile(core, cross, even):
    return jnp.concatenate([jnp.where(even, core, cross), jnp.where(even, cross, core)], axis=-2)


def shards(fwd, adj, cond, tens):
    s, gx, gy = lax.axis_index("source"), lax.axis_index("gx"), lax.axis_index("gy")
    h, z = s // NZC, s % NZC
    own = block_of(h, z)
    x_even, y_even = gx % 2 == 0, gy % 2 == 0

    def blocks(keys):
        return [block_of(jnp.where(half == 0, 1 - h, h), z ^ k) for half, k in keys]

    wrap = own + jnp.where(gx == 0, 1, 0) - jnp.where(gx == 3, 1, 0)
    inside = jnp.where((wrap >= 0) & (wrap < BLOCKS), 1, 0)
    sent_idx = jnp.stack(blocks(SENT)).astype(jnp.int32)
    kept_idx = jnp.stack(blocks(KEPT) + [own, jnp.clip(wrap, 0, BLOCKS - 1), inside]).astype(jnp.int32)
    far2, one, three = sent_products(sent_idx, fwd, adj, cond)
    kept_idx, far2, one, three = lax.optimization_barrier((kept_idx, far2, one, three))
    near2, far0, near0, d_own, d_odd = kept_products(kept_idx, fwd, adj, cond, tens)

    two_sum = near2 + lax.ppermute(far2, "source", Y_PERM)
    two_in = lax.ppermute(two_sum, "source", z_perm(2))
    one_in = lax.ppermute(one, "source", z_perm(1))
    three_in = lax.ppermute(three, "source", z_perm(3))
    far_sum = far0 + one_in[0] + three_in[0]
    near_sum = near0 + one_in[1] + three_in[1]
    from_far = lax.ppermute(far_sum, "source", Y_PERM)

    rims = jnp.stack([d_own, d_odd])
    d_core = lax.ppermute(core_tile(rims, y_even), "gy", CORE_PERM)
    d_cross = lax.ppermute(cross_tile(rims, y_even), "gy", CROSS_PERM)
    _, d_core, d_cross = lax.optimization_barrier((far_sum, d_core, d_cross))
    tiles = halo_tile(d_core, d_cross, y_even)
    d_own = jnp.concatenate([d_own, tiles[0]], axis=-2)
    d_odd = jnp.concatenate([d_odd, tiles[1]], axis=-2)
    d_odd_in = lax.ppermute(d_odd, "gx", X_ODD_RING)
    d_even_in = lax.ppermute(d_own, "gx", X_EVEN)
    field = near_sum + from_far
    field, two_in = lax.optimization_barrier((field, two_in))
    field = field + two_in

    core = lax.ppermute(core_tile(field, y_even), "gy", CORE_PERM)
    cross = lax.ppermute(cross_tile(field, y_even), "gy", CROSS_PERM)
    f_own = jnp.concatenate([field, halo_tile(core, cross, y_even)], axis=-2)
    f_odd_in = lax.ppermute(f_own, ("source", "gx"), x_odd_owner())
    f_even_in = lax.ppermute(f_own, "gx", X_EVEN)
    d_lo = jnp.where(x_even, d_odd_in, d_even_in)
    d_hi = jnp.where(x_even, d_even_in, d_odd_in)
    d_lo, d_hi, f_odd_in = lax.optimization_barrier((d_lo, d_hi, f_odd_in))
    f_hi = jnp.where(x_even, f_even_in, f_odd_in)
    f_lo = jnp.where(x_even, f_odd_in, f_even_in)
    f_hi, f_lo = lax.optimization_barrier((f_hi, f_lo))

    done = diffuse(f_lo, f_own, f_hi, d_lo, d_own, d_hi)

    two = lax.ppermute(done, "source", z_perm(2))
    other = lax.ppermute(done, "source", Y_PERM)
    one, three = (lax.ppermute(done, "source", z_perm(k)) for k in (1, 3))
    other_two = lax.ppermute(two, "source", Y_PERM)
    other_one, other_three = (lax.ppermute(other, "source", z_perm(k)) for k in (1, 3))
    out = jnp.zeros((2, BLOCKS, 4, 32, 128), F32)
    for half, k, piece in (
        (h, 2, two),
        (h, 0, done),
        (1 - h, 0, other),
        (h, 1, one),
        (h, 3, three),
        (1 - h, 2, other_two),
        (1 - h, 1, other_one),
        (1 - h, 3, other_three),
    ):
        out = lax.dynamic_update_index_in_dim(out, piece, block_of(half, z ^ k), 1)
    return out


def solution(mesh):
    fields = P("source", None, None, "gx", "gy", None)
    cells = P(None, None, "gx", "gy", None)
    return jax.shard_map(
        shards, mesh=mesh, in_specs=(fields, fields, cells, cells), out_specs=cells, check_vma=False
    )
```

```python
import jax
import jax.numpy as jnp
from jax import lax
from jax.experimental import pallas as pl
from jax.experimental.pallas import tpu as pltpu
from jax.sharding import PartitionSpec as P

PASSES = 4
STEP = 0.13
SCALE = 1.0 / 16.0
NZC = 4
BLOCKS = 2 * NZC
F32 = jnp.float32
SLAB = (2, 4, 32, 128)


def block_of(h, z):
    return jnp.where(h == 0, z, BLOCKS - 1 - z)


def source_of(b):
    return b if b < NZC else 3 * NZC - 1 - b


def z_perm(k):
    return [(s, s ^ k) for s in range(BLOCKS)]


Y_PERM = [(s, (s + NZC) % BLOCKS) for s in range(BLOCKS)]
CORE_PERM = [(i, i ^ 1) for i in range(4)]
CROSS_PERM = [(1, 2), (2, 1)]
X_EVEN = [(i, i ^ 1) for i in range(4)]
X_ODD_RING = [(1, 2), (2, 1), (3, 0), (0, 3)]


def x_odd_owner():
    pairs = []
    for s in range(BLOCKS):
        pairs += [(s * 4 + 1, s * 4 + 2), (s * 4 + 2, s * 4 + 1)]
    for b in range(BLOCKS - 1):
        low, high = source_of(b) * 4 + 3, source_of(b + 1) * 4
        pairs += [(low, high), (high, low)]
    return pairs


SENT = [(0, 2), (0, 1), (1, 1), (0, 3), (1, 3)]
KEPT = [(1, 2), (0, 0), (1, 0)]


def start_products(idx_ref, f_hbm, a_hbm, c_hbm, f_buf, a_buf, c_buf, sems, count):
    copies = []
    for k in range(count):
        b = idx_ref[k]
        group = [
            pltpu.make_async_copy(f_hbm.at[:, :, b], f_buf.at[k], sems.at[0, k]),
            pltpu.make_async_copy(a_hbm.at[:, :, b], a_buf.at[k], sems.at[1, k]),
            pltpu.make_async_copy(c_hbm.at[:, b], c_buf.at[k], sems.at[2, k]),
        ]
        for copy in group:
            copy.start()
        copies.append(group)
    return copies


def block_products(k, copies, f_buf, a_buf, c_buf, out):
    for copy in copies[k]:
        copy.wait()
    for r in range(4):
        hor = ver = None
        for t in range(2):
            prod = [f_buf[k, t, c, r].astype(F32) * a_buf[k, t, c, r].astype(F32) for c in range(6)]
            h1 = (prod[0] + prod[1]) - (prod[3] + prod[4])
            v1 = prod[2] - prod[5]
            hor = h1 if hor is None else hor + h1
            ver = v1 if ver is None else ver + v1
        out[0, r] = hor * (c_buf[k, 0, r] * SCALE)
        out[1, r] = ver * (c_buf[k, 1, r] * SCALE)


def sent_kernel(idx_ref, f_hbm, a_hbm, c_hbm, far2, one, three, f_buf, a_buf, c_buf, sems):
    copies = start_products(idx_ref, f_hbm, a_hbm, c_hbm, f_buf, a_buf, c_buf, sems, len(SENT))
    for k, out in enumerate((far2, one.at[0], one.at[1], three.at[0], three.at[1])):
        block_products(k, copies, f_buf, a_buf, c_buf, out)


def kept_kernel(
    idx_ref, f_hbm, a_hbm, c_hbm, t_hbm, near2, far0, near0, d_own, d_odd, f_buf, a_buf, c_buf, t_buf, sems, t_sems
):
    n = len(KEPT)
    t_copies = [pltpu.make_async_copy(t_hbm.at[:, idx_ref[n + k]], t_buf.at[k], t_sems.at[k]) for k in range(2)]
    for copy in t_copies:
        copy.start()
    copies = start_products(idx_ref, f_hbm, a_hbm, c_hbm, f_buf, a_buf, c_buf, sems, n)
    inside = idx_ref[n + 2] > 0
    for copy in t_copies:
        copy.wait()
    for e in range(6):
        for r in range(4):
            d_own[e, r] = t_buf[0, e, r].astype(F32)
            d_odd[e, r] = jnp.where(inside, t_buf[1, e, r].astype(F32), 0.0)
    for k, out in enumerate((near2, far0, near0)):
        block_products(k, copies, f_buf, a_buf, c_buf, out)


def products_scratch(n):
    return [
        pltpu.VMEM((n, 2, 6, 4, 32, 128), jnp.bfloat16),
        pltpu.VMEM((n, 2, 6, 4, 32, 128), jnp.bfloat16),
        pltpu.VMEM((n, *SLAB), F32),
    ]


def in_hbm(*arrays):
    return [pltpu.with_memory_space_constraint(x, pltpu.HBM) for x in arrays]


def sent_products(idx, fwd, adj, cond):
    hbm = pl.BlockSpec(memory_space=pltpu.HBM)
    pair = jax.ShapeDtypeStruct((2, *SLAB), F32)
    return pl.pallas_call(
        sent_kernel,
        in_specs=[pl.BlockSpec(memory_space=pltpu.SMEM), hbm, hbm, hbm],
        out_shape=[jax.ShapeDtypeStruct(SLAB, F32), pair, pair],
        scratch_shapes=products_scratch(len(SENT)) + [pltpu.SemaphoreType.DMA((3, len(SENT)))],
        compiler_params=pltpu.CompilerParams(vmem_limit_bytes=32 << 20),
    )(idx, *in_hbm(fwd, adj, cond))


def kept_products(idx, fwd, adj, cond, tens):
    hbm = pl.BlockSpec(memory_space=pltpu.HBM)
    slab = jax.ShapeDtypeStruct(SLAB, F32)
    rim = jax.ShapeDtypeStruct((6, 4, 32, 128), F32)
    return pl.pallas_call(
        kept_kernel,
        in_specs=[pl.BlockSpec(memory_space=pltpu.SMEM), hbm, hbm, hbm, hbm],
        out_shape=[slab, slab, slab, rim, rim],
        scratch_shapes=products_scratch(len(KEPT))
        + [
            pltpu.VMEM((2, 6, 4, 32, 128), jnp.bfloat16),
            pltpu.SemaphoreType.DMA((3, len(KEPT))),
            pltpu.SemaphoreType.DMA((2,)),
        ],
        compiler_params=pltpu.CompilerParams(vmem_limit_bytes=32 << 20),
    )(idx, *in_hbm(fwd, adj, cond, tens))


def diffuse_kernel(f_lo, f_own, f_hi, d_lo, d_own, d_hi, out, buf, after, part, flux_z):
    fs, ds = (f_lo, f_own, f_hi), (d_lo, d_own, d_hi)
    lane = lax.broadcasted_iota(jnp.int32, (40, 128), 1)
    first, last = lane == 0, lane == 127

    def tensor(e, r):
        return ds[(r + 4) // 4][e, (r + 4) % 4]

    for p in range(PASSES):
        m = PASSES - 1 - p

        def field(c, r):
            if p == 0:
                return fs[(r + 4) // 4][c, (r + 4) % 4]
            return buf[(p - 1) % 2, c, r + 4]

        for r in range(-m - 1, 4 + m):
            for c in range(2):
                after[c, r + 4] = jnp.where(last, 0.0, pltpu.roll(field(c, r), 127, 1))
        flux_x_before = [None, None]
        here = [field(c, -m - 1) for c in range(2)]
        for r in range(-m - 1, 4 + m):
            d = [tensor(e, r) for e in range(6)]
            for c in range(2):
                f = here[c]
                nxt = field(c, r + 1)
                gx = nxt - f
                gy = pltpu.roll(f, 39, 0) - f
                gz = after[c, r + 4] - f
                fx = d[0] * gx + d[3] * gy + d[4] * gz
                if r >= -m:
                    fy = d[3] * gx + d[1] * gy + d[5] * gz
                    fz = d[4] * gx + d[5] * gy + d[2] * gz
                    part[c, r + 4] = (fx - flux_x_before[c]) + (fy - pltpu.roll(fy, 1, 0)) + fz
                    flux_z[c, r + 4] = fz
                flux_x_before[c] = fx
                here[c] = nxt
        for r in range(-m, 4 + m):
            gain = jnp.where(tensor(0, r) > 0, F32(STEP), F32(0))
            for c in range(2):
                spread = part[c, r + 4] - jnp.where(first, 0.0, pltpu.roll(flux_z[c, r + 4], 1, 1))
                new = field(c, r) + gain * spread
                if p == PASSES - 1:
                    out[c, r] = new[:32]
                else:
                    buf[p % 2, c, r + 4] = new


def diffuse(*args):
    rows = pltpu.VMEM((2, 12, 40, 128), F32)
    return pl.pallas_call(
        diffuse_kernel,
        out_shape=jax.ShapeDtypeStruct(SLAB, F32),
        scratch_shapes=[pltpu.VMEM((2, 2, 12, 40, 128), F32), rows, rows, rows],
        compiler_params=pltpu.CompilerParams(vmem_limit_bytes=32 << 20),
    )(*args)


def core_tile(cells, even):
    return jnp.where(even, cells[..., 28:, :], cells[..., :4, :])


def cross_tile(cells, even):
    return jnp.where(even, cells[..., :4, :], cells[..., 28:, :])


def halo_tile(core, cross, even):
    return jnp.concatenate([jnp.where(even, core, cross), jnp.where(even, cross, core)], axis=-2)


def shards(fwd, adj, cond, tens):
    s, gx, gy = lax.axis_index("source"), lax.axis_index("gx"), lax.axis_index("gy")
    h, z = s // NZC, s % NZC
    own = block_of(h, z)
    x_even, y_even = gx % 2 == 0, gy % 2 == 0

    def blocks(keys):
        return [block_of(jnp.where(half == 0, 1 - h, h), z ^ k) for half, k in keys]

    wrap = own + jnp.where(gx == 0, 1, 0) - jnp.where(gx == 3, 1, 0)
    inside = jnp.where((wrap >= 0) & (wrap < BLOCKS), 1, 0)
    sent_idx = jnp.stack(blocks(SENT)).astype(jnp.int32)
    kept_idx = jnp.stack(blocks(KEPT) + [own, jnp.clip(wrap, 0, BLOCKS - 1), inside]).astype(jnp.int32)
    far2, one, three = sent_products(sent_idx, fwd, adj, cond)
    kept_idx, far2, one, three = lax.optimization_barrier((kept_idx, far2, one, three))
    near2, far0, near0, d_own, d_odd = kept_products(kept_idx, fwd, adj, cond, tens)

    two_sum = near2 + lax.ppermute(far2, "source", Y_PERM)
    one_in = lax.ppermute(one, "source", z_perm(1))
    three_in = lax.ppermute(three, "source", z_perm(3))
    far_sum = far0 + one_in[0] + three_in[0]
    near_sum = near0 + one_in[1] + three_in[1]
    two_sum, far_sum = lax.optimization_barrier((two_sum, far_sum))
    two_in = lax.ppermute(two_sum, "source", z_perm(2))
    from_far = lax.ppermute(far_sum, "source", Y_PERM)

    rims = jnp.stack([d_own, d_odd])
    d_core = lax.ppermute(core_tile(rims, y_even), "gy", CORE_PERM)
    d_cross = lax.ppermute(cross_tile(rims, y_even), "gy", CROSS_PERM)
    _, d_core, d_cross = lax.optimization_barrier((far_sum, d_core, d_cross))
    tiles = halo_tile(d_core, d_cross, y_even)
    d_own = jnp.concatenate([d_own, tiles[0]], axis=-2)
    d_odd = jnp.concatenate([d_odd, tiles[1]], axis=-2)
    d_odd_in = lax.ppermute(d_odd, "gx", X_ODD_RING)
    d_even_in = lax.ppermute(d_own, "gx", X_EVEN)
    field = near_sum + from_far + two_in

    core = lax.ppermute(core_tile(field, y_even), "gy", CORE_PERM)
    cross = lax.ppermute(cross_tile(field, y_even), "gy", CROSS_PERM)
    f_own = jnp.concatenate([field, halo_tile(core, cross, y_even)], axis=-2)
    f_odd_in = lax.ppermute(f_own, ("source", "gx"), x_odd_owner())
    f_even_in = lax.ppermute(f_own, "gx", X_EVEN)
    d_lo = jnp.where(x_even, d_odd_in, d_even_in)
    d_hi = jnp.where(x_even, d_even_in, d_odd_in)
    d_lo, d_hi, f_odd_in = lax.optimization_barrier((d_lo, d_hi, f_odd_in))
    f_hi = jnp.where(x_even, f_even_in, f_odd_in)
    f_lo = jnp.where(x_even, f_odd_in, f_even_in)
    f_hi, f_lo = lax.optimization_barrier((f_hi, f_lo))

    done = diffuse(f_lo, f_own, f_hi, d_lo, d_own, d_hi)

    two = lax.ppermute(done, "source", z_perm(2))
    other = lax.ppermute(done, "source", Y_PERM)
    one, three = (lax.ppermute(done, "source", z_perm(k)) for k in (1, 3))
    other_two = lax.ppermute(two, "source", Y_PERM)
    other_one, other_three = (lax.ppermute(other, "source", z_perm(k)) for k in (1, 3))
    out = jnp.zeros((2, BLOCKS, 4, 32, 128), F32)
    for half, k, piece in (
        (h, 2, two),
        (h, 0, done),
        (1 - h, 0, other),
        (h, 1, one),
        (h, 3, three),
        (1 - h, 2, other_two),
        (1 - h, 1, other_one),
        (1 - h, 3, other_three),
    ):
        out = lax.dynamic_update_index_in_dim(out, piece, block_of(half, z ^ k), 1)
    return out


def solution(mesh):
    fields = P("source", None, None, "gx", "gy", None)
    cells = P(None, None, "gx", "gy", None)
    return jax.shard_map(
        shards, mesh=mesh, in_specs=(fields, fields, cells, cells), out_specs=cells, check_vma=False
    )
```

```python
import jax
import jax.numpy as jnp
from jax import lax
from jax.experimental import pallas as pl
from jax.experimental.pallas import tpu as pltpu
from jax.sharding import PartitionSpec as P

PASSES = 4
STEP = 0.13
SCALE = 1.0 / 16.0
NZC = 4
BLOCKS = 2 * NZC
F32 = jnp.float32
SLAB = (2, 4, 32, 128)


def block_of(h, z):
    place = (z + 2) % NZC
    return jnp.where(h == 0, place, BLOCKS - 1 - place)


def source_of(b):
    return (b + 2) % NZC if b < NZC else NZC + (BLOCKS + 1 - b) % NZC


def z_perm(k):
    return [(s, s ^ k) for s in range(BLOCKS)]


Y_PERM = [(s, (s + NZC) % BLOCKS) for s in range(BLOCKS)]
CORE_PERM = [(i, i ^ 1) for i in range(4)]
CROSS_PERM = [(1, 2), (2, 1)]
X_EVEN = [(i, i ^ 1) for i in range(4)]
X_ODD_RING = [(1, 2), (2, 1), (3, 0), (0, 3)]


def x_odd_owner():
    pairs = []
    for s in range(BLOCKS):
        pairs += [(s * 4 + 1, s * 4 + 2), (s * 4 + 2, s * 4 + 1)]
    for b in range(BLOCKS - 1):
        low, high = source_of(b) * 4 + 3, source_of(b + 1) * 4
        pairs += [(low, high), (high, low)]
    return pairs


SENT = [(0, 2), (0, 1), (1, 1), (0, 3), (1, 3)]
KEPT = [(1, 2), (0, 0), (1, 0)]


def start_products(idx_ref, f_hbm, a_hbm, c_hbm, f_buf, a_buf, c_buf, sems, count):
    copies = []
    for k in range(count):
        b = idx_ref[k]
        group = [
            pltpu.make_async_copy(f_hbm.at[:, :, b], f_buf.at[k], sems.at[0, k]),
            pltpu.make_async_copy(a_hbm.at[:, :, b], a_buf.at[k], sems.at[1, k]),
            pltpu.make_async_copy(c_hbm.at[:, b], c_buf.at[k], sems.at[2, k]),
        ]
        for copy in group:
            copy.start()
        copies.append(group)
    return copies


def block_products(k, copies, f_buf, a_buf, c_buf, out):
    for copy in copies[k]:
        copy.wait()
    for r in range(4):
        hor = ver = None
        for t in range(2):
            prod = [f_buf[k, t, c, r].astype(F32) * a_buf[k, t, c, r].astype(F32) for c in range(6)]
            h1 = (prod[0] + prod[1]) - (prod[3] + prod[4])
            v1 = prod[2] - prod[5]
            hor = h1 if hor is None else hor + h1
            ver = v1 if ver is None else ver + v1
        out[0, r] = hor * (c_buf[k, 0, r] * SCALE)
        out[1, r] = ver * (c_buf[k, 1, r] * SCALE)


def sent_kernel(idx_ref, f_hbm, a_hbm, c_hbm, far2, one, three, f_buf, a_buf, c_buf, sems):
    copies = start_products(idx_ref, f_hbm, a_hbm, c_hbm, f_buf, a_buf, c_buf, sems, len(SENT))
    for k, out in enumerate((far2, one.at[0], one.at[1], three.at[0], three.at[1])):
        block_products(k, copies, f_buf, a_buf, c_buf, out)


def kept_kernel(
    idx_ref, f_hbm, a_hbm, c_hbm, t_hbm, near2, far0, near0, d_own, d_odd, f_buf, a_buf, c_buf, t_buf, sems, t_sems
):
    n = len(KEPT)
    t_copies = [pltpu.make_async_copy(t_hbm.at[:, idx_ref[n + k]], t_buf.at[k], t_sems.at[k]) for k in range(2)]
    for copy in t_copies:
        copy.start()
    copies = start_products(idx_ref, f_hbm, a_hbm, c_hbm, f_buf, a_buf, c_buf, sems, n)
    inside = idx_ref[n + 2] > 0
    for copy in t_copies:
        copy.wait()
    for e in range(6):
        for r in range(4):
            d_own[e, r] = t_buf[0, e, r].astype(F32)
            d_odd[e, r] = jnp.where(inside, t_buf[1, e, r].astype(F32), 0.0)
    for k, out in enumerate((near2, far0, near0)):
        block_products(k, copies, f_buf, a_buf, c_buf, out)


def products_scratch(n):
    return [
        pltpu.VMEM((n, 2, 6, 4, 32, 128), jnp.bfloat16),
        pltpu.VMEM((n, 2, 6, 4, 32, 128), jnp.bfloat16),
        pltpu.VMEM((n, *SLAB), F32),
    ]


def in_hbm(*arrays):
    return [pltpu.with_memory_space_constraint(x, pltpu.HBM) for x in arrays]


def sent_products(idx, fwd, adj, cond):
    hbm = pl.BlockSpec(memory_space=pltpu.HBM)
    pair = jax.ShapeDtypeStruct((2, *SLAB), F32)
    return pl.pallas_call(
        sent_kernel,
        in_specs=[pl.BlockSpec(memory_space=pltpu.SMEM), hbm, hbm, hbm],
        out_shape=[jax.ShapeDtypeStruct(SLAB, F32), pair, pair],
        scratch_shapes=products_scratch(len(SENT)) + [pltpu.SemaphoreType.DMA((3, len(SENT)))],
        compiler_params=pltpu.CompilerParams(vmem_limit_bytes=32 << 20),
    )(idx, *in_hbm(fwd, adj, cond))


def kept_products(idx, fwd, adj, cond, tens):
    hbm = pl.BlockSpec(memory_space=pltpu.HBM)
    slab = jax.ShapeDtypeStruct(SLAB, F32)
    rim = jax.ShapeDtypeStruct((6, 4, 32, 128), F32)
    return pl.pallas_call(
        kept_kernel,
        in_specs=[pl.BlockSpec(memory_space=pltpu.SMEM), hbm, hbm, hbm, hbm],
        out_shape=[slab, slab, slab, rim, rim],
        scratch_shapes=products_scratch(len(KEPT))
        + [
            pltpu.VMEM((2, 6, 4, 32, 128), jnp.bfloat16),
            pltpu.SemaphoreType.DMA((3, len(KEPT))),
            pltpu.SemaphoreType.DMA((2,)),
        ],
        compiler_params=pltpu.CompilerParams(vmem_limit_bytes=32 << 20),
    )(idx, *in_hbm(fwd, adj, cond, tens))


def diffuse_kernel(f_lo, f_own, f_hi, d_lo, d_own, d_hi, out, buf, after, part, flux_z):
    fs, ds = (f_lo, f_own, f_hi), (d_lo, d_own, d_hi)
    lane = lax.broadcasted_iota(jnp.int32, (40, 128), 1)
    first, last = lane == 0, lane == 127

    def tensor(e, r):
        return ds[(r + 4) // 4][e, (r + 4) % 4]

    for p in range(PASSES):
        m = PASSES - 1 - p

        def field(c, r):
            if p == 0:
                return fs[(r + 4) // 4][c, (r + 4) % 4]
            return buf[(p - 1) % 2, c, r + 4]

        for r in range(-m - 1, 4 + m):
            for c in range(2):
                after[c, r + 4] = jnp.where(last, 0.0, pltpu.roll(field(c, r), 127, 1))
        flux_x_before = [None, None]
        here = [field(c, -m - 1) for c in range(2)]
        for r in range(-m - 1, 4 + m):
            d = [tensor(e, r) for e in range(6)]
            for c in range(2):
                f = here[c]
                nxt = field(c, r + 1)
                gx = nxt - f
                gy = pltpu.roll(f, 39, 0) - f
                gz = after[c, r + 4] - f
                fx = d[0] * gx + d[3] * gy + d[4] * gz
                if r >= -m:
                    fy = d[3] * gx + d[1] * gy + d[5] * gz
                    fz = d[4] * gx + d[5] * gy + d[2] * gz
                    part[c, r + 4] = (fx - flux_x_before[c]) + (fy - pltpu.roll(fy, 1, 0)) + fz
                    flux_z[c, r + 4] = fz
                flux_x_before[c] = fx
                here[c] = nxt
        for r in range(-m, 4 + m):
            gain = jnp.where(tensor(0, r) > 0, F32(STEP), F32(0))
            for c in range(2):
                spread = part[c, r + 4] - jnp.where(first, 0.0, pltpu.roll(flux_z[c, r + 4], 1, 1))
                new = field(c, r) + gain * spread
                if p == PASSES - 1:
                    out[c, r] = new[:32]
                else:
                    buf[p % 2, c, r + 4] = new


def diffuse(*args):
    rows = pltpu.VMEM((2, 12, 40, 128), F32)
    return pl.pallas_call(
        diffuse_kernel,
        out_shape=jax.ShapeDtypeStruct(SLAB, F32),
        scratch_shapes=[pltpu.VMEM((2, 2, 12, 40, 128), F32), rows, rows, rows],
        compiler_params=pltpu.CompilerParams(vmem_limit_bytes=32 << 20),
    )(*args)


def core_tile(cells, even):
    return jnp.where(even, cells[..., 28:, :], cells[..., :4, :])


def cross_tile(cells, even):
    return jnp.where(even, cells[..., :4, :], cells[..., 28:, :])


def halo_tile(core, cross, even):
    return jnp.concatenate([jnp.where(even, core, cross), jnp.where(even, cross, core)], axis=-2)


def shards(fwd, adj, cond, tens):
    s, gx, gy = lax.axis_index("source"), lax.axis_index("gx"), lax.axis_index("gy")
    h, z = s // NZC, s % NZC
    own = block_of(h, z)
    x_even, y_even = gx % 2 == 0, gy % 2 == 0

    def blocks(keys):
        return [block_of(jnp.where(half == 0, 1 - h, h), z ^ k) for half, k in keys]

    wrap = own + jnp.where(gx == 0, 1, 0) - jnp.where(gx == 3, 1, 0)
    inside = jnp.where((wrap >= 0) & (wrap < BLOCKS), 1, 0)
    sent_idx = jnp.stack(blocks(SENT)).astype(jnp.int32)
    kept_idx = jnp.stack(blocks(KEPT) + [own, jnp.clip(wrap, 0, BLOCKS - 1), inside]).astype(jnp.int32)
    far2, one, three = sent_products(sent_idx, fwd, adj, cond)
    kept_idx, far2, one, three = lax.optimization_barrier((kept_idx, far2, one, three))
    near2, far0, near0, d_own, d_odd = kept_products(kept_idx, fwd, adj, cond, tens)

    two_sum = near2 + lax.ppermute(far2, "source", Y_PERM)
    two_in = lax.ppermute(two_sum, "source", z_perm(2))
    one_in = lax.ppermute(one, "source", z_perm(1))
    three_in = lax.ppermute(three, "source", z_perm(3))
    far_sum = far0 + one_in[0] + three_in[0]
    near_sum = near0 + one_in[1] + three_in[1]
    from_far = lax.ppermute(far_sum, "source", Y_PERM)

    rims = jnp.stack([d_own, d_odd])
    d_core = lax.ppermute(core_tile(rims, y_even), "gy", CORE_PERM)
    d_cross = lax.ppermute(cross_tile(rims, y_even), "gy", CROSS_PERM)
    _, d_core, d_cross = lax.optimization_barrier((far_sum, d_core, d_cross))
    tiles = halo_tile(d_core, d_cross, y_even)
    d_own = jnp.concatenate([d_own, tiles[0]], axis=-2)
    d_odd = jnp.concatenate([d_odd, tiles[1]], axis=-2)
    d_odd_in = lax.ppermute(d_odd, "gx", X_ODD_RING)
    d_even_in = lax.ppermute(d_own, "gx", X_EVEN)
    field = near_sum + from_far
    field, two_in = lax.optimization_barrier((field, two_in))
    field = field + two_in

    core = lax.ppermute(core_tile(field, y_even), "gy", CORE_PERM)
    cross = lax.ppermute(cross_tile(field, y_even), "gy", CROSS_PERM)
    f_own = jnp.concatenate([field, halo_tile(core, cross, y_even)], axis=-2)
    f_odd_in = lax.ppermute(f_own, ("source", "gx"), x_odd_owner())
    f_even_in = lax.ppermute(f_own, "gx", X_EVEN)
    d_lo = jnp.where(x_even, d_odd_in, d_even_in)
    d_hi = jnp.where(x_even, d_even_in, d_odd_in)
    d_lo, d_hi, f_odd_in = lax.optimization_barrier((d_lo, d_hi, f_odd_in))
    f_hi = jnp.where(x_even, f_even_in, f_odd_in)
    f_lo = jnp.where(x_even, f_odd_in, f_even_in)
    f_hi, f_lo = lax.optimization_barrier((f_hi, f_lo))

    done = diffuse(f_lo, f_own, f_hi, d_lo, d_own, d_hi)

    two = lax.ppermute(done, "source", z_perm(2))
    other = lax.ppermute(done, "source", Y_PERM)
    one, three = (lax.ppermute(done, "source", z_perm(k)) for k in (1, 3))
    other_two = lax.ppermute(two, "source", Y_PERM)
    other_one, other_three = (lax.ppermute(other, "source", z_perm(k)) for k in (1, 3))
    out = jnp.zeros((2, BLOCKS, 4, 32, 128), F32)
    for half, k, piece in (
        (h, 2, two),
        (h, 0, done),
        (1 - h, 0, other),
        (h, 1, one),
        (h, 3, three),
        (1 - h, 2, other_two),
        (1 - h, 1, other_one),
        (1 - h, 3, other_three),
    ):
        out = lax.dynamic_update_index_in_dim(out, piece, block_of(half, z ^ k), 1)
    return out


def solution(mesh):
    fields = P("source", None, None, "gx", "gy", None)
    cells = P(None, None, "gx", "gy", None)
    return jax.shard_map(
        shards, mesh=mesh, in_specs=(fields, fields, cells, cells), out_specs=cells, check_vma=False
    )
```

```python
import jax
import jax.numpy as jnp
from jax import lax
from jax.experimental import pallas as pl
from jax.experimental.pallas import tpu as pltpu
from jax.sharding import PartitionSpec as P

PASSES = 4
STEP = 0.13
SCALE = 1.0 / 16.0
NZC = 4
BLOCKS = 2 * NZC
F32 = jnp.float32
SLAB = (2, 4, 32, 128)


def block_of(h, z):
    return jnp.where(h == 0, z, BLOCKS - 1 - z)


def source_of(b):
    return b if b < NZC else 3 * NZC - 1 - b


def z_perm(k):
    return [(s, s ^ k) for s in range(BLOCKS)]


Y_PERM = [(s, (s + NZC) % BLOCKS) for s in range(BLOCKS)]
CORE_PERM = [(i, i ^ 1) for i in range(4)]
CROSS_PERM = [(1, 2), (2, 1)]
X_EVEN = [(i, i ^ 1) for i in range(4)]
X_ODD_RING = [(1, 2), (2, 1), (3, 0), (0, 3)]


def x_odd_owner():
    pairs = []
    for s in range(BLOCKS):
        pairs += [(s * 4 + 1, s * 4 + 2), (s * 4 + 2, s * 4 + 1)]
    for b in range(BLOCKS - 1):
        low, high = source_of(b) * 4 + 3, source_of(b + 1) * 4
        pairs += [(low, high), (high, low)]
    return pairs


SENT = [(0, 2), (0, 1), (1, 1), (0, 3), (1, 3)]
KEPT = [(1, 2), (0, 0), (1, 0)]


def start_products(idx_ref, f_hbm, a_hbm, f_buf, a_buf, sems, count):
    copies = []
    for k in range(count):
        b = idx_ref[k]
        group = [
            pltpu.make_async_copy(f_hbm.at[:, :, b], f_buf.at[k], sems.at[0, k]),
            pltpu.make_async_copy(a_hbm.at[:, :, b], a_buf.at[k], sems.at[1, k]),
        ]
        for copy in group:
            copy.start()
        copies.append(group)
    return copies


def block_products(k, copies, f_buf, a_buf, out):
    for copy in copies[k]:
        copy.wait()
    for r in range(4):
        hor = ver = None
        for t in range(2):
            prod = [f_buf[k, t, c, r].astype(F32) * a_buf[k, t, c, r].astype(F32) for c in range(6)]
            h1 = (prod[0] + prod[1]) - (prod[3] + prod[4])
            v1 = prod[2] - prod[5]
            hor = h1 if hor is None else hor + h1
            ver = v1 if ver is None else ver + v1
        out[0, r] = hor
        out[1, r] = ver


def sent_kernel(idx_ref, f_hbm, a_hbm, far2, one, three, f_buf, a_buf, sems):
    copies = start_products(idx_ref, f_hbm, a_hbm, f_buf, a_buf, sems, len(SENT))
    for k, out in enumerate((far2, one.at[0], one.at[1], three.at[0], three.at[1])):
        block_products(k, copies, f_buf, a_buf, out)


def kept_kernel(
    idx_ref, f_hbm, a_hbm, c_hbm, t_hbm, near2, far0, near0, c_own, d_own, d_odd, f_buf, a_buf, c_buf, t_buf, sems,
    t_sems, c_sem
):
    n = len(KEPT)
    t_copies = [pltpu.make_async_copy(t_hbm.at[:, idx_ref[n + k]], t_buf.at[k], t_sems.at[k]) for k in range(2)]
    for copy in t_copies:
        copy.start()
    copies = start_products(idx_ref, f_hbm, a_hbm, f_buf, a_buf, sems, n)
    c_copy = pltpu.make_async_copy(c_hbm.at[:, idx_ref[n]], c_buf, c_sem)
    c_copy.start()
    inside = idx_ref[n + 2] > 0
    for copy in t_copies:
        copy.wait()
    for e in range(6):
        for r in range(4):
            d_own[e, r] = t_buf[0, e, r].astype(F32)
            d_odd[e, r] = jnp.where(inside, t_buf[1, e, r].astype(F32), 0.0)
    for k, out in enumerate((near2, far0, near0)):
        block_products(k, copies, f_buf, a_buf, out)
    c_copy.wait()
    c_own[...] = c_buf[...] * SCALE


def products_scratch(n):
    return [
        pltpu.VMEM((n, 2, 6, 4, 32, 128), jnp.bfloat16),
        pltpu.VMEM((n, 2, 6, 4, 32, 128), jnp.bfloat16),
    ]


def in_hbm(*arrays):
    return [pltpu.with_memory_space_constraint(x, pltpu.HBM) for x in arrays]


def sent_products(idx, fwd, adj):
    hbm = pl.BlockSpec(memory_space=pltpu.HBM)
    pair = jax.ShapeDtypeStruct((2, *SLAB), F32)
    return pl.pallas_call(
        sent_kernel,
        in_specs=[pl.BlockSpec(memory_space=pltpu.SMEM), hbm, hbm],
        out_shape=[jax.ShapeDtypeStruct(SLAB, F32), pair, pair],
        scratch_shapes=products_scratch(len(SENT)) + [pltpu.SemaphoreType.DMA((2, len(SENT)))],
        compiler_params=pltpu.CompilerParams(vmem_limit_bytes=32 << 20),
    )(idx, *in_hbm(fwd, adj))


def kept_products(idx, fwd, adj, cond, tens):
    hbm = pl.BlockSpec(memory_space=pltpu.HBM)
    slab = jax.ShapeDtypeStruct(SLAB, F32)
    rim = jax.ShapeDtypeStruct((6, 4, 32, 128), F32)
    return pl.pallas_call(
        kept_kernel,
        in_specs=[pl.BlockSpec(memory_space=pltpu.SMEM), hbm, hbm, hbm, hbm],
        out_shape=[slab, slab, slab, slab, rim, rim],
        scratch_shapes=products_scratch(len(KEPT))
        + [
            pltpu.VMEM(SLAB, F32),
            pltpu.VMEM((2, 6, 4, 32, 128), jnp.bfloat16),
            pltpu.SemaphoreType.DMA((2, len(KEPT))),
            pltpu.SemaphoreType.DMA((2,)),
            pltpu.SemaphoreType.DMA(()),
        ],
        compiler_params=pltpu.CompilerParams(vmem_limit_bytes=32 << 20),
    )(idx, *in_hbm(fwd, adj, cond, tens))


def diffuse_kernel(f_lo, f_own, f_hi, d_lo, d_own, d_hi, out, buf, after, part, flux_z):
    fs, ds = (f_lo, f_own, f_hi), (d_lo, d_own, d_hi)
    lane = lax.broadcasted_iota(jnp.int32, (40, 128), 1)
    first, last = lane == 0, lane == 127

    def tensor(e, r):
        return ds[(r + 4) // 4][e, (r + 4) % 4]

    for p in range(PASSES):
        m = PASSES - 1 - p

        def field(c, r):
            if p == 0:
                return fs[(r + 4) // 4][c, (r + 4) % 4]
            return buf[(p - 1) % 2, c, r + 4]

        for r in range(-m - 1, 4 + m):
            for c in range(2):
                after[c, r + 4] = jnp.where(last, 0.0, pltpu.roll(field(c, r), 127, 1))
        flux_x_before = [None, None]
        here = [field(c, -m - 1) for c in range(2)]
        for r in range(-m - 1, 4 + m):
            d = [tensor(e, r) for e in range(6)]
            for c in range(2):
                f = here[c]
                nxt = field(c, r + 1)
                gx = nxt - f
                gy = pltpu.roll(f, 39, 0) - f
                gz = after[c, r + 4] - f
                fx = d[0] * gx + d[3] * gy + d[4] * gz
                if r >= -m:
                    fy = d[3] * gx + d[1] * gy + d[5] * gz
                    fz = d[4] * gx + d[5] * gy + d[2] * gz
                    part[c, r + 4] = (fx - flux_x_before[c]) + (fy - pltpu.roll(fy, 1, 0)) + fz
                    flux_z[c, r + 4] = fz
                flux_x_before[c] = fx
                here[c] = nxt
        for r in range(-m, 4 + m):
            gain = jnp.where(tensor(0, r) > 0, F32(STEP), F32(0))
            for c in range(2):
                spread = part[c, r + 4] - jnp.where(first, 0.0, pltpu.roll(flux_z[c, r + 4], 1, 1))
                new = field(c, r) + gain * spread
                if p == PASSES - 1:
                    out[c, r] = new[:32]
                else:
                    buf[p % 2, c, r + 4] = new


def diffuse(*args):
    rows = pltpu.VMEM((2, 12, 40, 128), F32)
    return pl.pallas_call(
        diffuse_kernel,
        out_shape=jax.ShapeDtypeStruct(SLAB, F32),
        scratch_shapes=[pltpu.VMEM((2, 2, 12, 40, 128), F32), rows, rows, rows],
        compiler_params=pltpu.CompilerParams(vmem_limit_bytes=32 << 20),
    )(*args)


def core_tile(cells, even):
    return jnp.where(even, cells[..., 28:, :], cells[..., :4, :])


def cross_tile(cells, even):
    return jnp.where(even, cells[..., :4, :], cells[..., 28:, :])


def halo_tile(core, cross, even):
    return jnp.concatenate([jnp.where(even, core, cross), jnp.where(even, cross, core)], axis=-2)


def shards(fwd, adj, cond, tens):
    s, gx, gy = lax.axis_index("source"), lax.axis_index("gx"), lax.axis_index("gy")
    h, z = s // NZC, s % NZC
    own = block_of(h, z)
    x_even, y_even = gx % 2 == 0, gy % 2 == 0

    def blocks(keys):
        return [block_of(jnp.where(half == 0, 1 - h, h), z ^ k) for half, k in keys]

    wrap = own + jnp.where(gx == 0, 1, 0) - jnp.where(gx == 3, 1, 0)
    inside = jnp.where((wrap >= 0) & (wrap < BLOCKS), 1, 0)
    sent_idx = jnp.stack(blocks(SENT)).astype(jnp.int32)
    kept_idx = jnp.stack(blocks(KEPT) + [own, jnp.clip(wrap, 0, BLOCKS - 1), inside]).astype(jnp.int32)
    far2, one, three = sent_products(sent_idx, fwd, adj)
    kept_idx, far2, one, three = lax.optimization_barrier((kept_idx, far2, one, three))
    near2, far0, near0, c_own, d_own, d_odd = kept_products(kept_idx, fwd, adj, cond, tens)

    two_sum = near2 + lax.ppermute(far2, "source", Y_PERM)
    two_in = lax.ppermute(two_sum, "source", z_perm(2))
    one_in = lax.ppermute(one, "source", z_perm(1))
    three_in = lax.ppermute(three, "source", z_perm(3))
    far_sum = far0 + one_in[0] + three_in[0]
    near_sum = near0 + one_in[1] + three_in[1]
    from_far = lax.ppermute(far_sum, "source", Y_PERM)

    rims = jnp.stack([d_own, d_odd])
    d_core = lax.ppermute(core_tile(rims, y_even), "gy", CORE_PERM)
    d_cross = lax.ppermute(cross_tile(rims, y_even), "gy", CROSS_PERM)
    _, d_core, d_cross = lax.optimization_barrier((far_sum, d_core, d_cross))
    tiles = halo_tile(d_core, d_cross, y_even)
    d_own = jnp.concatenate([d_own, tiles[0]], axis=-2)
    d_odd = jnp.concatenate([d_odd, tiles[1]], axis=-2)
    d_odd_in = lax.ppermute(d_odd, "gx", X_ODD_RING)
    d_even_in = lax.ppermute(d_own, "gx", X_EVEN)
    field = near_sum + from_far
    field, two_in = lax.optimization_barrier((field, two_in))
    field = (field + two_in) * c_own

    core = lax.ppermute(core_tile(field, y_even), "gy", CORE_PERM)
    cross = lax.ppermute(cross_tile(field, y_even), "gy", CROSS_PERM)
    f_own = jnp.concatenate([field, halo_tile(core, cross, y_even)], axis=-2)
    f_odd_in = lax.ppermute(f_own, ("source", "gx"), x_odd_owner())
    f_even_in = lax.ppermute(f_own, "gx", X_EVEN)
    d_lo = jnp.where(x_even, d_odd_in, d_even_in)
    d_hi = jnp.where(x_even, d_even_in, d_odd_in)
    d_lo, d_hi, f_odd_in = lax.optimization_barrier((d_lo, d_hi, f_odd_in))
    f_hi = jnp.where(x_even, f_even_in, f_odd_in)
    f_lo = jnp.where(x_even, f_odd_in, f_even_in)
    f_hi, f_lo = lax.optimization_barrier((f_hi, f_lo))

    done = diffuse(f_lo, f_own, f_hi, d_lo, d_own, d_hi)

    two = lax.ppermute(done, "source", z_perm(2))
    other = lax.ppermute(done, "source", Y_PERM)
    one, three = (lax.ppermute(done, "source", z_perm(k)) for k in (1, 3))
    other_two = lax.ppermute(two, "source", Y_PERM)
    other_one, other_three = (lax.ppermute(other, "source", z_perm(k)) for k in (1, 3))
    out = jnp.zeros((2, BLOCKS, 4, 32, 128), F32)
    for half, k, piece in (
        (h, 2, two),
        (h, 0, done),
        (1 - h, 0, other),
        (h, 1, one),
        (h, 3, three),
        (1 - h, 2, other_two),
        (1 - h, 1, other_one),
        (1 - h, 3, other_three),
    ):
        out = lax.dynamic_update_index_in_dim(out, piece, block_of(half, z ^ k), 1)
    return out


def solution(mesh):
    fields = P("source", None, None, "gx", "gy", None)
    cells = P(None, None, "gx", "gy", None)
    return jax.shard_map(
        shards, mesh=mesh, in_specs=(fields, fields, cells, cells), out_specs=cells, check_vma=False
    )
```

```python
import jax
import jax.numpy as jnp
from jax import lax
from jax.experimental import pallas as pl
from jax.experimental.pallas import tpu as pltpu
from jax.sharding import PartitionSpec as P

PASSES = 4
STEP = 0.13
SCALE = 1.0 / 16.0
NZC = 4
BLOCKS = 2 * NZC
F32 = jnp.float32
SLAB = (2, 4, 32, 128)


def block_of(h, z):
    return jnp.where(h == 0, z, BLOCKS - 1 - z)


def source_of(b):
    return b if b < NZC else 3 * NZC - 1 - b


def z_perm(k):
    return [(s, s ^ k) for s in range(BLOCKS)]


Y_PERM = [(s, (s + NZC) % BLOCKS) for s in range(BLOCKS)]
CORE_PERM = [(i, i ^ 1) for i in range(4)]
CROSS_PERM = [(1, 2), (2, 1)]
X_EVEN = [(i, i ^ 1) for i in range(4)]
X_ODD_RING = [(1, 2), (2, 1), (3, 0), (0, 3)]


def x_odd_owner():
    pairs = []
    for s in range(BLOCKS):
        pairs += [(s * 4 + 1, s * 4 + 2), (s * 4 + 2, s * 4 + 1)]
    for b in range(BLOCKS - 1):
        low, high = source_of(b) * 4 + 3, source_of(b + 1) * 4
        pairs += [(low, high), (high, low)]
    return pairs


SENT = [(0, 2), (0, 1), (1, 1), (0, 3), (1, 3)]
KEPT = [(1, 2), (0, 0), (1, 0)]


def start_products(idx_ref, f_hbm, a_hbm, f_buf, a_buf, sems, count):
    copies = []
    for k in range(count):
        b = idx_ref[k]
        group = [
            pltpu.make_async_copy(f_hbm.at[:, :, b], f_buf.at[k], sems.at[0, k]),
            pltpu.make_async_copy(a_hbm.at[:, :, b], a_buf.at[k], sems.at[1, k]),
        ]
        for copy in group:
            copy.start()
        copies.append(group)
    return copies


def block_products(k, copies, f_buf, a_buf, out):
    for copy in copies[k]:
        copy.wait()
    for r in range(4):
        hor = ver = None
        for t in range(2):
            prod = [f_buf[k, t, c, r].astype(F32) * a_buf[k, t, c, r].astype(F32) for c in range(6)]
            h1 = (prod[0] + prod[1]) - (prod[3] + prod[4])
            v1 = prod[2] - prod[5]
            hor = h1 if hor is None else hor + h1
            ver = v1 if ver is None else ver + v1
        out[0, r] = hor
        out[1, r] = ver


def sent_kernel(idx_ref, f_hbm, a_hbm, far2, one, three, f_buf, a_buf, sems):
    copies = start_products(idx_ref, f_hbm, a_hbm, f_buf, a_buf, sems, len(SENT))
    for k, out in enumerate((far2, one.at[0], one.at[1], three.at[0], three.at[1])):
        block_products(k, copies, f_buf, a_buf, out)


def kept_kernel(
    idx_ref, f_hbm, a_hbm, c_hbm, t_hbm, near2, far0, near0, c_own, d_own, d_odd, f_buf, a_buf, c_buf, t_buf, sems,
    t_sems, c_sem
):
    n = len(KEPT)
    t_copies = [pltpu.make_async_copy(t_hbm.at[:, idx_ref[n + k]], t_buf.at[k], t_sems.at[k]) for k in range(2)]
    for copy in t_copies:
        copy.start()
    copies = start_products(idx_ref, f_hbm, a_hbm, f_buf, a_buf, sems, n)
    c_copy = pltpu.make_async_copy(c_hbm.at[:, idx_ref[n]], c_buf, c_sem)
    c_copy.start()
    inside = idx_ref[n + 2] > 0
    for copy in t_copies:
        copy.wait()
    for e in range(6):
        for r in range(4):
            d_own[e, r] = t_buf[0, e, r].astype(F32)
            d_odd[e, r] = jnp.where(inside, t_buf[1, e, r].astype(F32), 0.0)
    for k, out in enumerate((near2, far0, near0)):
        block_products(k, copies, f_buf, a_buf, out)
    c_copy.wait()
    c_own[...] = c_buf[...] * SCALE


def products_scratch(n):
    return [
        pltpu.VMEM((n, 2, 6, 4, 32, 128), jnp.bfloat16),
        pltpu.VMEM((n, 2, 6, 4, 32, 128), jnp.bfloat16),
    ]


def in_hbm(*arrays):
    return [pltpu.with_memory_space_constraint(x, pltpu.HBM) for x in arrays]


def sent_products(idx, fwd, adj):
    hbm = pl.BlockSpec(memory_space=pltpu.HBM)
    pair = jax.ShapeDtypeStruct((2, *SLAB), F32)
    return pl.pallas_call(
        sent_kernel,
        in_specs=[pl.BlockSpec(memory_space=pltpu.SMEM), hbm, hbm],
        out_shape=[jax.ShapeDtypeStruct(SLAB, F32), pair, pair],
        scratch_shapes=products_scratch(len(SENT)) + [pltpu.SemaphoreType.DMA((2, len(SENT)))],
        compiler_params=pltpu.CompilerParams(vmem_limit_bytes=32 << 20),
    )(idx, *in_hbm(fwd, adj))


def kept_products(idx, fwd, adj, cond, tens):
    hbm = pl.BlockSpec(memory_space=pltpu.HBM)
    slab = jax.ShapeDtypeStruct(SLAB, F32)
    rim = jax.ShapeDtypeStruct((6, 4, 32, 128), F32)
    return pl.pallas_call(
        kept_kernel,
        in_specs=[pl.BlockSpec(memory_space=pltpu.SMEM), hbm, hbm, hbm, hbm],
        out_shape=[slab, slab, slab, slab, rim, rim],
        scratch_shapes=products_scratch(len(KEPT))
        + [
            pltpu.VMEM(SLAB, F32),
            pltpu.VMEM((2, 6, 4, 32, 128), jnp.bfloat16),
            pltpu.SemaphoreType.DMA((2, len(KEPT))),
            pltpu.SemaphoreType.DMA((2,)),
            pltpu.SemaphoreType.DMA(()),
        ],
        compiler_params=pltpu.CompilerParams(vmem_limit_bytes=32 << 20),
    )(idx, *in_hbm(fwd, adj, cond, tens))


def diffuse_kernel(f_lo, f_own, f_hi, d_lo, d_own, d_hi, out, buf, after, part, flux_z):
    fs, ds = (f_lo, f_own, f_hi), (d_lo, d_own, d_hi)
    lane = lax.broadcasted_iota(jnp.int32, (40, 128), 1)
    first, last = lane == 0, lane == 127

    def tensor(e, r):
        return ds[(r + 4) // 4][e, (r + 4) % 4]

    for p in range(PASSES):
        m = PASSES - 1 - p

        def field(c, r):
            if p == 0:
                return fs[(r + 4) // 4][c, (r + 4) % 4]
            return buf[(p - 1) % 2, c, r + 4]

        for r in range(-m - 1, 4 + m):
            for c in range(2):
                after[c, r + 4] = jnp.where(last, 0.0, pltpu.roll(field(c, r), 127, 1))
        flux_x_before = [None, None]
        here = [field(c, -m - 1) for c in range(2)]
        for r in range(-m - 1, 4 + m):
            d = [tensor(e, r) for e in range(6)]
            for c in range(2):
                f = here[c]
                nxt = field(c, r + 1)
                gx = nxt - f
                gy = pltpu.roll(f, 39, 0) - f
                gz = after[c, r + 4] - f
                fx = d[0] * gx + d[3] * gy + d[4] * gz
                if r >= -m:
                    fy = d[3] * gx + d[1] * gy + d[5] * gz
                    fz = d[4] * gx + d[5] * gy + d[2] * gz
                    part[c, r + 4] = (fx - flux_x_before[c]) + (fy - pltpu.roll(fy, 1, 0)) + fz
                    flux_z[c, r + 4] = fz
                flux_x_before[c] = fx
                here[c] = nxt
        for r in range(-m, 4 + m):
            gain = jnp.where(tensor(0, r) > 0, F32(STEP), F32(0))
            for c in range(2):
                spread = part[c, r + 4] - jnp.where(first, 0.0, pltpu.roll(flux_z[c, r + 4], 1, 1))
                new = field(c, r) + gain * spread
                if p == PASSES - 1:
                    out[c, r] = new[:32]
                else:
                    buf[p % 2, c, r + 4] = new


def diffuse(*args):
    rows = pltpu.VMEM((2, 12, 40, 128), F32)
    return pl.pallas_call(
        diffuse_kernel,
        out_shape=jax.ShapeDtypeStruct(SLAB, F32),
        scratch_shapes=[pltpu.VMEM((2, 2, 12, 40, 128), F32), rows, rows, rows],
        compiler_params=pltpu.CompilerParams(vmem_limit_bytes=32 << 20),
    )(*args)


def core_tile(cells, even):
    return jnp.where(even, cells[..., 28:, :], cells[..., :4, :])


def cross_tile(cells, even):
    return jnp.where(even, cells[..., :4, :], cells[..., 28:, :])


def halo_tile(core, cross, even):
    return jnp.concatenate([jnp.where(even, core, cross), jnp.where(even, cross, core)], axis=-2)


def shards(fwd, adj, cond, tens):
    s, gx, gy = lax.axis_index("source"), lax.axis_index("gx"), lax.axis_index("gy")
    h, z = s // NZC, s % NZC
    own = block_of(h, z)
    x_even, y_even = gx % 2 == 0, gy % 2 == 0

    def blocks(keys):
        return [block_of(jnp.where(half == 0, 1 - h, h), z ^ k) for half, k in keys]

    wrap = own + jnp.where(gx == 0, 1, 0) - jnp.where(gx == 3, 1, 0)
    inside = jnp.where((wrap >= 0) & (wrap < BLOCKS), 1, 0)
    sent_idx = jnp.stack(blocks(SENT)).astype(jnp.int32)
    kept_idx = jnp.stack(blocks(KEPT) + [own, jnp.clip(wrap, 0, BLOCKS - 1), inside]).astype(jnp.int32)
    far2, one, three = sent_products(sent_idx, fwd, adj)
    kept_idx, far2, one, three = lax.optimization_barrier((kept_idx, far2, one, three))
    near2, far0, near0, c_own, d_own, d_odd = kept_products(kept_idx, fwd, adj, cond, tens)

    two_sum = near2 + lax.ppermute(far2, "source", Y_PERM)
    two_in = lax.ppermute(two_sum, "source", z_perm(2))
    one_in = lax.ppermute(one, "source", z_perm(1))
    three_in = lax.ppermute(three, "source", z_perm(3))
    far_sum = far0 + one_in[0] + three_in[0]
    near_sum = near0 + one_in[1] + three_in[1]
    from_far = lax.ppermute(far_sum, "source", Y_PERM)

    rims = jnp.stack([d_own, d_odd])
    d_core = lax.ppermute(core_tile(rims, y_even), "gy", CORE_PERM)
    d_cross = lax.ppermute(cross_tile(rims, y_even), "gy", CROSS_PERM)
    _, d_core, d_cross = lax.optimization_barrier((far_sum, d_core, d_cross))
    tiles = halo_tile(d_core, d_cross, y_even)
    d_own = jnp.concatenate([d_own, tiles[0]], axis=-2)
    d_odd = jnp.concatenate([d_odd, tiles[1]], axis=-2)
    d_odd_in = lax.ppermute(d_odd, "gx", X_ODD_RING)
    d_even_in = lax.ppermute(d_own, "gx", X_EVEN)
    field = near_sum + from_far
    field, two_in = lax.optimization_barrier((field, two_in))
    field = (field + two_in) * c_own

    core = lax.ppermute(core_tile(field, y_even), "gy", CORE_PERM)
    cross = lax.ppermute(cross_tile(field, y_even), "gy", CROSS_PERM)
    f_own = jnp.concatenate([field, halo_tile(core, cross, y_even)], axis=-2)
    f_odd_in = lax.ppermute(f_own, ("source", "gx"), x_odd_owner())
    f_even_in = lax.ppermute(f_own, "gx", X_EVEN)
    d_lo = jnp.where(x_even, d_odd_in, d_even_in)
    d_hi = jnp.where(x_even, d_even_in, d_odd_in)
    d_lo, d_hi, f_odd_in = lax.optimization_barrier((d_lo, d_hi, f_odd_in))
    f_hi = jnp.where(x_even, f_even_in, f_odd_in)
    f_lo = jnp.where(x_even, f_odd_in, f_even_in)
    f_hi, f_lo = lax.optimization_barrier((f_hi, f_lo))

    done = diffuse(f_lo, f_own, f_hi, d_lo, d_own, d_hi)

    two = lax.ppermute(done, "source", z_perm(2))
    other = lax.ppermute(done, "source", Y_PERM)
    one, three = (lax.ppermute(done, "source", z_perm(k)) for k in (1, 3))
    other_two = lax.ppermute(two, "source", Y_PERM)
    other_one, other_three = (lax.ppermute(other, "source", z_perm(k)) for k in (1, 3))
    out = jnp.zeros((2, BLOCKS, 4, 32, 128), F32)
    for half, k, piece in (
        (1 - h, 0, other),
        (h, 2, two),
        (h, 0, done),
        (h, 1, one),
        (h, 3, three),
        (1 - h, 2, other_two),
        (1 - h, 1, other_one),
        (1 - h, 3, other_three),
    ):
        out = lax.dynamic_update_index_in_dim(out, piece, block_of(half, z ^ k), 1)
    return out


def solution(mesh):
    fields = P("source", None, None, "gx", "gy", None)
    cells = P(None, None, "gx", "gy", None)
    return jax.shard_map(
        shards, mesh=mesh, in_specs=(fields, fields, cells, cells), out_specs=cells, check_vma=False
    )
```

```python
import jax
import jax.numpy as jnp
from jax import lax
from jax.experimental import pallas as pl
from jax.experimental.pallas import tpu as pltpu
from jax.sharding import PartitionSpec as P

PASSES = 4
STEP = 0.13
SCALE = 1.0 / 16.0
NZC = 4
BLOCKS = 2 * NZC
F32 = jnp.float32
SLAB = (2, 4, 32, 128)
FLUX_X = (0, 3, 4)


def block_of(h, z):
    return jnp.where(h == 0, z, BLOCKS - 1 - z)


def source_of(b):
    return b if b < NZC else 3 * NZC - 1 - b


def z_perm(k):
    return [(s, s ^ k) for s in range(BLOCKS)]


Y_PERM = [(s, (s + NZC) % BLOCKS) for s in range(BLOCKS)]
CORE_PERM = [(i, i ^ 1) for i in range(4)]
CROSS_PERM = [(1, 2), (2, 1)]
X_EVEN = [(i, i ^ 1) for i in range(4)]
X_ODD_RING = [(1, 2), (2, 1), (3, 0), (0, 3)]


def x_odd_owner():
    pairs = []
    for s in range(BLOCKS):
        pairs += [(s * 4 + 1, s * 4 + 2), (s * 4 + 2, s * 4 + 1)]
    for b in range(BLOCKS - 1):
        low, high = source_of(b) * 4 + 3, source_of(b + 1) * 4
        pairs += [(low, high), (high, low)]
    return pairs


SENT = [(0, 2), (0, 1), (1, 1), (0, 3), (1, 3)]
KEPT = [(1, 2), (0, 0), (1, 0)]


def start_products(idx_ref, f_hbm, a_hbm, f_buf, a_buf, sems, count):
    copies = []
    for k in range(count):
        b = idx_ref[k]
        group = [
            pltpu.make_async_copy(f_hbm.at[:, :, b], f_buf.at[k], sems.at[0, k]),
            pltpu.make_async_copy(a_hbm.at[:, :, b], a_buf.at[k], sems.at[1, k]),
        ]
        for copy in group:
            copy.start()
        copies.append(group)
    return copies


def block_products(k, copies, f_buf, a_buf, out):
    for copy in copies[k]:
        copy.wait()
    for r in range(4):
        hor = ver = None
        for t in range(2):
            prod = [f_buf[k, t, c, r].astype(F32) * a_buf[k, t, c, r].astype(F32) for c in range(6)]
            h1 = (prod[0] + prod[1]) - (prod[3] + prod[4])
            v1 = prod[2] - prod[5]
            hor = h1 if hor is None else hor + h1
            ver = v1 if ver is None else ver + v1
        out[0, r] = hor
        out[1, r] = ver


def sent_kernel(idx_ref, f_hbm, a_hbm, far2, one, three, f_buf, a_buf, sems):
    copies = start_products(idx_ref, f_hbm, a_hbm, f_buf, a_buf, sems, len(SENT))
    for k, out in enumerate((far2, one.at[0], one.at[1], three.at[0], three.at[1])):
        block_products(k, copies, f_buf, a_buf, out)


def kept_kernel(
    idx_ref, f_hbm, a_hbm, c_hbm, t_hbm, near2, far0, near0, c_own, d_own, d_odd, f_buf, a_buf, c_buf, t_buf, sems,
    t_sems, c_sem
):
    n = len(KEPT)
    t_copies = [pltpu.make_async_copy(t_hbm.at[:, idx_ref[n + k]], t_buf.at[k], t_sems.at[k]) for k in range(2)]
    for copy in t_copies:
        copy.start()
    copies = start_products(idx_ref, f_hbm, a_hbm, f_buf, a_buf, sems, n)
    c_copy = pltpu.make_async_copy(c_hbm.at[:, idx_ref[n]], c_buf, c_sem)
    c_copy.start()
    inside = idx_ref[n + 2] > 0
    for copy in t_copies:
        copy.wait()
    for e in range(6):
        for r in range(4):
            d_own[e, r] = t_buf[0, e, r].astype(F32)
            d_odd[e, r] = jnp.where(inside, t_buf[1, e, r].astype(F32), 0.0)
    for k, out in enumerate((near2, far0, near0)):
        block_products(k, copies, f_buf, a_buf, out)
    c_copy.wait()
    c_own[...] = c_buf[...] * SCALE


def products_scratch(n):
    return [
        pltpu.VMEM((n, 2, 6, 4, 32, 128), jnp.bfloat16),
        pltpu.VMEM((n, 2, 6, 4, 32, 128), jnp.bfloat16),
    ]


def in_hbm(*arrays):
    return [pltpu.with_memory_space_constraint(x, pltpu.HBM) for x in arrays]


def sent_products(idx, fwd, adj):
    hbm = pl.BlockSpec(memory_space=pltpu.HBM)
    pair = jax.ShapeDtypeStruct((2, *SLAB), F32)
    return pl.pallas_call(
        sent_kernel,
        in_specs=[pl.BlockSpec(memory_space=pltpu.SMEM), hbm, hbm],
        out_shape=[jax.ShapeDtypeStruct(SLAB, F32), pair, pair],
        scratch_shapes=products_scratch(len(SENT)) + [pltpu.SemaphoreType.DMA((2, len(SENT)))],
        compiler_params=pltpu.CompilerParams(vmem_limit_bytes=32 << 20),
    )(idx, *in_hbm(fwd, adj))


def kept_products(idx, fwd, adj, cond, tens):
    hbm = pl.BlockSpec(memory_space=pltpu.HBM)
    slab = jax.ShapeDtypeStruct(SLAB, F32)
    rim = jax.ShapeDtypeStruct((6, 4, 32, 128), F32)
    return pl.pallas_call(
        kept_kernel,
        in_specs=[pl.BlockSpec(memory_space=pltpu.SMEM), hbm, hbm, hbm, hbm],
        out_shape=[slab, slab, slab, slab, rim, rim],
        scratch_shapes=products_scratch(len(KEPT))
        + [
            pltpu.VMEM(SLAB, F32),
            pltpu.VMEM((2, 6, 4, 32, 128), jnp.bfloat16),
            pltpu.SemaphoreType.DMA((2, len(KEPT))),
            pltpu.SemaphoreType.DMA((2,)),
            pltpu.SemaphoreType.DMA(()),
        ],
        compiler_params=pltpu.CompilerParams(vmem_limit_bytes=32 << 20),
    )(idx, *in_hbm(fwd, adj, cond, tens))


def diffuse_kernel(f_lo, f_own, f_hi, d_lo, d_own, d_hi, out, buf, after, part, flux_z):
    fs = (f_lo, f_own, f_hi)
    lane = lax.broadcasted_iota(jnp.int32, (40, 128), 1)
    first, last = lane == 0, lane == 127

    def tensor(e, r):
        if r == -4:
            return d_lo[18 + FLUX_X.index(e)]
        if r < 0:
            return d_lo[3 * e + r + 3]
        return d_own[e, r] if r < 4 else d_hi[3 * e + r - 4]

    for p in range(PASSES):
        m = PASSES - 1 - p

        def field(c, r):
            if p == 0:
                return fs[(r + 4) // 4][c, (r + 4) % 4]
            return buf[(p - 1) % 2, c, r + 4]

        for r in range(-m - 1, 4 + m):
            for c in range(2):
                after[c, r + 4] = jnp.where(last, 0.0, pltpu.roll(field(c, r), 127, 1))
        flux_x_before = [None, None]
        here = [field(c, -m - 1) for c in range(2)]
        for r in range(-m - 1, 4 + m):
            d = {e: tensor(e, r) for e in (range(6) if r >= -m else FLUX_X)}
            for c in range(2):
                f = here[c]
                nxt = field(c, r + 1)
                gx = nxt - f
                gy = pltpu.roll(f, 39, 0) - f
                gz = after[c, r + 4] - f
                fx = d[0] * gx + d[3] * gy + d[4] * gz
                if r >= -m:
                    fy = d[3] * gx + d[1] * gy + d[5] * gz
                    fz = d[4] * gx + d[5] * gy + d[2] * gz
                    part[c, r + 4] = (fx - flux_x_before[c]) + (fy - pltpu.roll(fy, 1, 0)) + fz
                    flux_z[c, r + 4] = fz
                flux_x_before[c] = fx
                here[c] = nxt
        for r in range(-m, 4 + m):
            gain = jnp.where(tensor(0, r) > 0, F32(STEP), F32(0))
            for c in range(2):
                spread = part[c, r + 4] - jnp.where(first, 0.0, pltpu.roll(flux_z[c, r + 4], 1, 1))
                new = field(c, r) + gain * spread
                if p == PASSES - 1:
                    out[c, r] = new[:32]
                else:
                    buf[p % 2, c, r + 4] = new


def diffuse(*args):
    rows = pltpu.VMEM((2, 12, 40, 128), F32)
    return pl.pallas_call(
        diffuse_kernel,
        out_shape=jax.ShapeDtypeStruct(SLAB, F32),
        scratch_shapes=[pltpu.VMEM((2, 2, 12, 40, 128), F32), rows, rows, rows],
        compiler_params=pltpu.CompilerParams(vmem_limit_bytes=32 << 20),
    )(*args)


def core_tile(cells, even):
    return jnp.where(even, cells[..., 28:, :], cells[..., :4, :])


def cross_tile(cells, even):
    return jnp.where(even, cells[..., :4, :], cells[..., 28:, :])


def halo_tile(core, cross, even):
    return jnp.concatenate([jnp.where(even, core, cross), jnp.where(even, cross, core)], axis=-2)


def rows_for(rim, upward):
    rows = jnp.where(upward, rim[:, 1:], rim[:, :3]).reshape(18, 40, 128)
    return jnp.concatenate([rows, rim[0:1, 0], rim[3:5, 0]], axis=0)


def shards(fwd, adj, cond, tens):
    s, gx, gy = lax.axis_index("source"), lax.axis_index("gx"), lax.axis_index("gy")
    h, z = s // NZC, s % NZC
    own = block_of(h, z)
    x_even, y_even = gx % 2 == 0, gy % 2 == 0

    def blocks(keys):
        return [block_of(jnp.where(half == 0, 1 - h, h), z ^ k) for half, k in keys]

    wrap = own + jnp.where(gx == 0, 1, 0) - jnp.where(gx == 3, 1, 0)
    inside = jnp.where((wrap >= 0) & (wrap < BLOCKS), 1, 0)
    sent_idx = jnp.stack(blocks(SENT)).astype(jnp.int32)
    kept_idx = jnp.stack(blocks(KEPT) + [own, jnp.clip(wrap, 0, BLOCKS - 1), inside]).astype(jnp.int32)
    far2, one, three = sent_products(sent_idx, fwd, adj)
    kept_idx, far2, one, three = lax.optimization_barrier((kept_idx, far2, one, three))
    near2, far0, near0, c_own, d_own, d_odd = kept_products(kept_idx, fwd, adj, cond, tens)

    two_sum = near2 + lax.ppermute(far2, "source", Y_PERM)
    two_in = lax.ppermute(two_sum, "source", z_perm(2))
    one_in = lax.ppermute(one, "source", z_perm(1))
    three_in = lax.ppermute(three, "source", z_perm(3))
    far_sum = far0 + one_in[0] + three_in[0]
    near_sum = near0 + one_in[1] + three_in[1]
    from_far = lax.ppermute(far_sum, "source", Y_PERM)

    rims = jnp.stack([d_own, d_odd])
    d_core = lax.ppermute(core_tile(rims, y_even), "gy", CORE_PERM)
    d_cross = lax.ppermute(cross_tile(rims, y_even), "gy", CROSS_PERM)
    _, d_core, d_cross = lax.optimization_barrier((far_sum, d_core, d_cross))
    tiles = halo_tile(d_core, d_cross, y_even)
    d_own = jnp.concatenate([d_own, tiles[0]], axis=-2)
    d_odd = jnp.concatenate([d_odd, tiles[1]], axis=-2)
    d_odd_in = lax.ppermute(rows_for(d_odd, jnp.logical_not(x_even)), "gx", X_ODD_RING)
    d_even_in = lax.ppermute(rows_for(d_own, x_even), "gx", X_EVEN)
    field = near_sum + from_far
    field, two_in = lax.optimization_barrier((field, two_in))
    field = (field + two_in) * c_own

    core = lax.ppermute(core_tile(field, y_even), "gy", CORE_PERM)
    cross = lax.ppermute(cross_tile(field, y_even), "gy", CROSS_PERM)
    f_own = jnp.concatenate([field, halo_tile(core, cross, y_even)], axis=-2)
    f_odd_in = lax.ppermute(f_own, ("source", "gx"), x_odd_owner())
    f_even_in = lax.ppermute(f_own, "gx", X_EVEN)
    d_lo = jnp.where(x_even, d_odd_in, d_even_in)
    d_hi = jnp.where(x_even, d_even_in, d_odd_in)
    d_lo, d_hi, f_odd_in = lax.optimization_barrier((d_lo, d_hi, f_odd_in))
    f_hi = jnp.where(x_even, f_even_in, f_odd_in)
    f_lo = jnp.where(x_even, f_odd_in, f_even_in)
    f_hi, f_lo = lax.optimization_barrier((f_hi, f_lo))

    done = diffuse(f_lo, f_own, f_hi, d_lo, d_own, d_hi)

    two = lax.ppermute(done, "source", z_perm(2))
    other = lax.ppermute(done, "source", Y_PERM)
    one, three = (lax.ppermute(done, "source", z_perm(k)) for k in (1, 3))
    other_two = lax.ppermute(two, "source", Y_PERM)
    other_one, other_three = (lax.ppermute(other, "source", z_perm(k)) for k in (1, 3))
    out = jnp.zeros((2, BLOCKS, 4, 32, 128), F32)
    for half, k, piece in (
        (h, 2, two),
        (h, 0, done),
        (1 - h, 0, other),
        (h, 1, one),
        (h, 3, three),
        (1 - h, 2, other_two),
        (1 - h, 1, other_one),
        (1 - h, 3, other_three),
    ):
        out = lax.dynamic_update_index_in_dim(out, piece, block_of(half, z ^ k), 1)
    return out


def solution(mesh):
    fields = P("source", None, None, "gx", "gy", None)
    cells = P(None, None, "gx", "gy", None)
    return jax.shard_map(
        shards, mesh=mesh, in_specs=(fields, fields, cells, cells), out_specs=cells, check_vma=False
    )
```

```python
import jax
import jax.numpy as jnp
from jax import lax
from jax.experimental import pallas as pl
from jax.experimental.pallas import tpu as pltpu
from jax.sharding import PartitionSpec as P

PASSES = 4
STEP = 0.13
SCALE = 1.0 / 16.0
NZC = 4
BLOCKS = 2 * NZC
F32 = jnp.float32
SLAB = (2, 4, 32, 128)
FLUX_X = (0, 3, 4)


def block_of(h, z):
    return jnp.where(h == 0, NZC - 1 - z, NZC + z)


def source_of(b):
    return NZC - 1 - b if b < NZC else b


def z_perm(k):
    return [(s, s ^ k) for s in range(BLOCKS)]


Y_PERM = [(s, (s + NZC) % BLOCKS) for s in range(BLOCKS)]
CORE_PERM = [(i, i ^ 1) for i in range(4)]
CROSS_PERM = [(1, 2), (2, 1)]
X_EVEN = [(i, i ^ 1) for i in range(4)]
X_ODD_RING = [(1, 2), (2, 1), (3, 0), (0, 3)]


def x_odd_owner():
    pairs = []
    for s in range(BLOCKS):
        pairs += [(s * 4 + 1, s * 4 + 2), (s * 4 + 2, s * 4 + 1)]
    for b in range(BLOCKS - 1):
        low, high = source_of(b) * 4 + 3, source_of(b + 1) * 4
        pairs += [(low, high), (high, low)]
    return pairs


SENT = [(0, 2), (0, 1), (1, 1), (0, 3), (1, 3)]
KEPT = [(1, 2), (0, 0), (1, 0)]


def start_products(idx_ref, f_hbm, a_hbm, f_buf, a_buf, sems, count):
    copies = []
    for k in range(count):
        b = idx_ref[k]
        group = [
            pltpu.make_async_copy(f_hbm.at[:, :, b], f_buf.at[k], sems.at[0, k]),
            pltpu.make_async_copy(a_hbm.at[:, :, b], a_buf.at[k], sems.at[1, k]),
        ]
        for copy in group:
            copy.start()
        copies.append(group)
    return copies


def block_products(k, copies, f_buf, a_buf, out):
    for copy in copies[k]:
        copy.wait()
    for r in range(4):
        hor = ver = None
        for t in range(2):
            prod = [f_buf[k, t, c, r].astype(F32) * a_buf[k, t, c, r].astype(F32) for c in range(6)]
            h1 = (prod[0] + prod[1]) - (prod[3] + prod[4])
            v1 = prod[2] - prod[5]
            hor = h1 if hor is None else hor + h1
            ver = v1 if ver is None else ver + v1
        out[0, r] = hor
        out[1, r] = ver


def sent_kernel(idx_ref, f_hbm, a_hbm, far2, one, three, f_buf, a_buf, sems):
    copies = start_products(idx_ref, f_hbm, a_hbm, f_buf, a_buf, sems, len(SENT))
    for k, out in enumerate((far2, one.at[0], one.at[1], three.at[0], three.at[1])):
        block_products(k, copies, f_buf, a_buf, out)


def kept_kernel(
    idx_ref, f_hbm, a_hbm, c_hbm, t_hbm, near2, far0, near0, c_own, d_own, d_odd, f_buf, a_buf, c_buf, t_buf, sems,
    t_sems, c_sem
):
    n = len(KEPT)
    t_copies = [pltpu.make_async_copy(t_hbm.at[:, idx_ref[n + k]], t_buf.at[k], t_sems.at[k]) for k in range(2)]
    for copy in t_copies:
        copy.start()
    copies = start_products(idx_ref, f_hbm, a_hbm, f_buf, a_buf, sems, n)
    c_copy = pltpu.make_async_copy(c_hbm.at[:, idx_ref[n]], c_buf, c_sem)
    c_copy.start()
    inside = idx_ref[n + 2] > 0
    for copy in t_copies:
        copy.wait()
    for e in range(6):
        for r in range(4):
            d_own[e, r] = t_buf[0, e, r].astype(F32)
            d_odd[e, r] = jnp.where(inside, t_buf[1, e, r].astype(F32), 0.0)
    for k, out in enumerate((near2, far0, near0)):
        block_products(k, copies, f_buf, a_buf, out)
    c_copy.wait()
    c_own[...] = c_buf[...] * SCALE


def products_scratch(n):
    return [
        pltpu.VMEM((n, 2, 6, 4, 32, 128), jnp.bfloat16),
        pltpu.VMEM((n, 2, 6, 4, 32, 128), jnp.bfloat16),
    ]


def in_hbm(*arrays):
    return [pltpu.with_memory_space_constraint(x, pltpu.HBM) for x in arrays]


def sent_products(idx, fwd, adj):
    hbm = pl.BlockSpec(memory_space=pltpu.HBM)
    pair = jax.ShapeDtypeStruct((2, *SLAB), F32)
    return pl.pallas_call(
        sent_kernel,
        in_specs=[pl.BlockSpec(memory_space=pltpu.SMEM), hbm, hbm],
        out_shape=[jax.ShapeDtypeStruct(SLAB, F32), pair, pair],
        scratch_shapes=products_scratch(len(SENT)) + [pltpu.SemaphoreType.DMA((2, len(SENT)))],
        compiler_params=pltpu.CompilerParams(vmem_limit_bytes=32 << 20),
    )(idx, *in_hbm(fwd, adj))


def kept_products(idx, fwd, adj, cond, tens):
    hbm = pl.BlockSpec(memory_space=pltpu.HBM)
    slab = jax.ShapeDtypeStruct(SLAB, F32)
    rim = jax.ShapeDtypeStruct((6, 4, 32, 128), F32)
    return pl.pallas_call(
        kept_kernel,
        in_specs=[pl.BlockSpec(memory_space=pltpu.SMEM), hbm, hbm, hbm, hbm],
        out_shape=[slab, slab, slab, slab, rim, rim],
        scratch_shapes=products_scratch(len(KEPT))
        + [
            pltpu.VMEM(SLAB, F32),
            pltpu.VMEM((2, 6, 4, 32, 128), jnp.bfloat16),
            pltpu.SemaphoreType.DMA((2, len(KEPT))),
            pltpu.SemaphoreType.DMA((2,)),
            pltpu.SemaphoreType.DMA(()),
        ],
        compiler_params=pltpu.CompilerParams(vmem_limit_bytes=32 << 20),
    )(idx, *in_hbm(fwd, adj, cond, tens))


def diffuse_kernel(f_lo, f_own, f_hi, d_lo, d_own, d_hi, out, buf, after, part, flux_z):
    fs = (f_lo, f_own, f_hi)
    lane = lax.broadcasted_iota(jnp.int32, (40, 128), 1)
    first, last = lane == 0, lane == 127

    def tensor(e, r):
        if r == -4:
            return d_lo[18 + FLUX_X.index(e)]
        if r < 0:
            return d_lo[3 * e + r + 3]
        return d_own[e, r] if r < 4 else d_hi[3 * e + r - 4]

    for p in range(PASSES):
        m = PASSES - 1 - p

        def field(c, r):
            if p == 0:
                return fs[(r + 4) // 4][c, (r + 4) % 4]
            return buf[(p - 1) % 2, c, r + 4]

        for r in range(-m - 1, 4 + m):
            for c in range(2):
                after[c, r + 4] = jnp.where(last, 0.0, pltpu.roll(field(c, r), 127, 1))
        flux_x_before = [None, None]
        here = [field(c, -m - 1) for c in range(2)]
        for r in range(-m - 1, 4 + m):
            d = {e: tensor(e, r) for e in (range(6) if r >= -m else FLUX_X)}
            for c in range(2):
                f = here[c]
                nxt = field(c, r + 1)
                gx = nxt - f
                gy = pltpu.roll(f, 39, 0) - f
                gz = after[c, r + 4] - f
                fx = d[0] * gx + d[3] * gy + d[4] * gz
                if r >= -m:
                    fy = d[3] * gx + d[1] * gy + d[5] * gz
                    fz = d[4] * gx + d[5] * gy + d[2] * gz
                    part[c, r + 4] = (fx - flux_x_before[c]) + (fy - pltpu.roll(fy, 1, 0)) + fz
                    flux_z[c, r + 4] = fz
                flux_x_before[c] = fx
                here[c] = nxt
        for r in range(-m, 4 + m):
            gain = jnp.where(tensor(0, r) > 0, F32(STEP), F32(0))
            for c in range(2):
                spread = part[c, r + 4] - jnp.where(first, 0.0, pltpu.roll(flux_z[c, r + 4], 1, 1))
                new = field(c, r) + gain * spread
                if p == PASSES - 1:
                    out[c, r] = new[:32]
                else:
                    buf[p % 2, c, r + 4] = new


def diffuse(*args):
    rows = pltpu.VMEM((2, 12, 40, 128), F32)
    return pl.pallas_call(
        diffuse_kernel,
        out_shape=jax.ShapeDtypeStruct(SLAB, F32),
        scratch_shapes=[pltpu.VMEM((2, 2, 12, 40, 128), F32), rows, rows, rows],
        compiler_params=pltpu.CompilerParams(vmem_limit_bytes=32 << 20),
    )(*args)


def core_tile(cells, even):
    return jnp.where(even, cells[..., 28:, :], cells[..., :4, :])


def cross_tile(cells, even):
    return jnp.where(even, cells[..., :4, :], cells[..., 28:, :])


def halo_tile(core, cross, even):
    return jnp.concatenate([jnp.where(even, core, cross), jnp.where(even, cross, core)], axis=-2)


def rows_for(rim, upward):
    rows = jnp.where(upward, rim[:, 1:], rim[:, :3]).reshape(18, 40, 128)
    return jnp.concatenate([rows, rim[0:1, 0], rim[3:5, 0]], axis=0)


def shards(fwd, adj, cond, tens):
    s, gx, gy = lax.axis_index("source"), lax.axis_index("gx"), lax.axis_index("gy")
    h, z = s // NZC, s % NZC
    own = block_of(h, z)
    x_even, y_even = gx % 2 == 0, gy % 2 == 0

    def blocks(keys):
        return [block_of(jnp.where(half == 0, 1 - h, h), z ^ k) for half, k in keys]

    wrap = own + jnp.where(gx == 0, 1, 0) - jnp.where(gx == 3, 1, 0)
    inside = jnp.where((wrap >= 0) & (wrap < BLOCKS), 1, 0)
    sent_idx = jnp.stack(blocks(SENT)).astype(jnp.int32)
    kept_idx = jnp.stack(blocks(KEPT) + [own, jnp.clip(wrap, 0, BLOCKS - 1), inside]).astype(jnp.int32)
    far2, one, three = sent_products(sent_idx, fwd, adj)
    kept_idx, far2, one, three = lax.optimization_barrier((kept_idx, far2, one, three))
    near2, far0, near0, c_own, d_own, d_odd = kept_products(kept_idx, fwd, adj, cond, tens)

    two_sum = near2 + lax.ppermute(far2, "source", Y_PERM)
    two_in = lax.ppermute(two_sum, "source", z_perm(2))
    one_in = lax.ppermute(one, "source", z_perm(1))
    three_in = lax.ppermute(three, "source", z_perm(3))
    far_sum = far0 + one_in[0] + three_in[0]
    near_sum = near0 + one_in[1] + three_in[1]
    from_far = lax.ppermute(far_sum, "source", Y_PERM)

    rims = jnp.stack([d_own, d_odd])
    d_core = lax.ppermute(core_tile(rims, y_even), "gy", CORE_PERM)
    d_cross = lax.ppermute(cross_tile(rims, y_even), "gy", CROSS_PERM)
    _, d_core, d_cross = lax.optimization_barrier((far_sum, d_core, d_cross))
    tiles = halo_tile(d_core, d_cross, y_even)
    d_own = jnp.concatenate([d_own, tiles[0]], axis=-2)
    d_odd = jnp.concatenate([d_odd, tiles[1]], axis=-2)
    d_odd_in = lax.ppermute(rows_for(d_odd, jnp.logical_not(x_even)), "gx", X_ODD_RING)
    d_even_in = lax.ppermute(rows_for(d_own, x_even), "gx", X_EVEN)
    field = near_sum + from_far
    field, two_in = lax.optimization_barrier((field, two_in))
    field = (field + two_in) * c_own

    core = lax.ppermute(core_tile(field, y_even), "gy", CORE_PERM)
    cross = lax.ppermute(cross_tile(field, y_even), "gy", CROSS_PERM)
    f_own = jnp.concatenate([field, halo_tile(core, cross, y_even)], axis=-2)
    f_odd_in = lax.ppermute(f_own, ("source", "gx"), x_odd_owner())
    f_even_in = lax.ppermute(f_own, "gx", X_EVEN)
    d_lo = jnp.where(x_even, d_odd_in, d_even_in)
    d_hi = jnp.where(x_even, d_even_in, d_odd_in)
    d_lo, d_hi, f_odd_in = lax.optimization_barrier((d_lo, d_hi, f_odd_in))
    f_hi = jnp.where(x_even, f_even_in, f_odd_in)
    f_lo = jnp.where(x_even, f_odd_in, f_even_in)
    f_hi, f_lo = lax.optimization_barrier((f_hi, f_lo))

    done = diffuse(f_lo, f_own, f_hi, d_lo, d_own, d_hi)

    two = lax.ppermute(done, "source", z_perm(2))
    other = lax.ppermute(done, "source", Y_PERM)
    one, three = (lax.ppermute(done, "source", z_perm(k)) for k in (1, 3))
    other_two = lax.ppermute(two, "source", Y_PERM)
    other_one, other_three = (lax.ppermute(other, "source", z_perm(k)) for k in (1, 3))
    out = jnp.zeros((2, BLOCKS, 4, 32, 128), F32)
    for half, k, piece in (
        (h, 2, two),
        (h, 0, done),
        (1 - h, 0, other),
        (h, 1, one),
        (h, 3, three),
        (1 - h, 2, other_two),
        (1 - h, 1, other_one),
        (1 - h, 3, other_three),
    ):
        out = lax.dynamic_update_index_in_dim(out, piece, block_of(half, z ^ k), 1)
    return out


def solution(mesh):
    fields = P("source", None, None, "gx", "gy", None)
    cells = P(None, None, "gx", "gy", None)
    return jax.shard_map(
        shards, mesh=mesh, in_specs=(fields, fields, cells, cells), out_specs=cells, check_vma=False
    )
```

```python
import jax
import jax.numpy as jnp
from jax import lax
from jax.experimental import pallas as pl
from jax.experimental.pallas import tpu as pltpu
from jax.sharding import PartitionSpec as P

PASSES = 4
STEP = 0.13
SCALE = 1.0 / 16.0
NZC = 4
BLOCKS = 2 * NZC
F32 = jnp.float32
SLAB = (2, 4, 32, 128)
FLUX_X = (0, 3, 4)


def block_of(h, z):
    return jnp.where(h == 0, z, BLOCKS - 1 - z)


def source_of(b):
    return b if b < NZC else 3 * NZC - 1 - b


def z_perm(k):
    return [(s, s ^ k) for s in range(BLOCKS)]


Y_PERM = [(s, (s + NZC) % BLOCKS) for s in range(BLOCKS)]
CORE_PERM = [(i, i ^ 1) for i in range(4)]
CROSS_PERM = [(1, 2), (2, 1)]
X_EVEN = [(i, i ^ 1) for i in range(4)]
X_ODD_RING = [(1, 2), (2, 1), (3, 0), (0, 3)]


def x_odd_owner():
    pairs = []
    for s in range(BLOCKS):
        pairs += [(s * 4 + 1, s * 4 + 2), (s * 4 + 2, s * 4 + 1)]
    for b in range(BLOCKS - 1):
        low, high = source_of(b) * 4 + 3, source_of(b + 1) * 4
        pairs += [(low, high), (high, low)]
    return pairs


SENT = [(0, 2), (0, 1), (1, 1), (0, 3), (1, 3)]
KEPT = [(1, 2), (0, 0), (1, 0)]


def start_products(idx_ref, f_hbm, a_hbm, f_buf, a_buf, sems, count):
    copies = []
    for k in range(count):
        b = idx_ref[k]
        group = [
            pltpu.make_async_copy(f_hbm.at[:, :, b], f_buf.at[k], sems.at[0, k]),
            pltpu.make_async_copy(a_hbm.at[:, :, b], a_buf.at[k], sems.at[1, k]),
        ]
        for copy in group:
            copy.start()
        copies.append(group)
    return copies


def block_products(k, copies, f_buf, a_buf, out):
    for copy in copies[k]:
        copy.wait()
    for r in range(4):
        hor = ver = None
        for t in range(2):
            prod = [f_buf[k, t, c, r].astype(F32) * a_buf[k, t, c, r].astype(F32) for c in range(6)]
            h1 = (prod[0] + prod[1]) - (prod[3] + prod[4])
            v1 = prod[2] - prod[5]
            hor = h1 if hor is None else hor + h1
            ver = v1 if ver is None else ver + v1
        out[0, r] = hor
        out[1, r] = ver


def sent_kernel(idx_ref, f_hbm, a_hbm, far2, one, three, f_buf, a_buf, sems):
    copies = start_products(idx_ref, f_hbm, a_hbm, f_buf, a_buf, sems, len(SENT))
    for k, out in enumerate((far2, one.at[0], one.at[1], three.at[0], three.at[1])):
        block_products(k, copies, f_buf, a_buf, out)


def kept_kernel(
    idx_ref, f_hbm, a_hbm, c_hbm, t_hbm, near2, far0, near0, c_own, d_own, d_odd, f_buf, a_buf, c_buf, t_buf, sems,
    t_sems, c_sem
):
    n = len(KEPT)
    t_copies = [pltpu.make_async_copy(t_hbm.at[:, idx_ref[n + k]], t_buf.at[k], t_sems.at[k]) for k in range(2)]
    for copy in t_copies:
        copy.start()
    copies = start_products(idx_ref, f_hbm, a_hbm, f_buf, a_buf, sems, n)
    c_copy = pltpu.make_async_copy(c_hbm.at[:, idx_ref[n]], c_buf, c_sem)
    c_copy.start()
    inside = idx_ref[n + 2] > 0
    for copy in t_copies:
        copy.wait()
    for e in range(6):
        for r in range(4):
            d_own[e, r] = t_buf[0, e, r].astype(F32)
            d_odd[e, r] = jnp.where(inside, t_buf[1, e, r].astype(F32), 0.0)
    for k, out in enumerate((near2, far0, near0)):
        block_products(k, copies, f_buf, a_buf, out)
    c_copy.wait()
    c_own[...] = c_buf[...] * SCALE


def products_scratch(n):
    return [
        pltpu.VMEM((n, 2, 6, 4, 32, 128), jnp.bfloat16),
        pltpu.VMEM((n, 2, 6, 4, 32, 128), jnp.bfloat16),
    ]


def in_hbm(*arrays):
    return [pltpu.with_memory_space_constraint(x, pltpu.HBM) for x in arrays]


def sent_products(idx, fwd, adj):
    hbm = pl.BlockSpec(memory_space=pltpu.HBM)
    pair = jax.ShapeDtypeStruct((2, *SLAB), F32)
    return pl.pallas_call(
        sent_kernel,
        in_specs=[pl.BlockSpec(memory_space=pltpu.SMEM), hbm, hbm],
        out_shape=[jax.ShapeDtypeStruct(SLAB, F32), pair, pair],
        scratch_shapes=products_scratch(len(SENT)) + [pltpu.SemaphoreType.DMA((2, len(SENT)))],
        compiler_params=pltpu.CompilerParams(vmem_limit_bytes=32 << 20),
    )(idx, *in_hbm(fwd, adj))


def kept_products(idx, fwd, adj, cond, tens):
    hbm = pl.BlockSpec(memory_space=pltpu.HBM)
    slab = jax.ShapeDtypeStruct(SLAB, F32)
    rim = jax.ShapeDtypeStruct((6, 4, 32, 128), F32)
    return pl.pallas_call(
        kept_kernel,
        in_specs=[pl.BlockSpec(memory_space=pltpu.SMEM), hbm, hbm, hbm, hbm],
        out_shape=[slab, slab, slab, slab, rim, rim],
        scratch_shapes=products_scratch(len(KEPT))
        + [
            pltpu.VMEM(SLAB, F32),
            pltpu.VMEM((2, 6, 4, 32, 128), jnp.bfloat16),
            pltpu.SemaphoreType.DMA((2, len(KEPT))),
            pltpu.SemaphoreType.DMA((2,)),
            pltpu.SemaphoreType.DMA(()),
        ],
        compiler_params=pltpu.CompilerParams(vmem_limit_bytes=32 << 20),
    )(idx, *in_hbm(fwd, adj, cond, tens))


def diffuse_kernel(f_lo, f_own, f_hi, d_lo, d_own, d_hi, out, buf, after, part, flux_z):
    fs = (f_lo, f_own, f_hi)
    lane = lax.broadcasted_iota(jnp.int32, (40, 128), 1)
    first, last = lane == 0, lane == 127

    def tensor(e, r):
        if r == -4:
            return d_lo[18 + FLUX_X.index(e)]
        if r < 0:
            return d_lo[3 * e + r + 3]
        return d_own[e, r] if r < 4 else d_hi[3 * e + r - 4]

    for p in range(PASSES):
        m = PASSES - 1 - p

        def field(c, r):
            if p == 0:
                return fs[(r + 4) // 4][c, (r + 4) % 4]
            return buf[(p - 1) % 2, c, r + 4]

        for r in range(-m - 1, 4 + m):
            for c in range(2):
                after[c, r + 4] = jnp.where(last, 0.0, pltpu.roll(field(c, r), 127, 1))
        flux_x_before = [None, None]
        here = [field(c, -m - 1) for c in range(2)]
        for r in range(-m - 1, 4 + m):
            d = {e: tensor(e, r) for e in (range(6) if r >= -m else FLUX_X)}
            for c in range(2):
                f = here[c]
                nxt = field(c, r + 1)
                gx = nxt - f
                gy = pltpu.roll(f, 39, 0) - f
                gz = after[c, r + 4] - f
                fx = d[0] * gx + d[3] * gy + d[4] * gz
                if r >= -m:
                    fy = d[3] * gx + d[1] * gy + d[5] * gz
                    fz = d[4] * gx + d[5] * gy + d[2] * gz
                    part[c, r + 4] = (fx - flux_x_before[c]) + (fy - pltpu.roll(fy, 1, 0)) + fz
                    flux_z[c, r + 4] = fz
                flux_x_before[c] = fx
                here[c] = nxt
        for r in range(-m, 4 + m):
            gain = jnp.where(tensor(0, r) > 0, F32(STEP), F32(0))
            for c in range(2):
                spread = part[c, r + 4] - jnp.where(first, 0.0, pltpu.roll(flux_z[c, r + 4], 1, 1))
                new = field(c, r) + gain * spread
                if p == PASSES - 1:
                    out[c, r] = new[:32]
                else:
                    buf[p % 2, c, r + 4] = new


def diffuse(*args):
    rows = pltpu.VMEM((2, 12, 40, 128), F32)
    return pl.pallas_call(
        diffuse_kernel,
        out_shape=jax.ShapeDtypeStruct(SLAB, F32),
        scratch_shapes=[pltpu.VMEM((2, 2, 12, 40, 128), F32), rows, rows, rows],
        compiler_params=pltpu.CompilerParams(vmem_limit_bytes=32 << 20),
    )(*args)


def core_tile(cells, even):
    return jnp.where(even, cells[..., 28:, :], cells[..., :4, :])


def cross_tile(cells, even):
    return jnp.where(even, cells[..., :4, :], cells[..., 28:, :])


def halo_tile(core, cross, even):
    return jnp.concatenate([jnp.where(even, core, cross), jnp.where(even, cross, core)], axis=-2)


def rows_for(rim, upward):
    rows = jnp.where(upward, rim[:, 1:], rim[:, :3]).reshape(18, 40, 128)
    return jnp.concatenate([rows, rim[0:1, 0], rim[3:5, 0]], axis=0)


def shards(fwd, adj, cond, tens):
    s, gx, gy = lax.axis_index("source"), lax.axis_index("gx"), lax.axis_index("gy")
    h, z = s // NZC, s % NZC
    own = block_of(h, z)
    x_even, y_even = gx % 2 == 0, gy % 2 == 0

    def blocks(keys):
        return [block_of(jnp.where(half == 0, 1 - h, h), z ^ k) for half, k in keys]

    wrap = own + jnp.where(gx == 0, 1, 0) - jnp.where(gx == 3, 1, 0)
    inside = jnp.where((wrap >= 0) & (wrap < BLOCKS), 1, 0)
    sent_idx = jnp.stack(blocks(SENT)).astype(jnp.int32)
    kept_idx = jnp.stack(blocks(KEPT) + [own, jnp.clip(wrap, 0, BLOCKS - 1), inside]).astype(jnp.int32)
    far2, one, three = sent_products(sent_idx, fwd, adj)
    kept_idx, far2, one, three = lax.optimization_barrier((kept_idx, far2, one, three))
    near2, far0, near0, c_own, d_own, d_odd = kept_products(kept_idx, fwd, adj, cond, tens)

    two_sum = near2 + lax.ppermute(far2, "source", Y_PERM)
    two_in = lax.ppermute(two_sum, "source", z_perm(2))
    one_in = lax.ppermute(one, "source", z_perm(1))
    three_in = lax.ppermute(three, "source", z_perm(3))
    far_sum = far0 + one_in[0] + three_in[0]
    near_sum = near0 + one_in[1] + three_in[1]
    from_far = lax.ppermute(far_sum, "source", Y_PERM)

    rims = jnp.stack([d_own, d_odd])
    d_core = lax.ppermute(core_tile(rims, y_even), "gy", CORE_PERM)
    d_cross = lax.ppermute(cross_tile(rims, y_even), "gy", CROSS_PERM)
    d_cross, d_core, _ = lax.optimization_barrier((d_cross, d_core, far_sum))
    tiles = halo_tile(d_core, d_cross, y_even)
    d_own = jnp.concatenate([d_own, tiles[0]], axis=-2)
    d_odd = jnp.concatenate([d_odd, tiles[1]], axis=-2)
    d_odd_in = lax.ppermute(rows_for(d_odd, jnp.logical_not(x_even)), "gx", X_ODD_RING)
    d_even_in = lax.ppermute(rows_for(d_own, x_even), "gx", X_EVEN)
    field = near_sum + from_far
    field, two_in = lax.optimization_barrier((field, two_in))
    field = (field + two_in) * c_own

    core = lax.ppermute(core_tile(field, y_even), "gy", CORE_PERM)
    cross = lax.ppermute(cross_tile(field, y_even), "gy", CROSS_PERM)
    f_own = jnp.concatenate([field, halo_tile(core, cross, y_even)], axis=-2)
    f_odd_in = lax.ppermute(f_own, ("source", "gx"), x_odd_owner())
    f_even_in = lax.ppermute(f_own, "gx", X_EVEN)
    d_lo = jnp.where(x_even, d_odd_in, d_even_in)
    d_hi = jnp.where(x_even, d_even_in, d_odd_in)
    d_lo, d_hi, f_odd_in = lax.optimization_barrier((d_lo, d_hi, f_odd_in))
    f_hi = jnp.where(x_even, f_even_in, f_odd_in)
    f_lo = jnp.where(x_even, f_odd_in, f_even_in)
    f_hi, f_lo = lax.optimization_barrier((f_hi, f_lo))

    done = diffuse(f_lo, f_own, f_hi, d_lo, d_own, d_hi)

    two = lax.ppermute(done, "source", z_perm(2))
    other = lax.ppermute(done, "source", Y_PERM)
    one, three = (lax.ppermute(done, "source", z_perm(k)) for k in (1, 3))
    other_two = lax.ppermute(two, "source", Y_PERM)
    other_one, other_three = (lax.ppermute(other, "source", z_perm(k)) for k in (1, 3))
    out = jnp.zeros((2, BLOCKS, 4, 32, 128), F32)
    for half, k, piece in (
        (h, 2, two),
        (h, 0, done),
        (1 - h, 0, other),
        (h, 1, one),
        (h, 3, three),
        (1 - h, 2, other_two),
        (1 - h, 1, other_one),
        (1 - h, 3, other_three),
    ):
        out = lax.dynamic_update_index_in_dim(out, piece, block_of(half, z ^ k), 1)
    return out


def solution(mesh):
    fields = P("source", None, None, "gx", "gy", None)
    cells = P(None, None, "gx", "gy", None)
    return jax.shard_map(
        shards, mesh=mesh, in_specs=(fields, fields, cells, cells), out_specs=cells, check_vma=False
    )
```
